32 devices in a mesh: node: 8 (over z, y), ctr: 4 (over x, core).
Axes of the slice: x: 2, y: 2, z: 4, core: 2. Of those that a mesh axis runs over, the one named last changes fastest.
Arguments:
- surface_xyz: float32 [3, 65536], P(None, ('node', 'ctr')), may hold values from 0 to 1
- centre_idx: int32 [32768], P(('node', 'ctr')), may hold values from 0 to 65535, as said below
- volume_xyz: float32 [3, 32768], P(None, 'node'), may hold values from 0 to 1
- slab_ids: int32 [32768], P('node'), may hold values from 0 to 32767, as said below
- cotangent: float32 [12, 32768], P(None, 'node'), may hold values from -6 to 6
Outputs:
- coef_adjoint: float32 [12, 32768], P(None, ('node', 'ctr'))
- residual: float32 [12, 32768], P(None, ('node', 'ctr'))
The draws below stay inside these ranges and needn't reach their ends.
Inputs may be any that keep to these rules, and one draw needn't show every extreme that they name: `centre_idx`: all entries are distinct, and 0 and 65535 are always among them. `slab_ids`: within each aligned block of 4096 entries (the nodes of one index of node) the entries are the ids of that same block, each once.
All inputs are finite; a program needn't handle non-finite values.
Results may differ from the reference program's by a relative error of at most 0.0003.
Values sent between devices are 32-bit elements; how exact they have to be, the bound alone decides.
A program may use at most 320 MiB of HBM per device.

```python
import math
import jax
import jax.numpy as jnp
from jax import lax

C = 32768
RHS = 12
ND = 4096
ITERS = 2
NODES = 32768
SURF = 65536


def draw_centre_idx(key, part):
    first_key, second_key = jax.random.split(key)
    inner = 1 + jax.random.permutation(first_key, SURF - 2)[:C - 2].astype(jnp.int32)
    chosen = jnp.concatenate([jnp.array([0, SURF - 1], jnp.int32), inner])
    return jax.random.permutation(second_key, chosen).astype(jnp.int32)


def draw_slab_ids(key, part):
    blocks = NODES // ND
    keys = jax.random.split(key, blocks)

    def block_order(block_key):
        return jax.random.permutation(block_key, ND).astype(jnp.int32)
    orders = jax.vmap(block_order)(keys)
    offsets = (jnp.arange(blocks, dtype=jnp.int32) * ND)[:, None]
    return (orders + offsets).reshape(-1).astype(jnp.int32)


def block_levels(key, shape, cuts, smallest, top_value):
    loudness, own = 1.0, jax.random.fold_in(key, 6)
    for axis_at, shards_of in cuts:
        draws = jnp.exp(jax.random.uniform(jax.random.fold_in(own, axis_at), (shards_of,), jnp.float32, smallest / len(cuts), top_value / len(cuts)))
        loudness = loudness * jnp.repeat(draws, shape[axis_at] // shards_of).reshape([-1 if axis == axis_at else 1 for axis in range(len(shape))])
    return loudness


def bell_draw(stream_key, extent, scale, bound, shards=(), kind=jnp.bfloat16):
    values = scale * jax.random.normal(stream_key, extent, jnp.float32)
    if shards:
        values = values * block_levels(stream_key, extent, shards, -0.22, 0.18)
    return jnp.clip(values, -bound, bound).astype(kind)


def setup_inputs(seed: int = 0) -> dict:
    streams_of = jax.random.split(jax.random.key(seed), 6)
    surface_xyz = jnp.clip(1.0 * jax.random.uniform(streams_of[0], (3, SURF), jnp.float32) ** block_levels(streams_of[0], (3, SURF), ((1, 32),), -0.2, 0.2), 0.0, 1.0)
    centre_idx = draw_centre_idx(jax.random.fold_in(streams_of[5], 71), 0)
    volume_xyz = jnp.clip(1.0 * jax.random.uniform(streams_of[2], (3, NODES), jnp.float32) ** block_levels(streams_of[2], (3, NODES), ((1, 8),), -0.2, 0.2), 0.0, 1.0)
    slab_ids = draw_slab_ids(jax.random.fold_in(streams_of[5], 71), 0)
    cotangent = bell_draw(streams_of[4], (RHS, NODES), 1.0, 6.0, ((1, 8),), jnp.float32)
    return {"surface_xyz": surface_xyz, "centre_idx": centre_idx, "volume_xyz": volume_xyz, "slab_ids": slab_ids, "cotangent": cotangent}


def support_radius(count):
    return 0.2

def kernel_apply(row_xyz, col_xyz, vectors, radius, tile_entries):
    rows = row_xyz.shape[1]
    cols = col_xyz.shape[1]
    row_step = math.gcd(rows, 2048)
    col_step = math.gcd(cols, max(1, tile_entries // row_step))
    blocks = row_xyz.reshape(3, rows // row_step, row_step).transpose(1, 0, 2)
    width = vectors.shape[0]

    def one_block(block_xyz):

        def add_tile(index, acc):
            tile_xyz = lax.dynamic_slice_in_dim(col_xyz, index * col_step, col_step, 1)
            tile_vec = lax.dynamic_slice_in_dim(vectors, index * col_step, col_step, 1)
            diff_x = block_xyz[0][:, None] - tile_xyz[0][None, :]
            diff_y = block_xyz[1][:, None] - tile_xyz[1][None, :]
            diff_z = block_xyz[2][:, None] - tile_xyz[2][None, :]
            dist_sq = diff_x * diff_x + diff_y * diff_y + diff_z * diff_z
            scaled = jnp.sqrt(dist_sq) / radius
            weight = jnp.maximum(1.0 - scaled, 0.0)
            weight_sq = weight * weight
            kernel = weight_sq * weight_sq * (4.0 * scaled + 1.0)
            return acc + lax.dot_general(tile_vec, kernel, (((1,), (1,)), ((), ())), precision=lax.Precision.HIGHEST, preferred_element_type=jnp.float32)
        return lax.fori_loop(0, cols // col_step, add_tile, jnp.zeros((width, row_step), jnp.float32))
    result = lax.map(one_block, blocks)
    return result.transpose(1, 0, 2).reshape(width, rows)

def reference(surface_xyz, centre_idx, volume_xyz, slab_ids, cotangent):
    centres = jnp.take(surface_xyz, centre_idx, axis=1)
    nodes = jnp.take(volume_xyz, slab_ids, axis=1)
    radius = support_radius(centres.shape[1])
    pulled = kernel_apply(centres, nodes, cotangent, radius, 1 << 22)
    solution = jnp.zeros_like(pulled)
    resid = pulled
    direction = pulled
    norm_now = lax.optimization_barrier(jnp.sum(resid * resid, axis=1))
    for step in range(ITERS):
        image = kernel_apply(centres, centres, direction, radius, 1 << 22)
        step_len = norm_now / lax.optimization_barrier(jnp.sum(direction * image, axis=1))
        solution = solution + step_len[:, None] * direction
        resid = resid - step_len[:, None] * image
        norm_next = lax.optimization_barrier(jnp.sum(resid * resid, axis=1))
        direction = resid + (norm_next / norm_now)[:, None] * direction
        norm_now = norm_next
    return (solution, resid)
```

```python
import functools
import math

import jax
import jax.numpy as jnp
from jax import lax
from jax.experimental import pallas as pl
from jax.experimental.pallas import tpu as pltpu
from jax.sharding import PartitionSpec as P

RADIUS = 0.2
LANES = 128
GROUP = 32
BATCH = 8
PAIR = 2
CELLS = 5
DEPTH = 64
PAD = 16
VMEM = 50 * 1024 * 1024
NT = (((1,), (1,)), ((), ()))
MESH = pl.DeviceIdType.MESH


def split3(value):
    first = lax.reduce_precision(value, 8, 7)
    rest = value - first
    second = lax.reduce_precision(rest, 8, 7)
    return first, second, lax.reduce_precision(rest - second, 8, 7)


def lookup(table, ids):
    rows = table.shape[1] // LANES
    parts = jnp.concatenate([part.reshape(3, rows, LANES) for part in split3(table)], axis=0)
    parts = parts.transpose(1, 0, 2).reshape(rows, 9 * LANES).astype(jnp.bfloat16)
    high = (ids[:, None] // LANES == jnp.arange(rows, dtype=jnp.int32)[None, :]).astype(jnp.bfloat16)
    picked = jnp.dot(high, parts, preferred_element_type=jnp.float32)
    low = ids[:, None] % LANES == jnp.arange(LANES, dtype=jnp.int32)[None, :]
    picked = picked.reshape(-1, 9, LANES)
    picked = jnp.sum(jnp.where(low[:, None, :], picked, 0.0), axis=2)
    return (picked[:, 0:3] + picked[:, 3:6] + picked[:, 6:9]).T


def scaled(xyz):
    point = (xyz - 0.5) * (1.0 / RADIUS)
    return jnp.concatenate([point, jnp.ones((1, xyz.shape[1]), jnp.float32)], axis=0)


def row_features(point):
    square = jnp.sum(point[:3] * point[:3], axis=0, keepdims=True)
    alpha = jnp.concatenate(
        [jnp.ones_like(square), jnp.zeros_like(point[:3]), -2.0 * point[:3], square], axis=0
    )
    a1, a2, a3 = split3(alpha)
    return jnp.concatenate([a1, a1, a2, a2, a1, a3], axis=0).T.astype(jnp.bfloat16)


def rounded(value):
    return value.astype(jnp.bfloat16).astype(jnp.float32)


def right_factor(group):
    row = lax.broadcasted_iota(jnp.int32, group.shape, 0)
    place = jnp.where(row >= 4, group, 0.0)
    square = jnp.sum(jnp.where(row < 7, place * place, 0.0), axis=0, keepdims=True)
    beta = jnp.where(row == 0, square, place)
    b1 = rounded(beta)
    rest = beta - b1
    b2 = rounded(rest)
    b3 = rest - b2
    return jnp.concatenate([b1, b2, b1, b2, b3, b1], axis=0).astype(jnp.bfloat16)


def two_parts(vectors):
    v1 = rounded(vectors)
    return jnp.concatenate([v1, vectors - v1], axis=0).astype(jnp.bfloat16)


def sort_key(xyz):
    count = xyz.shape[1]
    cell = jnp.minimum((xyz[:2] * CELLS).astype(jnp.int32), CELLS - 1)
    deep = jnp.minimum((xyz[2] * DEPTH).astype(jnp.int32), DEPTH - 1)
    column = cell[0] * CELLS + jnp.where(cell[0] % 2 == 1, CELLS - 1 - cell[1], cell[1])
    deep = jnp.where(column % 2 == 1, DEPTH - 1 - deep, deep)
    return (column * DEPTH + deep) * count + jnp.arange(count, dtype=jnp.int32)


def boxes(points, size):
    tiles = points[:3].reshape(3, -1, size)
    return jnp.min(tiles, axis=2), jnp.max(tiles, axis=2)


def near_lists(tiles, groups):
    gap = jnp.maximum(
        jnp.maximum(tiles[0][:, :, None] - groups[1][:, None, :], groups[0][:, None, :] - tiles[1][:, :, None]),
        0.0,
    )
    near = jnp.sum(gap * gap, axis=0) < 1.0 + 1e-4
    count = jnp.sum(near.astype(jnp.int32), axis=1)
    size = near.shape[1]
    upto = (jnp.arange(size)[:, None] <= jnp.arange(size)[None, :]).astype(jnp.bfloat16)
    seen = jnp.dot(near.astype(jnp.bfloat16), upto, preferred_element_type=jnp.float32).astype(jnp.int32)
    every = jnp.arange(size, dtype=jnp.int32)
    place = jnp.where(near, seen - 1, count[:, None] + every[None, :] - seen)
    order = jnp.sum(
        jnp.where(place[:, :, None] == every[None, None, :], every[None, :, None], 0), axis=1
    )
    return count, order


def apply_body(count, order, left_ref, beta_ref, vec_ref, out_ref, acc, right, vec, items, q0, q1, k0, k1):
    rows = left_ref.shape[0]
    tiles = beta_ref.shape[0]
    span = GROUP * BATCH
    acc[...] = jnp.zeros_like(acc)
    for ref in (q0, q1, k0, k1):
        ref[...] = jnp.zeros_like(ref)

    def prepare(tile, _):
        right[tile] = right_factor(beta_ref[tile])
        parts = two_parts(vec_ref[tile])
        vec[tile] = jnp.concatenate([parts, parts], axis=1)
        return 0

    lax.fori_loop(0, tiles, prepare, 0)
    right[tiles] = jnp.zeros_like(right[tiles])
    vec[tiles] = jnp.zeros_like(vec[tiles])

    nothing = tiles * rows
    for index in range(2 * PAIR):
        items[index] = nothing

    def fill(tile, at):
        def one(batch, at):
            items[at] = tile * rows + batch * BATCH
            return at + 1

        return lax.fori_loop(0, (count[tile] + BATCH - 1) // BATCH, one, at)

    end = lax.fori_loop(0, tiles, fill, 2 * PAIR)
    for index in range(4 * PAIR):
        items[end + index] = nothing

    def item(index):
        code = items[index]
        tile = code // rows
        first = code - tile * rows
        listed = jnp.minimum(tile, tiles - 1)
        return tile, [pl.multiple_of(order[listed, first + i] * GROUP, GROUP) for i in range(BATCH)]

    def step(index, q_in, q_out, k_in, k_out):
        for unit in range(PAIR):
            tile, places = item(index * PAIR + unit)
            part = lax.dot_general(
                k_in[pl.ds(unit * span, span), :], vec[tile], NT, preferred_element_type=jnp.float32
            )
            for j, place in enumerate(places):
                acc[pl.ds(place, GROUP), :] += part[j * GROUP : (j + 1) * GROUP]
        q = jnp.minimum(jnp.maximum(q_in[...], 1e-30), 1.0)
        s = q * lax.rsqrt(q)
        w = 1.0 - s
        w2 = w * w
        k = (w2 * w2) * (0.25 + s)
        hi = k.astype(jnp.bfloat16)
        k_out[:, :LANES] = hi
        k_out[:, LANES:] = (k - hi.astype(jnp.float32)).astype(jnp.bfloat16)
        for unit in range(PAIR):
            tile, places = item((index + 2) * PAIR + unit)
            left = jnp.concatenate([left_ref[pl.ds(place, GROUP), :] for place in places], axis=0)
            q_out[pl.ds(unit * span, span), :] = jnp.dot(
                left, right[tile], preferred_element_type=jnp.float32
            )

    def two_steps(index, _):
        step(2 * index, q0, q1, k0, k1)
        step(2 * index + 1, q1, q0, k1, k0)
        return 0

    steps = (end - 2 * PAIR + PAIR - 1) // PAIR + 2
    lax.fori_loop(0, (steps + 1) // 2, two_steps, 0)

    owners, width, owned = out_ref.shape
    for owner in range(owners):
        total = acc[pl.ds(owner * owned, owned), :].T
        out_ref[owner] = 4.0 * (total[:width] + total[PAD : PAD + width])


def apply_kernel(lists, left, beta, vec, owners):
    count, order = lists
    rows = left.shape[0]
    tiles = beta.shape[0]
    width = vec.shape[1]
    vec = jnp.pad(vec, ((0, 0), (0, PAD - width), (0, 0)))
    wide = PAIR * GROUP * BATCH
    return pl.pallas_call(
        apply_body,
        out_shape=jax.ShapeDtypeStruct((owners, width, rows // owners), jnp.float32),
        in_specs=[pl.BlockSpec(memory_space=pltpu.SMEM)] * 2 + [pl.BlockSpec(memory_space=pltpu.VMEM)] * 3,
        out_specs=pl.BlockSpec(memory_space=pltpu.VMEM),
        scratch_shapes=[
            pltpu.VMEM((rows, 2 * PAD), jnp.float32),
            pltpu.VMEM((tiles + 1, 48, LANES), jnp.bfloat16),
            pltpu.VMEM((tiles + 1, 2 * PAD, 2 * LANES), jnp.bfloat16),
            pltpu.SMEM((tiles * (rows // (GROUP * BATCH)) + 8 * PAIR,), jnp.int32),
            pltpu.VMEM((wide, LANES), jnp.float32),
            pltpu.VMEM((wide, LANES), jnp.float32),
            pltpu.VMEM((wide, 2 * LANES), jnp.bfloat16),
            pltpu.VMEM((wide, 2 * LANES), jnp.bfloat16),
        ],
        compiler_params=pltpu.CompilerParams(vmem_limit_bytes=VMEM),
    )(count, order, left, beta, vec)


def node_rows_body(slab_ref, perm_ref, xyz_ref, cot_ref, xyz_out, cot_out, rows_a, rows_b, rows_c):
    count = cot_ref.shape[1]
    width = cot_ref.shape[0]
    blank = jnp.zeros((PAD - width, LANES), jnp.float32)
    for tile in range(count // LANES):
        here = pl.ds(tile * LANES, LANES)
        rows_a[here, :PAD] = jnp.concatenate([cot_ref[:, here], blank], axis=0).T

    def scatter(index, _):
        base = pl.multiple_of(index * 16, 16)
        for i in range(16):
            rows_b[pl.ds(slab_ref[base + i], 1), :] = rows_a[pl.ds(base + i, 1), :]
        return 0

    lax.fori_loop(0, count // 16, scatter, 0)
    for tile in range(count // LANES):
        here = pl.ds(tile * LANES, LANES)
        rows_b[here, PAD : PAD + 8] = xyz_ref[:, here].T

    def gather(index, _):
        base = pl.multiple_of(index * 16, 16)
        for i in range(16):
            rows_c[pl.ds(base + i, 1), :] = rows_b[pl.ds(perm_ref[base + i], 1), :]
        return 0

    lax.fori_loop(0, count // 16, gather, 0)
    for tile in range(count // LANES):
        here = rows_c[pl.ds(tile * LANES, LANES), :].T
        cot_out[tile] = here[:width]
        xyz_out[tile] = here[PAD : PAD + 8]


def node_rows(slab, perm, xyz, cotangent):
    count = cotangent.shape[1]
    width = cotangent.shape[0]
    tiles = count // LANES
    return pl.pallas_call(
        node_rows_body,
        out_shape=[
            jax.ShapeDtypeStruct((tiles, 8, LANES), jnp.float32),
            jax.ShapeDtypeStruct((tiles, width, LANES), jnp.float32),
        ],
        in_specs=[pl.BlockSpec(memory_space=pltpu.SMEM)] * 2 + [pl.BlockSpec(memory_space=pltpu.VMEM)] * 2,
        out_specs=[pl.BlockSpec(memory_space=pltpu.VMEM)] * 2,
        scratch_shapes=[pltpu.VMEM((count, LANES), jnp.float32)] * 3,
        compiler_params=pltpu.CompilerParams(vmem_limit_bytes=VMEM),
    )(slab, perm, xyz, cotangent)


def pick_body(slot_ref, table_ref, out_ref, rows_a, rows_b):
    blocks, width, span = table_ref.shape
    count = out_ref.shape[1]
    for block in range(blocks):
        for tile in range(span // LANES):
            rows_a[pl.ds(block * span + tile * LANES, LANES), :width] = table_ref[
                block, :, pl.ds(tile * LANES, LANES)
            ].T

    def gather(index, _):
        base = pl.multiple_of(index * 16, 16)
        for i in range(16):
            rows_b[pl.ds(base + i, 1), :] = rows_a[pl.ds(slot_ref[base + i], 1), :]
        return 0

    lax.fori_loop(0, count // 16, gather, 0)
    for tile in range(count // LANES):
        here = pl.ds(tile * LANES, LANES)
        out_ref[:, here] = rows_b[here, :].T[:width]


def pick(slots, table):
    blocks, width, span = table.shape
    count = slots.shape[0]
    return pl.pallas_call(
        pick_body,
        out_shape=jax.ShapeDtypeStruct((width, count), jnp.float32),
        in_specs=[pl.BlockSpec(memory_space=pltpu.SMEM), pl.BlockSpec(memory_space=pltpu.VMEM)],
        out_specs=pl.BlockSpec(memory_space=pltpu.VMEM),
        scratch_shapes=[
            pltpu.VMEM((blocks * span, LANES), jnp.float32),
            pltpu.VMEM((count, LANES), jnp.float32),
        ],
        compiler_params=pltpu.CompilerParams(vmem_limit_bytes=VMEM),
    )(slots, table)


class Links:
    def __init__(self, nodes, ctrs):
        self.nodes, self.ctrs = nodes, ctrs
        self.node, self.ctr = lax.axis_index("node"), lax.axis_index("ctr")
        self.me = self.node * ctrs + self.ctr

    def on_node(self, hop):
        return (lax.rem(self.node + hop, self.nodes), self.ctr)

    def on_ctr(self, hop):
        return (self.node, lax.rem(self.ctr + hop, self.ctrs))

    def anyone(self, hop):
        other = lax.rem(self.me + hop, self.nodes * self.ctrs)
        return (other // self.ctrs, lax.rem(other, self.ctrs))

    def meet(self, targets):
        barrier = pltpu.get_barrier_semaphore()
        for target in targets:
            pl.semaphore_signal(barrier, inc=1, device_id=target, device_id_type=MESH)
        pl.semaphore_wait(barrier, len(targets))

    def node_hops(self):
        return range(1, self.nodes)

    def ctr_hops(self):
        return range(1, self.ctrs)

    def meet_sides(self):
        self.meet([self.on_node(h) for h in self.node_hops()] + [self.on_ctr(h) for h in self.ctr_hops()])

    def meet_all(self):
        self.meet([self.anyone(h) for h in range(1, self.nodes * self.ctrs)])


def send(source, target, sems, index, device):
    copy = pltpu.make_async_remote_copy(
        src_ref=source,
        dst_ref=target,
        send_sem=sems[0].at[index],
        recv_sem=sems[1].at[index],
        device_id=device,
        device_id_type=MESH,
    )
    copy.start()
    return copy


def finish(copies):
    for copy in copies:
        copy.wait()


def comm_call(body, nodes, ctrs, out_shape, scratch, collective, *args):
    return pl.pallas_call(
        functools.partial(body, nodes, ctrs),
        out_shape=out_shape,
        in_specs=[pl.BlockSpec(memory_space=pltpu.VMEM)] * len(args),
        out_specs=jax.tree.map(lambda _: pl.BlockSpec(memory_space=pltpu.VMEM), out_shape),
        scratch_shapes=scratch,
        compiler_params=pltpu.CompilerParams(
            collective_id=collective, has_side_effects=True, vmem_limit_bytes=VMEM
        ),
    )(*args)


def dma_pair(count):
    return [pltpu.SemaphoreType.DMA((count,))] * 2


def surface_body(nodes, ctrs, own_ref, all_ref, *sems):
    links = Links(nodes, ctrs)
    links.meet_sides()
    mine = all_ref.at[links.ctr, links.node]
    copies = [send(own_ref, mine, sems, h - 1, links.on_node(h)) for h in links.node_hops()]
    all_ref[links.ctr, links.node] = own_ref[...]
    finish(copies)
    whole = all_ref.at[links.ctr]
    finish([send(whole, whole, sems, nodes - 2 + h, links.on_ctr(h)) for h in links.ctr_hops()])


def node_body(nodes, ctrs, own_ref, all_ref, *sems):
    links = Links(nodes, ctrs)
    links.meet([links.on_node(h) for h in links.node_hops()])
    mine = all_ref.at[links.node]
    copies = [send(own_ref, mine, sems, h - 1, links.on_node(h)) for h in links.node_hops()]
    all_ref[links.node] = own_ref[...]
    finish(copies)


def cross_body(nodes, ctrs, own_ref, node_ref, ctr_ref, *sems):
    links = Links(nodes, ctrs)
    links.meet_sides()
    copies = [send(own_ref, node_ref.at[links.node], sems, h - 1, links.on_node(h)) for h in links.node_hops()]
    copies += [
        send(own_ref, ctr_ref.at[links.ctr], sems, nodes - 2 + h, links.on_ctr(h)) for h in links.ctr_hops()
    ]
    node_ref[links.node] = own_ref[...]
    ctr_ref[links.ctr] = own_ref[...]
    finish(copies)


def reduced(links, part_ref, landing, sems):
    copies = []
    for h in links.node_hops():
        device = links.on_node(h)
        copies.append(send(part_ref.at[device[0]], landing.at[h - 1], sems, h - 1, device))
    total = part_ref[links.node]
    for h, copy in zip(links.node_hops(), copies):
        copy.wait()
        total = total + landing[h - 1]
    return total


def shared(links, values, own, everyone, sems):
    own[...] = jnp.concatenate(
        [jnp.broadcast_to(v, (v.shape[0], LANES // len(values))) for v in values], axis=1
    )
    hops = range(1, links.nodes * links.ctrs)
    copies = [send(own, everyone.at[links.me], sems, h - 1, links.anyone(h)) for h in hops]
    everyone[links.me] = own[...]
    finish(copies)
    total = jnp.sum(everyone[...], axis=0)
    step = LANES // len(values)
    return [total[:, i * step : i * step + 1] for i in range(len(values))]


def rowsum(value):
    return jnp.sum(value, axis=1, keepdims=True)


def pulled_body(nodes, ctrs, part_ref, own_ref, cols_ref, landing, s0, s1, t0, t1):
    links = Links(nodes, ctrs)
    links.meet_sides()
    own_ref[...] = reduced(links, part_ref, landing, (s0, s1))
    copies = [
        send(own_ref, cols_ref.at[links.ctr], (t0, t1), h - 1, links.on_ctr(h)) for h in links.ctr_hops()
    ]
    cols_ref[links.ctr] = own_ref[...]
    finish(copies)


def first_body(
    nodes, ctrs, part_ref, pulled_ref, pulled_cols, resid_ref, dir_cols, scal_ref,
    landing, cols, own0, every0, own1, every1, s0, s1, t0, t1, u0, u1, v0, v1,
):
    links = Links(nodes, ctrs)
    links.meet_all()
    image = reduced(links, part_ref, landing, (s0, s1))
    pulled = pulled_ref[...]
    norm, curve = shared(
        links, [rowsum(pulled * pulled), rowsum(pulled * image)], own0, every0, (t0, t1)
    )
    alpha = norm / curve
    resid = pulled - alpha * image
    resid_ref[...] = resid
    copies = [
        send(resid_ref, cols.at[links.ctr], (u0, u1), h - 1, links.on_ctr(h)) for h in links.ctr_hops()
    ]
    cols[links.ctr] = resid
    (after,) = shared(links, [rowsum(resid * resid)], own1, every1, (v0, v1))
    ratio = after / norm
    finish(copies)
    dir_cols[...] = cols[...] + ratio[None] * pulled_cols[...]
    step = LANES // 4
    wide = (alpha.shape[0], step)
    scal_ref[...] = jnp.concatenate(
        [jnp.broadcast_to(v, wide) for v in (alpha, ratio, after, norm)], axis=1
    )


def second_body(
    nodes, ctrs, part_ref, pulled_ref, resid_ref, scal_ref, out_ref,
    landing, final, own0, every0, s0, s1, t0, t1, u0, u1,
):
    links = Links(nodes, ctrs)
    links.meet_all()
    image = reduced(links, part_ref, landing, (s0, s1))
    pulled, resid, scal = pulled_ref[...], resid_ref[...], scal_ref[...]
    step = LANES // 4
    alpha, ratio, after = (scal[:, i * step : i * step + 1] for i in range(3))
    direction = resid + ratio * pulled
    (curve,) = shared(links, [rowsum(direction * image)], own0, every0, (t0, t1))
    second = after / curve
    final[...] = jnp.concatenate(
        [alpha * pulled + second * direction, resid - second * image], axis=0
    )
    copies = [
        send(final, out_ref.at[links.node], (u0, u1), h - 1, links.on_node(h)) for h in links.node_hops()
    ]
    out_ref[links.node] = final[...]
    finish(copies)


def local(nodes, ctrs, surface_xyz, centre_idx, volume_xyz, slab_ids, cotangent):
    width = cotangent.shape[0]
    owned = centre_idx.shape[0]
    total = owned * nodes
    here = lax.axis_index("node")
    f32 = jnp.float32
    vmem = lambda *shape: pltpu.VMEM(shape, f32)
    out = lambda *shape: jax.ShapeDtypeStruct(shape, f32)
    devices = nodes * ctrs

    slab = slab_ids % volume_xyz.shape[1]
    node_perm = lax.sort(sort_key(volume_xyz)) % volume_xyz.shape[1]
    volume_points = jnp.concatenate(
        [scaled(volume_xyz), jnp.zeros((4, volume_xyz.shape[1]), f32)], axis=0
    )
    volume_points = jnp.concatenate([volume_points[4:], volume_points[:4]], axis=0)
    node_points, node_vec = node_rows(slab, node_perm, volume_points, cotangent)

    rows = surface_xyz.shape[1] // LANES
    surface = comm_call(
        surface_body, nodes, ctrs, out(ctrs, nodes, 3, rows, LANES), dma_pair(nodes + ctrs - 2), 0,
        surface_xyz.reshape(3, rows, LANES),
    )
    surface = surface.transpose(2, 1, 0, 3, 4).reshape(3, -1)
    mine = lookup(surface, centre_idx)

    plane = comm_call(
        node_body, nodes, ctrs, out(nodes, 8, owned), dma_pair(nodes - 1), 1,
        jnp.pad(mine, ((0, 5), (0, 0))),
    )[:, :3]
    plane = plane.transpose(1, 0, 2).reshape(3, total)
    perm = lax.sort(sort_key(plane)) % total
    by_owner = perm.reshape(owned // LANES, nodes, LANES)
    own_perm = lax.dynamic_index_in_dim(by_owner, here, 1, False).reshape(owned)
    sorted_mine = scaled(lookup(plane, own_perm))
    sorted_mine = jnp.concatenate([jnp.zeros_like(sorted_mine), sorted_mine], axis=0)
    row_points, col_points = comm_call(
        cross_body, nodes, ctrs, (out(nodes, 8, owned), out(ctrs, 8, owned)), dma_pair(nodes + ctrs - 2), 2,
        sorted_mine,
    )
    row_points = row_points.transpose(1, 0, 2).reshape(8, total)[4:]
    left = row_features(row_points)
    tiles = owned // LANES

    def tiled(value):
        shape = (value.shape[0], value.shape[1], tiles, LANES)
        return value.reshape(shape).transpose(0, 2, 1, 3).reshape(-1, shape[1], LANES)

    col_tiles = tiled(col_points)
    groups = boxes(row_points, GROUP)
    flat = lambda value: value.transpose(1, 0, 2).reshape(8, -1)[4:]
    node_lists = near_lists(boxes(flat(node_points), LANES), groups)
    col_lists = near_lists(boxes(flat(col_tiles), LANES), groups)

    places = jnp.arange(total, dtype=jnp.int32)
    hit = (by_owner.transpose(1, 0, 2).reshape(total) // LANES)[None, :] == (
        here * tiles + jnp.arange(tiles, dtype=jnp.int32)
    )[:, None]
    spots = jnp.concatenate(
        [jnp.where(hit, (places // LANES)[None, :], 0), jnp.where(hit, (places % LANES)[None, :], 0)], axis=0
    ).astype(jnp.bfloat16)
    lane = (
        by_owner.transpose(1, 0, 2).reshape(total)[:, None] % LANES == jnp.arange(LANES, dtype=jnp.int32)[None, :]
    ).astype(jnp.bfloat16)
    spots = jnp.dot(spots, lane, preferred_element_type=f32).astype(jnp.int32)
    slots = (spots[:tiles] * LANES + spots[tiles:]).reshape(owned)

    part = apply_kernel(node_lists, left, node_points, node_vec, nodes)
    own_shape, small = out(width, owned), vmem(width, LANES)
    landing = vmem(nodes - 1, width, owned)
    every = vmem(devices, width, LANES)
    pulled, pulled_cols = comm_call(
        pulled_body, nodes, ctrs, (own_shape, out(ctrs, width, owned)),
        [landing] + dma_pair(nodes - 1) + dma_pair(ctrs - 1), 3, part,
    )
    part = apply_kernel(col_lists, left, col_tiles, tiled(pulled_cols), nodes)
    resid, dir_cols, scal = comm_call(
        first_body, nodes, ctrs, (own_shape, out(ctrs, width, owned), out(width, LANES)),
        [landing, vmem(ctrs, width, owned), small, every, small, every]
        + dma_pair(nodes - 1) + dma_pair(devices - 1) + dma_pair(ctrs - 1) + dma_pair(devices - 1),
        4, part, pulled, pulled_cols,
    )
    part = apply_kernel(col_lists, left, col_tiles, tiled(dir_cols), nodes)
    final = comm_call(
        second_body, nodes, ctrs, out(nodes, 2 * width, owned),
        [landing, vmem(2 * width, owned), small, every]
        + dma_pair(nodes - 1) + dma_pair(devices - 1) + dma_pair(nodes - 1),
        5, part, pulled, resid, scal,
    )
    final = pick(slots, final)
    return final[:width], final[width:]


def solution(mesh):
    return jax.shard_map(
        functools.partial(local, mesh.shape["node"], mesh.shape["ctr"]),
        mesh=mesh,
        in_specs=(
            P(None, ("node", "ctr")),
            P(("node", "ctr")),
            P(None, "node"),
            P("node"),
            P(None, "node"),
        ),
        out_specs=(P(None, ("node", "ctr")), P(None, ("node", "ctr"))),
        check_vma=False,
    )
```

```python
import functools
import math

import jax
import jax.numpy as jnp
from jax import lax
from jax.experimental import pallas as pl
from jax.experimental.pallas import tpu as pltpu
from jax.sharding import PartitionSpec as P

RADIUS = 0.2
LANES = 128
GROUP = 32
BATCH = 8
PAIR = 2
CELLS = 5
DEPTH = 64
PAD = 16
VMEM = 50 * 1024 * 1024
NT = (((1,), (1,)), ((), ()))
MESH = pl.DeviceIdType.MESH


def split3(value):
    first = lax.reduce_precision(value, 8, 7)
    rest = value - first
    second = lax.reduce_precision(rest, 8, 7)
    return first, second, lax.reduce_precision(rest - second, 8, 7)


def lookup(table, ids):
    rows = table.shape[1] // LANES
    parts = jnp.concatenate([part.reshape(3, rows, LANES) for part in split3(table)], axis=0)
    parts = parts.transpose(1, 0, 2).reshape(rows, 9 * LANES).astype(jnp.bfloat16)
    high = (ids[:, None] // LANES == jnp.arange(rows, dtype=jnp.int32)[None, :]).astype(jnp.bfloat16)
    picked = jnp.dot(high, parts, preferred_element_type=jnp.float32)
    low = ids[:, None] % LANES == jnp.arange(LANES, dtype=jnp.int32)[None, :]
    picked = picked.reshape(-1, 9, LANES)
    picked = jnp.sum(jnp.where(low[:, None, :], picked, 0.0), axis=2)
    return (picked[:, 0:3] + picked[:, 3:6] + picked[:, 6:9]).T


def scaled(xyz):
    point = (xyz - 0.5) * (1.0 / RADIUS)
    return jnp.concatenate([point, jnp.ones((1, xyz.shape[1]), jnp.float32)], axis=0)


def row_features(point):
    square = jnp.sum(point[:3] * point[:3], axis=0, keepdims=True)
    alpha = jnp.concatenate(
        [jnp.ones_like(square), jnp.zeros_like(point[:3]), -2.0 * point[:3], square], axis=0
    )
    a1, a2, a3 = split3(alpha)
    return jnp.concatenate([a1, a1, a2, a2, a1, a3], axis=0).T.astype(jnp.bfloat16)


def rounded(value):
    return value.astype(jnp.bfloat16).astype(jnp.float32)


def right_factor(group):
    row = lax.broadcasted_iota(jnp.int32, group.shape, 0)
    place = jnp.where(row >= 4, group, 0.0)
    square = jnp.sum(jnp.where(row < 7, place * place, 0.0), axis=0, keepdims=True)
    beta = jnp.where(row == 0, square, place)
    b1 = rounded(beta)
    rest = beta - b1
    b2 = rounded(rest)
    b3 = rest - b2
    return jnp.concatenate([b1, b2, b1, b2, b3, b1], axis=0).astype(jnp.bfloat16)


def two_parts(vectors):
    v1 = rounded(vectors)
    return jnp.concatenate([v1, vectors - v1], axis=0).astype(jnp.bfloat16)


def sort_key(xyz):
    count = xyz.shape[1]
    cell = jnp.minimum((xyz[:2] * CELLS).astype(jnp.int32), CELLS - 1)
    deep = jnp.minimum((xyz[2] * DEPTH).astype(jnp.int32), DEPTH - 1)
    column = cell[0] * CELLS + jnp.where(cell[0] % 2 == 1, CELLS - 1 - cell[1], cell[1])
    deep = jnp.where(column % 2 == 1, DEPTH - 1 - deep, deep)
    return (column * DEPTH + deep) * count + jnp.arange(count, dtype=jnp.int32)


def boxes(points, size):
    tiles = points[:3].reshape(3, -1, size)
    return jnp.min(tiles, axis=2), jnp.max(tiles, axis=2)


def near_lists(tiles, groups):
    gap = jnp.maximum(
        jnp.maximum(tiles[0][:, :, None] - groups[1][:, None, :], groups[0][:, None, :] - tiles[1][:, :, None]),
        0.0,
    )
    near = jnp.sum(gap * gap, axis=0) < 1.0 + 1e-4
    count = jnp.sum(near.astype(jnp.int32), axis=1)
    size = near.shape[1]
    upto = (jnp.arange(size)[:, None] <= jnp.arange(size)[None, :]).astype(jnp.bfloat16)
    seen = jnp.dot(near.astype(jnp.bfloat16), upto, preferred_element_type=jnp.float32).astype(jnp.int32)
    every = jnp.arange(size, dtype=jnp.int32)
    place = jnp.where(near, seen - 1, count[:, None] + every[None, :] - seen)
    order = jnp.sum(
        jnp.where(place[:, :, None] == every[None, None, :], every[None, :, None], 0), axis=1
    )
    return count, jnp.pad((order * GROUP).reshape(-1), (0, size))


def apply_body(count, order, left_ref, right_ref, vec_ref, out_ref, acc, vec, items, q0, q1, k0, k1):
    rows = left_ref.shape[0]
    tiles = right_ref.shape[0]
    span = GROUP * BATCH
    half = span // 2
    banks, width, deep = vec_ref.shape[:3]
    acc[...] = jnp.zeros_like(acc)
    for ref in (q0, q1, k0, k1):
        ref[...] = jnp.zeros_like(ref)

    blank = jnp.zeros((PAD - width, LANES), jnp.float32)
    for bank in range(banks):
        for at in range(deep):
            parts = two_parts(jnp.concatenate([vec_ref[bank, :, at, :], blank], axis=0))
            vec[bank * deep + at] = jnp.concatenate([parts, parts], axis=1)
    vec[tiles] = jnp.zeros_like(vec[tiles])

    groups = rows // GROUP
    nothing = tiles * groups
    for index in range(2 * PAIR):
        items[index] = nothing

    def fill(tile, at):
        def one(batch, at):
            items[at] = tile * groups + batch * BATCH
            return at + 1

        return lax.fori_loop(0, (count[tile] + BATCH - 1) // BATCH, one, at)

    end = lax.fori_loop(0, tiles, fill, 2 * PAIR)
    for index in range(4 * PAIR):
        items[end + index] = nothing

    first_half = lax.broadcasted_iota(jnp.int32, (half, LANES), 1) < LANES // 2

    def item(index):
        code = items[index]
        tile = lax.div(code, groups)
        return tile, jnp.minimum(tile, tiles - 1), [
            pl.multiple_of(order[code + i], GROUP) for i in range(BATCH)
        ]

    def rows_at(places):
        return jnp.concatenate([left_ref[pl.ds(place, GROUP), :] for place in places], axis=0)

    def step(index, q_in, q_out, k_in, k_out):
        for unit in range(PAIR):
            tile, _, places = item(index * PAIR + unit)
            part = lax.dot_general(
                k_in[pl.ds(unit * span, span), :], vec[tile], NT, preferred_element_type=jnp.float32
            )
            for j, place in enumerate(places):
                acc[pl.ds(place, GROUP), :] += part[j * GROUP : (j + 1) * GROUP]
        for unit in range(PAIR):
            q = jnp.minimum(jnp.maximum(q_in[pl.ds(unit * half, half), :], 1e-30), 1.0)
            s = q * lax.rsqrt(q)
            w = 1.0 - s
            w2 = w * w
            k = (w2 * w2) * (0.25 + s)
            hi = k.astype(jnp.bfloat16)
            lo = (k - hi.astype(jnp.float32)).astype(jnp.bfloat16)
            for side in range(2):
                here = pl.ds(unit * span + side * half, half)
                lanes = slice(side * LANES, (side + 1) * LANES)
                k_out[here, :LANES] = hi[:, lanes]
                k_out[here, LANES:] = lo[:, lanes]
        for unit in range(PAIR):
            _, listed, places = item((index + 2) * PAIR + unit)
            left = jnp.where(first_half, rows_at(places[: BATCH // 2]), rows_at(places[BATCH // 2 :]))
            q_out[pl.ds(unit * half, half), :] = jnp.dot(
                left, right_ref[listed], preferred_element_type=jnp.float32
            )

    def two_steps(index, _):
        step(2 * index, q0, q1, k0, k1)
        step(2 * index + 1, q1, q0, k1, k0)
        return 0

    steps = (end - 2 * PAIR + PAIR - 1) // PAIR + 2
    lax.fori_loop(0, (steps + 1) // 2, two_steps, 0)

    owners, _, high, _ = out_ref.shape
    for owner in range(owners):
        for at in range(high):
            total = acc[pl.ds((owner * high + at) * LANES, LANES), :].T
            out_ref[owner, :, at, :] = 4.0 * (total[:width] + total[PAD : PAD + width])


def apply_kernel(lists, left, right, vec, owners):
    count, order = lists
    rows = left.shape[0]
    tiles = right.shape[0]
    width = vec.shape[1]
    wide = PAIR * GROUP * BATCH
    return pl.pallas_call(
        apply_body,
        out_shape=jax.ShapeDtypeStruct((owners, width, rows // owners // LANES, LANES), jnp.float32),
        in_specs=[pl.BlockSpec(memory_space=pltpu.SMEM)] * 2 + [pl.BlockSpec(memory_space=pltpu.VMEM)] * 3,
        out_specs=pl.BlockSpec(memory_space=pltpu.VMEM),
        scratch_shapes=[
            pltpu.VMEM((rows, 2 * PAD), jnp.float32),
            pltpu.VMEM((tiles + 1, 2 * PAD, 2 * LANES), jnp.bfloat16),
            pltpu.SMEM((tiles * (rows // (GROUP * BATCH)) + 8 * PAIR,), jnp.int32),
            pltpu.VMEM((wide // 2, 2 * LANES), jnp.float32),
            pltpu.VMEM((wide // 2, 2 * LANES), jnp.float32),
            pltpu.VMEM((wide, 2 * LANES), jnp.bfloat16),
            pltpu.VMEM((wide, 2 * LANES), jnp.bfloat16),
        ],
        compiler_params=pltpu.CompilerParams(vmem_limit_bytes=VMEM),
    )(count, order, left, right, vec)


def factor_body(row_ref, col_ref, node_ref, left_ref, col_out, node_out):
    blocks, _, span = row_ref.shape
    blank = jnp.zeros((16, LANES), jnp.float32)
    for block in range(blocks):
        for at in range(span // LANES):
            group = row_ref[block, :, pl.ds(at * LANES, LANES)]
            row = lax.broadcasted_iota(jnp.int32, group.shape, 0)
            place = jnp.where((row >= 4) & (row < 7), group, 0.0)
            square = jnp.sum(place * place, axis=0, keepdims=True)
            alpha = jnp.where(row == 0, 1.0, jnp.where(row == 7, square, -2.0 * place))
            a1 = rounded(alpha)
            a2 = rounded(alpha - a1)
            a3 = alpha - a1 - a2
            parts = [a1, a1, a2, a2, a1, a3, blank]
            left_ref[pl.ds((block * (span // LANES) + at) * LANES, LANES), :] = (
                jnp.concatenate(parts + parts, axis=0).T.astype(jnp.bfloat16)
            )

    def fill(source, target):
        blocks, _, span = source.shape
        per = span // LANES
        zero = jnp.zeros((64, LANES), jnp.bfloat16)
        pad = jnp.zeros((16, LANES), jnp.bfloat16)
        for block in range(blocks):
            for at in range(per):
                right = jnp.concatenate([right_factor(source[block, :, pl.ds(at * LANES, LANES)]), pad], axis=0)
                target[block * per + at] = jnp.concatenate(
                    [jnp.concatenate([right, zero], axis=0), jnp.concatenate([zero, right], axis=0)], axis=1
                )

    fill(col_ref, col_out)
    fill(node_ref, node_out)


def factors(row_points, col_points, node_points):
    def tiles(points):
        return points.shape[0] * points.shape[2] // LANES

    def shape(points):
        return jax.ShapeDtypeStruct((tiles(points), LANES, 2 * LANES), jnp.bfloat16)

    return pl.pallas_call(
        factor_body,
        out_shape=[
            jax.ShapeDtypeStruct((tiles(row_points) * LANES, LANES), jnp.bfloat16),
            shape(col_points),
            shape(node_points),
        ],
        in_specs=[pl.BlockSpec(memory_space=pltpu.VMEM)] * 3,
        out_specs=[pl.BlockSpec(memory_space=pltpu.VMEM)] * 3,
        compiler_params=pltpu.CompilerParams(vmem_limit_bytes=VMEM),
    )(row_points, col_points, node_points)


def node_rows_body(slab_ref, perm_ref, xyz_ref, cot_ref, xyz_out, cot_out, rows_a, rows_b, rows_c):
    count = cot_ref.shape[1]
    width = cot_ref.shape[0]
    blank = jnp.zeros((PAD - width, LANES), jnp.float32)
    for tile in range(count // LANES):
        here = pl.ds(tile * LANES, LANES)
        rows_a[here, :PAD] = jnp.concatenate([cot_ref[:, here], blank], axis=0).T

    def scatter(index, _):
        base = pl.multiple_of(index * 16, 16)
        for i in range(16):
            rows_b[pl.ds(slab_ref[base + i], 1), :] = rows_a[pl.ds(base + i, 1), :]
        return 0

    lax.fori_loop(0, count // 16, scatter, 0)
    for tile in range(count // LANES):
        here = pl.ds(tile * LANES, LANES)
        rows_b[here, PAD : PAD + 8] = xyz_ref[:, here].T

    def gather(index, _):
        base = pl.multiple_of(index * 16, 16)
        for i in range(16):
            rows_c[pl.ds(base + i, 1), :] = rows_b[pl.ds(perm_ref[base + i], 1), :]
        return 0

    lax.fori_loop(0, count // 16, gather, 0)
    for tile in range(count // LANES):
        here = rows_c[pl.ds(tile * LANES, LANES), :].T
        cot_out[0, :, tile, :] = here[:width]
        xyz_out[0, :, pl.ds(tile * LANES, LANES)] = here[PAD : PAD + 8]


def node_rows(slab, perm, xyz, cotangent):
    count = cotangent.shape[1]
    width = cotangent.shape[0]
    tiles = count // LANES
    return pl.pallas_call(
        node_rows_body,
        out_shape=[
            jax.ShapeDtypeStruct((1, 8, count), jnp.float32),
            jax.ShapeDtypeStruct((1, width, tiles, LANES), jnp.float32),
        ],
        in_specs=[pl.BlockSpec(memory_space=pltpu.SMEM)] * 2 + [pl.BlockSpec(memory_space=pltpu.VMEM)] * 2,
        out_specs=[pl.BlockSpec(memory_space=pltpu.VMEM)] * 2,
        scratch_shapes=[pltpu.VMEM((count, LANES), jnp.float32)] * 3,
        compiler_params=pltpu.CompilerParams(vmem_limit_bytes=VMEM),
    )(slab, perm, xyz, cotangent)


def pick_body(slot_ref, table_ref, out_ref, rows_a, rows_b):
    blocks, width, deep, _ = table_ref.shape
    count = out_ref.shape[1]
    for block in range(blocks):
        for tile in range(deep):
            rows_a[pl.ds((block * deep + tile) * LANES, LANES), :width] = table_ref[block, :, tile, :].T

    def gather(index, _):
        base = pl.multiple_of(index * 16, 16)
        for i in range(16):
            rows_b[pl.ds(base + i, 1), :] = rows_a[pl.ds(slot_ref[base + i], 1), :]
        return 0

    lax.fori_loop(0, count // 16, gather, 0)
    for tile in range(count // LANES):
        here = pl.ds(tile * LANES, LANES)
        out_ref[:, here] = rows_b[here, :].T[:width]


def pick(slots, table):
    blocks, width, deep, _ = table.shape
    count = slots.shape[0]
    return pl.pallas_call(
        pick_body,
        out_shape=jax.ShapeDtypeStruct((width, count), jnp.float32),
        in_specs=[pl.BlockSpec(memory_space=pltpu.SMEM), pl.BlockSpec(memory_space=pltpu.VMEM)],
        out_specs=pl.BlockSpec(memory_space=pltpu.VMEM),
        scratch_shapes=[
            pltpu.VMEM((blocks * deep * LANES, LANES), jnp.float32),
            pltpu.VMEM((count, LANES), jnp.float32),
        ],
        compiler_params=pltpu.CompilerParams(vmem_limit_bytes=VMEM),
    )(slots, table)


class Links:
    def __init__(self, nodes, ctrs):
        self.nodes, self.ctrs = nodes, ctrs
        self.node, self.ctr = lax.axis_index("node"), lax.axis_index("ctr")
        self.me = self.node * ctrs + self.ctr

    def on_node(self, hop):
        return (lax.rem(self.node + hop, self.nodes), self.ctr)

    def on_ctr(self, hop):
        return (self.node, lax.rem(self.ctr + hop, self.ctrs))

    def anyone(self, hop):
        other = lax.rem(self.me + hop, self.nodes * self.ctrs)
        return (other // self.ctrs, lax.rem(other, self.ctrs))

    def meet(self, targets):
        barrier = pltpu.get_barrier_semaphore()
        for target in targets:
            pl.semaphore_signal(barrier, inc=1, device_id=target, device_id_type=MESH)
        pl.semaphore_wait(barrier, len(targets))

    def node_hops(self):
        return range(1, self.nodes)

    def ctr_hops(self):
        return range(1, self.ctrs)

    def meet_sides(self):
        self.meet([self.on_node(h) for h in self.node_hops()] + [self.on_ctr(h) for h in self.ctr_hops()])

    def meet_all(self):
        self.meet([self.anyone(h) for h in range(1, self.nodes * self.ctrs)])


def send(source, target, sems, index, device):
    copy = pltpu.make_async_remote_copy(
        src_ref=source,
        dst_ref=target,
        send_sem=sems[0].at[index],
        recv_sem=sems[1].at[index],
        device_id=device,
        device_id_type=MESH,
    )
    copy.start()
    return copy


def finish(copies):
    for copy in copies:
        copy.wait()


def comm_call(body, nodes, ctrs, out_shape, scratch, collective, *args):
    return pl.pallas_call(
        functools.partial(body, nodes, ctrs),
        out_shape=out_shape,
        in_specs=[pl.BlockSpec(memory_space=pltpu.VMEM)] * len(args),
        out_specs=jax.tree.map(lambda _: pl.BlockSpec(memory_space=pltpu.VMEM), out_shape),
        scratch_shapes=scratch,
        compiler_params=pltpu.CompilerParams(
            collective_id=collective, has_side_effects=True, vmem_limit_bytes=VMEM
        ),
    )(*args)


def dma_pair(count):
    return [pltpu.SemaphoreType.DMA((count,))] * 2


def surface_body(nodes, ctrs, own_ref, all_ref, *sems):
    links = Links(nodes, ctrs)
    links.meet_sides()
    mine = all_ref.at[links.ctr, links.node]
    copies = [send(own_ref, mine, sems, h - 1, links.on_node(h)) for h in links.node_hops()]
    all_ref[links.ctr, links.node] = own_ref[...]
    finish(copies)
    whole = all_ref.at[links.ctr]
    last = nodes - 1
    if ctrs != 4:
        finish([send(whole, whole, sems, last - 1 + h, links.on_ctr(h)) for h in links.ctr_hops()])
        return
    far = lax.rem(links.ctr + 2, 4)
    near = (links.node, links.ctr + 1 - 2 * lax.rem(links.ctr, 2))
    across = send(whole, whole, sems, last, (links.node, far))
    beside = send(whole, whole, sems, last + 1, near)
    across.wait()
    other = all_ref.at[far]
    finish([send(other, other, sems, last + 2, near), beside])


def node_body(nodes, ctrs, own_ref, all_ref, *sems):
    links = Links(nodes, ctrs)
    links.meet([links.on_node(h) for h in links.node_hops()])
    mine = all_ref.at[links.node]
    copies = [send(own_ref, mine, sems, h - 1, links.on_node(h)) for h in links.node_hops()]
    all_ref[links.node] = own_ref[...]
    finish(copies)


def cross_body(nodes, ctrs, own_ref, node_ref, ctr_ref, *sems):
    links = Links(nodes, ctrs)
    links.meet_sides()
    copies = [send(own_ref, node_ref.at[links.node], sems, h - 1, links.on_node(h)) for h in links.node_hops()]
    copies += [
        send(own_ref, ctr_ref.at[links.ctr], sems, nodes - 2 + h, links.on_ctr(h)) for h in links.ctr_hops()
    ]
    node_ref[links.node] = own_ref[...]
    ctr_ref[links.ctr] = own_ref[...]
    finish(copies)


def reduced(links, part_ref, landing, sems):
    copies = []
    for h in links.node_hops():
        device = links.on_node(h)
        copies.append(send(part_ref.at[device[0]], landing.at[h - 1], sems, h - 1, device))
    total = part_ref[links.node]
    for h, copy in zip(links.node_hops(), copies):
        copy.wait()
        total = total + landing[h - 1]
    return total


def wanted(rows, index):
    row = lax.broadcasted_iota(jnp.int32, (rows, LANES), 0)
    lane = lax.broadcasted_iota(jnp.int32, (rows, LANES), 1)
    return lane == row + 32 * index


def share_start(links, values, own, everyone, sems):
    line = 0.0
    for index, value in enumerate(values):
        column = jnp.sum(jnp.sum(value, axis=1), axis=1, keepdims=True)
        line += jnp.sum(
            jnp.where(wanted(column.shape[0], index), column, 0.0), axis=0, keepdims=True
        )
    own[...] = line
    hops = range(1, links.nodes * links.ctrs)
    copies = [send(own, everyone.at[links.me], sems, h - 1, links.anyone(h)) for h in hops]
    everyone[links.me] = own[...]
    return copies


def share_end(copies, count, rows, everyone):
    finish(copies)
    line = jnp.sum(everyone[...], axis=0)
    return [
        jnp.sum(jnp.where(wanted(rows, index), line, 0.0), axis=1, keepdims=True) for index in range(count)
    ]


def spread(column, ref):
    ref[...] = jnp.broadcast_to(column, ref.shape)
    return [ref[v : v + 1, :] for v in range(ref.shape[0])]


def pulled_body(nodes, ctrs, part_ref, own_ref, cols_ref, landing, s0, s1, t0, t1):
    links = Links(nodes, ctrs)
    links.meet_sides()
    own_ref[...] = reduced(links, part_ref, landing, (s0, s1))
    copies = [
        send(own_ref, cols_ref.at[links.ctr], (t0, t1), h - 1, links.on_ctr(h)) for h in links.ctr_hops()
    ]
    cols_ref[links.ctr] = own_ref[...]
    finish(copies)


def first_body(
    nodes, ctrs, part_ref, pulled_ref, pulled_cols, resid_ref, dir_cols, scal_ref,
    landing, image_ref, cols, line, every, scr0, scr1, s0, s1, t0, t1, u0, u1,
):
    links = Links(nodes, ctrs)
    links.meet_all()
    image = reduced(links, part_ref, landing, (s0, s1))
    image_ref[...] = image
    pulled = pulled_ref[...]
    told = share_start(
        links, [pulled * pulled, pulled * image, image * image], line, every, (t0, t1)
    )
    copies = [
        send(image_ref, cols.at[links.ctr], (u0, u1), h - 1, links.on_ctr(h)) for h in links.ctr_hops()
    ]
    cols[links.ctr] = image
    width = pulled_ref.shape[0]
    norm, curve, square = share_end(told, 3, width, every)
    alpha = norm / curve
    ratio = alpha * square / curve - 1.0
    alphas, ratios = spread(alpha, scr0), spread(ratio, scr1)
    scal_ref[0] = scr0[...]
    scal_ref[1] = scr1[...]
    for v in range(width):
        resid_ref[v] = pulled_ref[v] - alphas[v] * image_ref[v]
    finish(copies)
    for c in range(ctrs):
        for v in range(width):
            dir_cols[c, v] = (pulled_cols[c, v] - alphas[v] * cols[c, v]) + ratios[v] * pulled_cols[c, v]


def second_body(
    nodes, ctrs, part_ref, pulled_ref, resid_ref, scal_ref, out_ref,
    landing, final, line, every, scr0, s0, s1, t0, t1, u0, u1,
):
    links = Links(nodes, ctrs)
    links.meet_all()
    image = reduced(links, part_ref, landing, (s0, s1))
    width = pulled_ref.shape[0]
    alphas = [scal_ref[0, v : v + 1, :] for v in range(width)]
    ratios = [scal_ref[1, v : v + 1, :] for v in range(width)]
    for v in range(width):
        final[v] = resid_ref[v] + ratios[v] * pulled_ref[v]
    resid = resid_ref[...]
    told = share_start(links, [resid * resid, final[:width] * image], line, every, (t0, t1))
    final[width:] = image
    norm, curve = share_end(told, 2, width, every)
    seconds = spread(norm / curve, scr0)
    for v in range(width):
        final[v] = alphas[v] * pulled_ref[v] + seconds[v] * final[v]
        final[width + v] = resid_ref[v] - seconds[v] * final[width + v]
    copies = [
        send(final, out_ref.at[links.node], (u0, u1), h - 1, links.on_node(h)) for h in links.node_hops()
    ]
    out_ref[links.node] = final[...]
    finish(copies)


def local(nodes, ctrs, surface_xyz, centre_idx, volume_xyz, slab_ids, cotangent):
    width = cotangent.shape[0]
    owned = centre_idx.shape[0]
    total = owned * nodes
    here = lax.axis_index("node")
    f32 = jnp.float32
    vmem = lambda *shape: pltpu.VMEM(shape, f32)
    out = lambda *shape: jax.ShapeDtypeStruct(shape, f32)
    devices = nodes * ctrs

    slab = slab_ids % volume_xyz.shape[1]
    node_perm = lax.sort(sort_key(volume_xyz)) % volume_xyz.shape[1]
    volume_points = jnp.concatenate(
        [scaled(volume_xyz), jnp.zeros((4, volume_xyz.shape[1]), f32)], axis=0
    )
    volume_points = jnp.concatenate([volume_points[4:], volume_points[:4]], axis=0)
    node_points, node_vec = node_rows(slab, node_perm, volume_points, cotangent)

    rows = surface_xyz.shape[1] // LANES
    surface = comm_call(
        surface_body, nodes, ctrs, out(ctrs, nodes, 3, rows, LANES), dma_pair(nodes + ctrs - 2), 0,
        surface_xyz.reshape(3, rows, LANES),
    )
    surface = surface.transpose(2, 1, 0, 3, 4).reshape(3, -1)
    mine = lookup(surface, centre_idx)

    plane = comm_call(
        node_body, nodes, ctrs, out(nodes, 8, owned), dma_pair(nodes - 1), 1,
        jnp.pad(mine, ((0, 5), (0, 0))),
    )[:, :3]
    plane = plane.transpose(1, 0, 2).reshape(3, total)
    perm = lax.sort(sort_key(plane)) % total
    by_owner = perm.reshape(owned // LANES, nodes, LANES)
    own_perm = lax.dynamic_index_in_dim(by_owner, here, 1, False).reshape(owned)
    sorted_mine = scaled(lookup(plane, own_perm))
    sorted_mine = jnp.concatenate([jnp.zeros_like(sorted_mine), sorted_mine], axis=0)
    row_points, col_points = comm_call(
        cross_body, nodes, ctrs, (out(nodes, 8, owned), out(ctrs, 8, owned)), dma_pair(nodes + ctrs - 2), 2,
        sorted_mine,
    )
    left, col_right, node_right = factors(row_points, col_points, node_points)
    tiles = owned // LANES
    flat = lambda value: value.transpose(1, 0, 2).reshape(8, -1)[4:]
    groups = boxes(flat(row_points), GROUP)
    node_lists = near_lists(boxes(flat(node_points), LANES), groups)
    col_lists = near_lists(boxes(flat(col_points), LANES), groups)

    places = jnp.arange(total, dtype=jnp.int32)
    hit = (by_owner.transpose(1, 0, 2).reshape(total) // LANES)[None, :] == (
        here * tiles + jnp.arange(tiles, dtype=jnp.int32)
    )[:, None]
    spots = jnp.concatenate(
        [jnp.where(hit, (places // LANES)[None, :], 0), jnp.where(hit, (places % LANES)[None, :], 0)], axis=0
    ).astype(jnp.bfloat16)
    lane = (
        by_owner.transpose(1, 0, 2).reshape(total)[:, None] % LANES == jnp.arange(LANES, dtype=jnp.int32)[None, :]
    ).astype(jnp.bfloat16)
    spots = jnp.dot(spots, lane, preferred_element_type=f32).astype(jnp.int32)
    slots = (spots[:tiles] * LANES + spots[tiles:]).reshape(owned)

    own_shape, scr = out(width, tiles, LANES), vmem(width, LANES)
    cols_shape = out(ctrs, width, tiles, LANES)
    landing = vmem(nodes - 1, width, tiles, LANES)
    line, every = vmem(1, LANES), vmem(devices, 1, LANES)
    part = apply_kernel(node_lists, left, node_right, node_vec, nodes)
    pulled, pulled_cols = comm_call(
        pulled_body, nodes, ctrs, (own_shape, cols_shape),
        [landing] + dma_pair(nodes - 1) + dma_pair(ctrs - 1), 3, part,
    )
    part = apply_kernel(col_lists, left, col_right, pulled_cols, nodes)
    resid, dir_cols, scal = comm_call(
        first_body, nodes, ctrs, (own_shape, cols_shape, out(2, width, LANES)),
        [landing, vmem(width, tiles, LANES), vmem(ctrs, width, tiles, LANES), line, every, scr, scr]
        + dma_pair(nodes - 1) + dma_pair(devices - 1) + dma_pair(ctrs - 1),
        4, part, pulled, pulled_cols,
    )
    part = apply_kernel(col_lists, left, col_right, dir_cols, nodes)
    final = comm_call(
        second_body, nodes, ctrs, out(nodes, 2 * width, tiles, LANES),
        [landing, vmem(2 * width, tiles, LANES), line, every, scr]
        + dma_pair(nodes - 1) + dma_pair(devices - 1) + dma_pair(nodes - 1),
        5, part, pulled, resid, scal,
    )
    final = pick(slots, final)
    return final[:width], final[width:]


def solution(mesh):
    return jax.shard_map(
        functools.partial(local, mesh.shape["node"], mesh.shape["ctr"]),
        mesh=mesh,
        in_specs=(
            P(None, ("node", "ctr")),
            P(("node", "ctr")),
            P(None, "node"),
            P("node"),
            P(None, "node"),
        ),
        out_specs=(P(None, ("node", "ctr")), P(None, ("node", "ctr"))),
        check_vma=False,
    )
```

```python
import functools
import math

import jax
import jax.numpy as jnp
from jax import lax
from jax.experimental import pallas as pl
from jax.experimental.pallas import tpu as pltpu
from jax.sharding import PartitionSpec as P

RADIUS = 0.2
LANES = 128
GROUP = 32
BATCH = 8
PAIR = 2
CELLS = 5
DEPTH = 64
PAD = 16
VMEM = 50 * 1024 * 1024
NT = (((1,), (1,)), ((), ()))
MESH = pl.DeviceIdType.MESH


def split3(value):
    first = lax.reduce_precision(value, 8, 7)
    rest = value - first
    second = lax.reduce_precision(rest, 8, 7)
    return first, second, lax.reduce_precision(rest - second, 8, 7)


def lookup(table, ids):
    rows = table.shape[1] // LANES
    parts = jnp.concatenate([part.reshape(3, rows, LANES) for part in split3(table)], axis=0)
    parts = parts.transpose(1, 0, 2).reshape(rows, 9 * LANES).astype(jnp.bfloat16)
    high = (ids[:, None] // LANES == jnp.arange(rows, dtype=jnp.int32)[None, :]).astype(jnp.bfloat16)
    picked = jnp.dot(high, parts, preferred_element_type=jnp.float32)
    low = ids[:, None] % LANES == jnp.arange(LANES, dtype=jnp.int32)[None, :]
    picked = picked.reshape(-1, 9, LANES)
    picked = jnp.sum(jnp.where(low[:, None, :], picked, 0.0), axis=2)
    return (picked[:, 0:3] + picked[:, 3:6] + picked[:, 6:9]).T


def scaled(xyz):
    point = (xyz - 0.5) * (1.0 / RADIUS)
    return jnp.concatenate([point, jnp.ones((1, xyz.shape[1]), jnp.float32)], axis=0)


def row_features(point):
    square = jnp.sum(point[:3] * point[:3], axis=0, keepdims=True)
    alpha = jnp.concatenate(
        [jnp.ones_like(square), jnp.zeros_like(point[:3]), -2.0 * point[:3], square], axis=0
    )
    a1, a2, a3 = split3(alpha)
    return jnp.concatenate([a1, a1, a2, a2, a1, a3], axis=0).T.astype(jnp.bfloat16)


def rounded(value):
    return value.astype(jnp.bfloat16).astype(jnp.float32)


def right_factor(group):
    row = lax.broadcasted_iota(jnp.int32, group.shape, 0)
    place = jnp.where(row >= 4, group, 0.0)
    square = jnp.sum(jnp.where(row < 7, place * place, 0.0), axis=0, keepdims=True)
    beta = jnp.where(row == 0, square, place)
    b1 = rounded(beta)
    rest = beta - b1
    b2 = rounded(rest)
    b3 = rest - b2
    return jnp.concatenate([b1, b2, b1, b2, b3, b1], axis=0).astype(jnp.bfloat16)


def two_parts(vectors):
    v1 = rounded(vectors)
    return jnp.concatenate([v1, vectors - v1], axis=0).astype(jnp.bfloat16)


def sort_key(xyz):
    count = xyz.shape[1]
    cell = jnp.minimum((xyz[:2] * CELLS).astype(jnp.int32), CELLS - 1)
    deep = jnp.minimum((xyz[2] * DEPTH).astype(jnp.int32), DEPTH - 1)
    column = cell[0] * CELLS + jnp.where(cell[0] % 2 == 1, CELLS - 1 - cell[1], cell[1])
    deep = jnp.where(column % 2 == 1, DEPTH - 1 - deep, deep)
    return (column * DEPTH + deep) * count + jnp.arange(count, dtype=jnp.int32)


def boxes(points, size):
    tiles = points[:3].reshape(3, -1, size)
    return jnp.min(tiles, axis=2), jnp.max(tiles, axis=2)


def near_lists(tiles, groups, pieces):
    gap = jnp.maximum(
        jnp.maximum(tiles[0][:, :, None] - groups[1][:, None, :], groups[0][:, None, :] - tiles[1][:, :, None]),
        0.0,
    )
    near = jnp.sum(gap * gap, axis=0) < 1.0 + 1e-4
    size = near.shape[1]
    near = jnp.any(near.reshape(-1, pieces, size), axis=1)
    total = near.shape[0]
    count = jnp.sum(near.astype(jnp.int32), axis=1)
    upto = (jnp.arange(size)[:, None] <= jnp.arange(size)[None, :]).astype(jnp.bfloat16)
    seen = jnp.dot(near.astype(jnp.bfloat16), upto, preferred_element_type=jnp.float32).astype(jnp.int32)
    every = jnp.arange(size, dtype=jnp.int32)
    place = jnp.where(near, seen - 1, count[:, None] + every[None, :] - seen)
    order = jnp.sum(
        jnp.where(place[:, :, None] == every[None, None, :], every[None, :, None], 0), axis=1
    )
    batches = (count + BATCH - 1) // BATCH
    ranks = jnp.arange(total)
    ends = jnp.sum(jnp.where(ranks[:, None] <= ranks[None, :], batches[:, None], 0), axis=0)
    at = jnp.arange(total * size // BATCH + 8 * PAIR, dtype=jnp.int32) - 2 * PAIR
    passed = ends[:, None] <= at[None, :]
    tile = jnp.sum(passed.astype(jnp.int32), axis=0)
    start = jnp.sum(jnp.where(passed, batches[:, None], 0), axis=0)
    code = tile * size + (at - start) * BATCH
    items = jnp.where((at < 0) | (tile == total), total * size, code)
    return ends[-1:], items, jnp.pad((order * GROUP).reshape(-1), (0, size))


def apply_body(count, items, order, left_ref, right_ref, vec_ref, out_ref, acc, vec, q0, q1, k0, k1):
    rows = left_ref.shape[0]
    tiles = right_ref.shape[0]
    span = GROUP * BATCH
    half = span // 2
    banks, width, deep = vec_ref.shape[:3]
    acc[...] = jnp.zeros_like(acc)
    for ref in (q0, q1, k0, k1):
        ref[...] = jnp.zeros_like(ref)

    blank = jnp.zeros((PAD - width, LANES), jnp.float32)
    for bank in range(banks):
        for at in range(deep):
            parts = two_parts(jnp.concatenate([vec_ref[bank, :, at, :], blank], axis=0))
            vec[bank * deep + at] = jnp.concatenate([parts, parts], axis=1)
    vec[tiles] = jnp.zeros_like(vec[tiles])

    groups = rows // GROUP
    first_half = lax.broadcasted_iota(jnp.int32, (half, LANES), 1) < LANES // 2

    def item(index):
        code = items[index]
        tile = lax.div(code, groups)
        return tile, jnp.minimum(tile, tiles - 1), [
            pl.multiple_of(order[code + i], GROUP) for i in range(BATCH)
        ]

    def rows_at(places):
        return jnp.concatenate([left_ref[pl.ds(place, GROUP), :] for place in places], axis=0)

    def step(index, q_in, q_out, k_in, k_out):
        for unit in range(PAIR):
            tile, _, places = item(index * PAIR + unit)
            part = lax.dot_general(
                k_in[pl.ds(unit * span, span), :], vec[tile], NT, preferred_element_type=jnp.float32
            )
            for j, place in enumerate(places):
                acc[pl.ds(place, GROUP), :] += part[j * GROUP : (j + 1) * GROUP]
        for unit in range(PAIR):
            q = jnp.minimum(jnp.maximum(q_in[pl.ds(unit * half, half), :], 1e-30), 1.0)
            s = q * lax.rsqrt(q)
            w = 1.0 - s
            w2 = w * w
            k = (w2 * w2) * (0.25 + s)
            hi = k.astype(jnp.bfloat16)
            lo = (k - hi.astype(jnp.float32)).astype(jnp.bfloat16)
            for side in range(2):
                here = pl.ds(unit * span + side * half, half)
                lanes = slice(side * LANES, (side + 1) * LANES)
                k_out[here, :LANES] = hi[:, lanes]
                k_out[here, LANES:] = lo[:, lanes]
        for unit in range(PAIR):
            _, listed, places = item((index + 2) * PAIR + unit)
            left = jnp.where(first_half, rows_at(places[: BATCH // 2]), rows_at(places[BATCH // 2 :]))
            q_out[pl.ds(unit * half, half), :] = jnp.dot(
                left, right_ref[listed], preferred_element_type=jnp.float32
            )

    def two_steps(index, _):
        step(2 * index, q0, q1, k0, k1)
        step(2 * index + 1, q1, q0, k1, k0)
        return 0

    steps = (count[0] + PAIR - 1) // PAIR + 2
    lax.fori_loop(0, (steps + 1) // 2, two_steps, 0)

    owners, _, high, _ = out_ref.shape
    for owner in range(owners):
        for at in range(high):
            total = acc[pl.ds((owner * high + at) * LANES, LANES), :].T
            out_ref[owner, :, at, :] = 4.0 * (total[:width] + total[PAD : PAD + width])


def apply_kernel(lists, left, right, vec, owners):
    rows = left.shape[0]
    tiles = right.shape[0]
    width = vec.shape[1]
    wide = PAIR * GROUP * BATCH
    return pl.pallas_call(
        apply_body,
        out_shape=jax.ShapeDtypeStruct((owners, width, rows // owners // LANES, LANES), jnp.float32),
        in_specs=[pl.BlockSpec(memory_space=pltpu.SMEM)] * 3 + [pl.BlockSpec(memory_space=pltpu.VMEM)] * 3,
        out_specs=pl.BlockSpec(memory_space=pltpu.VMEM),
        scratch_shapes=[
            pltpu.VMEM((rows, 2 * PAD), jnp.float32),
            pltpu.VMEM((tiles + 1, 2 * PAD, 2 * LANES), jnp.bfloat16),
            pltpu.VMEM((wide // 2, 2 * LANES), jnp.float32),
            pltpu.VMEM((wide // 2, 2 * LANES), jnp.float32),
            pltpu.VMEM((wide, 2 * LANES), jnp.bfloat16),
            pltpu.VMEM((wide, 2 * LANES), jnp.bfloat16),
        ],
        compiler_params=pltpu.CompilerParams(vmem_limit_bytes=VMEM),
    )(*lists, left, right, vec)


def factor_body(row_ref, col_ref, node_ref, left_ref, col_out, node_out):
    blocks, _, span = row_ref.shape
    blank = jnp.zeros((16, LANES), jnp.float32)
    for block in range(blocks):
        for at in range(span // LANES):
            group = row_ref[block, :, pl.ds(at * LANES, LANES)]
            row = lax.broadcasted_iota(jnp.int32, group.shape, 0)
            place = jnp.where((row >= 4) & (row < 7), group, 0.0)
            square = jnp.sum(place * place, axis=0, keepdims=True)
            alpha = jnp.where(row == 0, 1.0, jnp.where(row == 7, square, -2.0 * place))
            a1 = rounded(alpha)
            a2 = rounded(alpha - a1)
            a3 = alpha - a1 - a2
            parts = [a1, a1, a2, a2, a1, a3, blank]
            left_ref[pl.ds((block * (span // LANES) + at) * LANES, LANES), :] = (
                jnp.concatenate(parts + parts, axis=0).T.astype(jnp.bfloat16)
            )

    def fill(source, target):
        blocks, _, span = source.shape
        per = span // LANES
        zero = jnp.zeros((64, LANES), jnp.bfloat16)
        pad = jnp.zeros((16, LANES), jnp.bfloat16)
        for block in range(blocks):
            for at in range(per):
                right = jnp.concatenate([right_factor(source[block, :, pl.ds(at * LANES, LANES)]), pad], axis=0)
                target[block * per + at] = jnp.concatenate(
                    [jnp.concatenate([right, zero], axis=0), jnp.concatenate([zero, right], axis=0)], axis=1
                )

    fill(col_ref, col_out)
    fill(node_ref, node_out)


def factors(row_points, col_points, node_points):
    def tiles(points):
        return points.shape[0] * points.shape[2] // LANES

    def shape(points):
        return jax.ShapeDtypeStruct((tiles(points), LANES, 2 * LANES), jnp.bfloat16)

    return pl.pallas_call(
        factor_body,
        out_shape=[
            jax.ShapeDtypeStruct((tiles(row_points) * LANES, LANES), jnp.bfloat16),
            shape(col_points),
            shape(node_points),
        ],
        in_specs=[pl.BlockSpec(memory_space=pltpu.VMEM)] * 3,
        out_specs=[pl.BlockSpec(memory_space=pltpu.VMEM)] * 3,
        compiler_params=pltpu.CompilerParams(vmem_limit_bytes=VMEM),
    )(row_points, col_points, node_points)


def node_rows_body(slab_ref, perm_ref, xyz_ref, cot_ref, xyz_out, cot_out, rows_a, rows_b, rows_c):
    count = cot_ref.shape[1]
    width = cot_ref.shape[0]
    blank = jnp.zeros((PAD - width, LANES), jnp.float32)
    for tile in range(count // LANES):
        here = pl.ds(tile * LANES, LANES)
        rows_a[here, :PAD] = jnp.concatenate([cot_ref[:, here], blank], axis=0).T

    def scatter(index, _):
        base = pl.multiple_of(index * 64, 64)
        for i in range(64):
            rows_b[pl.ds(slab_ref[base + i], 1), :] = rows_a[pl.ds(base + i, 1), :]
        return 0

    lax.fori_loop(0, count // 64, scatter, 0)
    for tile in range(count // LANES):
        here = pl.ds(tile * LANES, LANES)
        rows_b[here, PAD : PAD + 8] = xyz_ref[:, here].T

    def gather(index, _):
        base = pl.multiple_of(index * 64, 64)
        for i in range(64):
            rows_c[pl.ds(base + i, 1), :] = rows_b[pl.ds(perm_ref[base + i], 1), :]
        return 0

    lax.fori_loop(0, count // 64, gather, 0)
    for tile in range(count // LANES):
        here = rows_c[pl.ds(tile * LANES, LANES), :].T
        cot_out[0, :, tile, :] = here[:width]
        xyz_out[0, :, pl.ds(tile * LANES, LANES)] = here[PAD : PAD + 8]


def node_rows(slab, perm, xyz, cotangent):
    count = cotangent.shape[1]
    width = cotangent.shape[0]
    tiles = count // LANES
    return pl.pallas_call(
        node_rows_body,
        out_shape=[
            jax.ShapeDtypeStruct((1, 8, count), jnp.float32),
            jax.ShapeDtypeStruct((1, width, tiles, LANES), jnp.float32),
        ],
        in_specs=[pl.BlockSpec(memory_space=pltpu.SMEM)] * 2 + [pl.BlockSpec(memory_space=pltpu.VMEM)] * 2,
        out_specs=[pl.BlockSpec(memory_space=pltpu.VMEM)] * 2,
        scratch_shapes=[pltpu.VMEM((count, LANES), jnp.float32)] * 3,
        compiler_params=pltpu.CompilerParams(vmem_limit_bytes=VMEM),
    )(slab, perm, xyz, cotangent)


def pick_body(slot_ref, table_ref, out_ref, rows_a, rows_b):
    blocks, width, deep, _ = table_ref.shape
    count = out_ref.shape[1]
    for block in range(blocks):
        for tile in range(deep):
            rows_a[pl.ds((block * deep + tile) * LANES, LANES), :width] = table_ref[block, :, tile, :].T

    def gather(index, _):
        base = pl.multiple_of(index * 64, 64)
        for i in range(64):
            rows_b[pl.ds(base + i, 1), :] = rows_a[pl.ds(slot_ref[base + i], 1), :]
        return 0

    lax.fori_loop(0, count // 64, gather, 0)
    for tile in range(count // LANES):
        here = pl.ds(tile * LANES, LANES)
        out_ref[:, here] = rows_b[here, :].T[:width]


def pick(slots, table):
    blocks, width, deep, _ = table.shape
    count = slots.shape[0]
    return pl.pallas_call(
        pick_body,
        out_shape=jax.ShapeDtypeStruct((width, count), jnp.float32),
        in_specs=[pl.BlockSpec(memory_space=pltpu.SMEM), pl.BlockSpec(memory_space=pltpu.VMEM)],
        out_specs=pl.BlockSpec(memory_space=pltpu.VMEM),
        scratch_shapes=[
            pltpu.VMEM((blocks * deep * LANES, LANES), jnp.float32),
            pltpu.VMEM((count, LANES), jnp.float32),
        ],
        compiler_params=pltpu.CompilerParams(vmem_limit_bytes=VMEM),
    )(slots, table)


class Links:
    def __init__(self, nodes, ctrs):
        self.nodes, self.ctrs = nodes, ctrs
        self.node, self.ctr = lax.axis_index("node"), lax.axis_index("ctr")
        self.me = self.node * ctrs + self.ctr

    def on_node(self, hop):
        return (lax.rem(self.node + hop, self.nodes), self.ctr)

    def on_ctr(self, hop):
        return (self.node, lax.rem(self.ctr + hop, self.ctrs))

    def anyone(self, hop):
        other = lax.rem(self.me + hop, self.nodes * self.ctrs)
        return (other // self.ctrs, lax.rem(other, self.ctrs))

    def meet(self, targets):
        barrier = pltpu.get_barrier_semaphore()
        for target in targets:
            pl.semaphore_signal(barrier, inc=1, device_id=target, device_id_type=MESH)
        pl.semaphore_wait(barrier, len(targets))

    def node_hops(self):
        return range(1, self.nodes)

    def ctr_hops(self):
        return range(1, self.ctrs)

    def meet_sides(self):
        self.meet([self.on_node(h) for h in self.node_hops()] + [self.on_ctr(h) for h in self.ctr_hops()])

    def meet_all(self):
        self.meet([self.anyone(h) for h in range(1, self.nodes * self.ctrs)])


def send(source, target, sems, index, device):
    copy = pltpu.make_async_remote_copy(
        src_ref=source,
        dst_ref=target,
        send_sem=sems[0].at[index],
        recv_sem=sems[1].at[index],
        device_id=device,
        device_id_type=MESH,
    )
    copy.start()
    return copy


def finish(copies):
    for copy in copies:
        copy.wait()


def comm_call(body, nodes, ctrs, out_shape, scratch, collective, *args):
    return pl.pallas_call(
        functools.partial(body, nodes, ctrs),
        out_shape=out_shape,
        in_specs=[pl.BlockSpec(memory_space=pltpu.VMEM)] * len(args),
        out_specs=jax.tree.map(lambda _: pl.BlockSpec(memory_space=pltpu.VMEM), out_shape),
        scratch_shapes=scratch,
        compiler_params=pltpu.CompilerParams(
            collective_id=collective, has_side_effects=True, vmem_limit_bytes=VMEM
        ),
    )(*args)


def dma_pair(count):
    return [pltpu.SemaphoreType.DMA((count,))] * 2


def surface_body(nodes, ctrs, own_ref, all_ref, *sems):
    links = Links(nodes, ctrs)
    links.meet_sides()
    mine = all_ref.at[links.ctr, links.node]
    copies = [send(own_ref, mine, sems, h - 1, links.on_node(h)) for h in links.node_hops()]
    all_ref[links.ctr, links.node] = own_ref[...]
    finish(copies)
    whole = all_ref.at[links.ctr]
    last = nodes - 1
    if ctrs != 4:
        finish([send(whole, whole, sems, last - 1 + h, links.on_ctr(h)) for h in links.ctr_hops()])
        return
    far = lax.rem(links.ctr + 2, 4)
    near = (links.node, links.ctr + 1 - 2 * lax.rem(links.ctr, 2))
    across = send(whole, whole, sems, last, (links.node, far))
    beside = send(whole, whole, sems, last + 1, near)
    across.wait()
    other = all_ref.at[far]
    finish([send(other, other, sems, last + 2, near), beside])


def node_body(nodes, ctrs, own_ref, all_ref, *sems):
    links = Links(nodes, ctrs)
    links.meet([links.on_node(h) for h in links.node_hops()])
    mine = all_ref.at[links.node]
    copies = [send(own_ref, mine, sems, h - 1, links.on_node(h)) for h in links.node_hops()]
    all_ref[links.node] = own_ref[...]
    finish(copies)


def cross_body(nodes, ctrs, own_ref, node_ref, ctr_ref, *sems):
    links = Links(nodes, ctrs)
    links.meet_sides()
    copies = [send(own_ref, node_ref.at[links.node], sems, h - 1, links.on_node(h)) for h in links.node_hops()]
    copies += [
        send(own_ref, ctr_ref.at[links.ctr], sems, nodes - 2 + h, links.on_ctr(h)) for h in links.ctr_hops()
    ]
    node_ref[links.node] = own_ref[...]
    ctr_ref[links.ctr] = own_ref[...]
    finish(copies)


def reduced(links, part_ref, landing, sems):
    copies = []
    for h in links.node_hops():
        device = links.on_node(h)
        copies.append(send(part_ref.at[device[0]], landing.at[h - 1], sems, h - 1, device))
    total = part_ref[links.node]
    for h, copy in zip(links.node_hops(), copies):
        copy.wait()
        total = total + landing[h - 1]
    return total


def wanted(rows, index):
    row = lax.broadcasted_iota(jnp.int32, (rows, LANES), 0)
    lane = lax.broadcasted_iota(jnp.int32, (rows, LANES), 1)
    return lane == row + 32 * index


def share_start(links, values, own, everyone, sems):
    line = 0.0
    for index, value in enumerate(values):
        column = jnp.sum(jnp.sum(value, axis=1), axis=1, keepdims=True)
        line += jnp.sum(
            jnp.where(wanted(column.shape[0], index), column, 0.0), axis=0, keepdims=True
        )
    own[...] = line
    hops = range(1, links.nodes * links.ctrs)
    copies = [send(own, everyone.at[links.me], sems, h - 1, links.anyone(h)) for h in hops]
    everyone[links.me] = own[...]
    return copies


def share_end(copies, count, rows, everyone):
    finish(copies)
    line = jnp.sum(everyone[...], axis=0)
    return [
        jnp.sum(jnp.where(wanted(rows, index), line, 0.0), axis=1, keepdims=True) for index in range(count)
    ]


def spread(column, ref):
    ref[...] = jnp.broadcast_to(column, ref.shape)
    return [ref[v : v + 1, :] for v in range(ref.shape[0])]


def pulled_body(nodes, ctrs, part_ref, own_ref, cols_ref, landing, s0, s1, t0, t1):
    links = Links(nodes, ctrs)
    links.meet_sides()
    own_ref[...] = reduced(links, part_ref, landing, (s0, s1))
    copies = [
        send(own_ref, cols_ref.at[links.ctr], (t0, t1), h - 1, links.on_ctr(h)) for h in links.ctr_hops()
    ]
    cols_ref[links.ctr] = own_ref[...]
    finish(copies)


def first_body(
    nodes, ctrs, part_ref, pulled_ref, pulled_cols, resid_ref, dir_cols, scal_ref,
    landing, image_ref, cols, line, every, scr0, scr1, s0, s1, t0, t1, u0, u1,
):
    links = Links(nodes, ctrs)
    links.meet_all()
    image = reduced(links, part_ref, landing, (s0, s1))
    image_ref[...] = image
    pulled = pulled_ref[...]
    told = share_start(
        links, [pulled * pulled, pulled * image, image * image], line, every, (t0, t1)
    )
    copies = [
        send(image_ref, cols.at[links.ctr], (u0, u1), h - 1, links.on_ctr(h)) for h in links.ctr_hops()
    ]
    cols[links.ctr] = image
    width = pulled_ref.shape[0]
    norm, curve, square = share_end(told, 3, width, every)
    alpha = norm / curve
    ratio = alpha * square / curve - 1.0
    alphas, ratios = spread(alpha, scr0), spread(ratio, scr1)
    scal_ref[0] = scr0[...]
    scal_ref[1] = scr1[...]
    for v in range(width):
        resid_ref[v] = pulled_ref[v] - alphas[v] * image_ref[v]
    finish(copies)
    for c in range(ctrs):
        for v in range(width):
            dir_cols[c, v] = (pulled_cols[c, v] - alphas[v] * cols[c, v]) + ratios[v] * pulled_cols[c, v]


def second_body(
    nodes, ctrs, part_ref, pulled_ref, resid_ref, scal_ref, out_ref,
    landing, final, line, every, scr0, s0, s1, t0, t1, u0, u1,
):
    links = Links(nodes, ctrs)
    links.meet_all()
    image = reduced(links, part_ref, landing, (s0, s1))
    width = pulled_ref.shape[0]
    alphas = [scal_ref[0, v : v + 1, :] for v in range(width)]
    ratios = [scal_ref[1, v : v + 1, :] for v in range(width)]
    for v in range(width):
        final[v] = resid_ref[v] + ratios[v] * pulled_ref[v]
    resid = resid_ref[...]
    told = share_start(links, [resid * resid, final[:width] * image], line, every, (t0, t1))
    final[width:] = image
    norm, curve = share_end(told, 2, width, every)
    seconds = spread(norm / curve, scr0)
    for v in range(width):
        final[v] = alphas[v] * pulled_ref[v] + seconds[v] * final[v]
        final[width + v] = resid_ref[v] - seconds[v] * final[width + v]
    copies = [
        send(final, out_ref.at[links.node], (u0, u1), h - 1, links.on_node(h)) for h in links.node_hops()
    ]
    out_ref[links.node] = final[...]
    finish(copies)


def local(nodes, ctrs, surface_xyz, centre_idx, volume_xyz, slab_ids, cotangent):
    width = cotangent.shape[0]
    owned = centre_idx.shape[0]
    total = owned * nodes
    here = lax.axis_index("node")
    f32 = jnp.float32
    vmem = lambda *shape: pltpu.VMEM(shape, f32)
    out = lambda *shape: jax.ShapeDtypeStruct(shape, f32)
    devices = nodes * ctrs

    slab = slab_ids % volume_xyz.shape[1]
    node_perm = lax.sort(sort_key(volume_xyz)) % volume_xyz.shape[1]
    volume_points = jnp.concatenate(
        [scaled(volume_xyz), jnp.zeros((4, volume_xyz.shape[1]), f32)], axis=0
    )
    volume_points = jnp.concatenate([volume_points[4:], volume_points[:4]], axis=0)
    node_points, node_vec = node_rows(slab, node_perm, volume_points, cotangent)

    rows = surface_xyz.shape[1] // LANES
    surface = comm_call(
        surface_body, nodes, ctrs, out(ctrs, nodes, 3, rows, LANES), dma_pair(nodes + ctrs - 2), 0,
        surface_xyz.reshape(3, rows, LANES),
    )
    surface = surface.transpose(2, 1, 0, 3, 4).reshape(3, -1)
    mine = lookup(surface, centre_idx)

    plane = comm_call(
        node_body, nodes, ctrs, out(nodes, 8, owned), dma_pair(nodes - 1), 1,
        jnp.pad(mine, ((0, 5), (0, 0))),
    )[:, :3]
    plane = plane.transpose(1, 0, 2).reshape(3, total)
    perm = lax.sort(sort_key(plane)) % total
    by_owner = perm.reshape(owned // LANES, nodes, LANES)
    own_perm = lax.dynamic_index_in_dim(by_owner, here, 1, False).reshape(owned)
    sorted_mine = scaled(lookup(plane, own_perm))
    sorted_mine = jnp.concatenate([jnp.zeros_like(sorted_mine), sorted_mine], axis=0)
    row_points, col_points = comm_call(
        cross_body, nodes, ctrs, (out(nodes, 8, owned), out(ctrs, 8, owned)), dma_pair(nodes + ctrs - 2), 2,
        sorted_mine,
    )
    left, col_right, node_right = factors(row_points, col_points, node_points)
    tiles = owned // LANES
    flat = lambda value: value.transpose(1, 0, 2).reshape(8, -1)[4:]
    groups = boxes(flat(row_points), GROUP)
    node_lists = near_lists(boxes(flat(node_points), LANES // 2), groups, 2)
    col_lists = near_lists(boxes(flat(col_points), LANES), groups, 1)

    places = jnp.arange(total, dtype=jnp.int32)
    hit = (by_owner.transpose(1, 0, 2).reshape(total) // LANES)[None, :] == (
        here * tiles + jnp.arange(tiles, dtype=jnp.int32)
    )[:, None]
    spots = jnp.concatenate(
        [jnp.where(hit, (places // LANES)[None, :], 0), jnp.where(hit, (places % LANES)[None, :], 0)], axis=0
    ).astype(jnp.bfloat16)
    lane = (
        by_owner.transpose(1, 0, 2).reshape(total)[:, None] % LANES == jnp.arange(LANES, dtype=jnp.int32)[None, :]
    ).astype(jnp.bfloat16)
    spots = jnp.dot(spots, lane, preferred_element_type=f32).astype(jnp.int32)
    slots = (spots[:tiles] * LANES + spots[tiles:]).reshape(owned)

    own_shape, scr = out(width, tiles, LANES), vmem(width, LANES)
    cols_shape = out(ctrs, width, tiles, LANES)
    landing = vmem(nodes - 1, width, tiles, LANES)
    line, every = vmem(1, LANES), vmem(devices, 1, LANES)
    part = apply_kernel(node_lists, left, node_right, node_vec, nodes)
    pulled, pulled_cols = comm_call(
        pulled_body, nodes, ctrs, (own_shape, cols_shape),
        [landing] + dma_pair(nodes - 1) + dma_pair(ctrs - 1), 3, part,
    )
    part = apply_kernel(col_lists, left, col_right, pulled_cols, nodes)
    resid, dir_cols, scal = comm_call(
        first_body, nodes, ctrs, (own_shape, cols_shape, out(2, width, LANES)),
        [landing, vmem(width, tiles, LANES), vmem(ctrs, width, tiles, LANES), line, every, scr, scr]
        + dma_pair(nodes - 1) + dma_pair(devices - 1) + dma_pair(ctrs - 1),
        4, part, pulled, pulled_cols,
    )
    part = apply_kernel(col_lists, left, col_right, dir_cols, nodes)
    final = comm_call(
        second_body, nodes, ctrs, out(nodes, 2 * width, tiles, LANES),
        [landing, vmem(2 * width, tiles, LANES), line, every, scr]
        + dma_pair(nodes - 1) + dma_pair(devices - 1) + dma_pair(nodes - 1),
        5, part, pulled, resid, scal,
    )
    final = pick(slots, final)
    return final[:width], final[width:]


def solution(mesh):
    return jax.shard_map(
        functools.partial(local, mesh.shape["node"], mesh.shape["ctr"]),
        mesh=mesh,
        in_specs=(
            P(None, ("node", "ctr")),
            P(("node", "ctr")),
            P(None, "node"),
            P("node"),
            P(None, "node"),
        ),
        out_specs=(P(None, ("node", "ctr")), P(None, ("node", "ctr"))),
        check_vma=False,
    )
```

```python
import functools
import math

import jax
import jax.numpy as jnp
from jax import lax
from jax.experimental import pallas as pl
from jax.experimental.pallas import tpu as pltpu
from jax.sharding import PartitionSpec as P

RADIUS = 0.2
LANES = 128
GROUP = 32
BATCH = 4
PAIR = 4
CELLS = 5
DEPTH = 64
PAD = 16
VMEM = 50 * 1024 * 1024
NT = (((1,), (1,)), ((), ()))
MESH = pl.DeviceIdType.MESH


def scaled(xyz):
    point = (xyz - 0.5) * (1.0 / RADIUS)
    return jnp.concatenate([point, jnp.ones((1, xyz.shape[1]), jnp.float32)], axis=0)


def rounded(value):
    return value.astype(jnp.bfloat16).astype(jnp.float32)


def right_factor(group):
    row = lax.broadcasted_iota(jnp.int32, group.shape, 0)
    place = jnp.where(row >= 4, group, 0.0)
    square = jnp.sum(jnp.where(row < 7, place * place, 0.0), axis=0, keepdims=True)
    beta = jnp.where(row == 0, square, place)
    b1 = rounded(beta)
    rest = beta - b1
    b2 = rounded(rest)
    b3 = rest - b2
    return jnp.concatenate([b1, b2, b1, b2, b3, b1], axis=0).astype(jnp.bfloat16)


def two_parts(vectors):
    v1 = rounded(vectors)
    return jnp.concatenate([v1, vectors - v1], axis=0).astype(jnp.bfloat16)


def boxes(points, size):
    tiles = points[:3].reshape(3, -1, size)
    return jnp.min(tiles, axis=2), jnp.max(tiles, axis=2)


def near_lists(tiles, groups, pieces):
    gap = jnp.maximum(
        jnp.maximum(tiles[0][:, :, None] - groups[1][:, None, :], groups[0][:, None, :] - tiles[1][:, :, None]),
        0.0,
    )
    near = jnp.sum(gap * gap, axis=0) < 1.0 + 1e-4
    size = near.shape[1]
    near = jnp.any(near.reshape(-1, pieces, size), axis=1)
    total = near.shape[0]
    count = jnp.sum(near.astype(jnp.int32), axis=1)
    upto = (jnp.arange(size)[:, None] <= jnp.arange(size)[None, :]).astype(jnp.bfloat16)
    seen = jnp.dot(near.astype(jnp.bfloat16), upto, preferred_element_type=jnp.float32).astype(jnp.int32)
    every = jnp.arange(size, dtype=jnp.int32)
    place = jnp.where(near, seen - 1, count[:, None] + every[None, :] - seen)
    order = jnp.sum(
        jnp.where(place[:, :, None] == every[None, None, :], every[None, :, None], 0), axis=1
    )
    batches = (count + BATCH - 1) // BATCH
    ranks = jnp.arange(total)
    ends = jnp.sum(jnp.where(ranks[:, None] <= ranks[None, :], batches[:, None], 0), axis=0)
    at = jnp.arange(total * size // BATCH + 8 * PAIR, dtype=jnp.int32) - 2 * PAIR
    passed = ends[:, None] <= at[None, :]
    tile = jnp.sum(passed.astype(jnp.int32), axis=0)
    start = jnp.sum(jnp.where(passed, batches[:, None], 0), axis=0)
    code = tile * size + (at - start) * BATCH
    items = jnp.where((at < 0) | (tile == total), total * size, code)
    return ends[-1:], items, jnp.pad((order * GROUP).reshape(-1), (0, size))


def apply_body(count, items, order, left_ref, right_ref, vec_ref, out_ref, acc, vec, q0, q1, k0, k1):
    rows = left_ref.shape[0]
    tiles = right_ref.shape[0]
    span = GROUP * BATCH
    half = span // 2
    banks, width, deep = vec_ref.shape[:3]
    acc[...] = jnp.zeros_like(acc)
    for ref in (q0, q1, k0, k1):
        ref[...] = jnp.zeros_like(ref)

    blank = jnp.zeros((PAD - width, LANES), jnp.float32)
    for bank in range(banks):
        for at in range(deep):
            parts = two_parts(jnp.concatenate([vec_ref[bank, :, at, :], blank], axis=0))
            vec[bank * deep + at] = jnp.concatenate([parts, parts], axis=1)
    vec[tiles] = jnp.zeros_like(vec[tiles])

    groups = rows // GROUP
    first_half = lax.broadcasted_iota(jnp.int32, (half, LANES), 1) < LANES // 2

    def item(index):
        code = items[index]
        tile = lax.div(code, groups)
        return tile, jnp.minimum(tile, tiles - 1), [
            pl.multiple_of(order[code + i], GROUP) for i in range(BATCH)
        ]

    def rows_at(places):
        return jnp.concatenate([left_ref[pl.ds(place, GROUP), :] for place in places], axis=0)

    def step(index, q_in, q_out, k_in, k_out):
        for unit in range(PAIR):
            tile, _, places = item(index * PAIR + unit)
            part = lax.dot_general(
                k_in[pl.ds(unit * span, span), :], vec[tile], NT, preferred_element_type=jnp.float32
            )
            for j, place in enumerate(places):
                acc[pl.ds(place, GROUP), :] += part[j * GROUP : (j + 1) * GROUP]
        for unit in range(PAIR):
            q = jnp.minimum(jnp.maximum(q_in[pl.ds(unit * half, half), :], 1e-30), 1.0)
            s = q * lax.rsqrt(q)
            w = 1.0 - s
            w2 = w * w
            k = (w2 * w2) * (0.25 + s)
            hi = k.astype(jnp.bfloat16)
            lo = (k - hi.astype(jnp.float32)).astype(jnp.bfloat16)
            for side in range(2):
                here = pl.ds(unit * span + side * half, half)
                lanes = slice(side * LANES, (side + 1) * LANES)
                k_out[here, :LANES] = hi[:, lanes]
                k_out[here, LANES:] = lo[:, lanes]
        for unit in range(PAIR):
            _, listed, places = item((index + 2) * PAIR + unit)
            left = jnp.where(first_half, rows_at(places[: BATCH // 2]), rows_at(places[BATCH // 2 :]))
            q_out[pl.ds(unit * half, half), :] = jnp.dot(
                left, right_ref[listed], preferred_element_type=jnp.float32
            )

    def two_steps(index, _):
        step(2 * index, q0, q1, k0, k1)
        step(2 * index + 1, q1, q0, k1, k0)
        return 0

    steps = (count[0] + PAIR - 1) // PAIR + 2
    lax.fori_loop(0, (steps + 1) // 2, two_steps, 0)

    owners, _, high, _ = out_ref.shape
    for owner in range(owners):
        for at in range(high):
            total = acc[pl.ds((owner * high + at) * LANES, LANES), :].T
            out_ref[owner, :, at, :] = 4.0 * (total[:width] + total[PAD : PAD + width])


def apply_kernel(lists, left, right, vec, owners):
    rows = left.shape[0]
    tiles = right.shape[0]
    width = vec.shape[1]
    wide = PAIR * GROUP * BATCH
    return pl.pallas_call(
        apply_body,
        out_shape=jax.ShapeDtypeStruct((owners, width, rows // owners // LANES, LANES), jnp.float32),
        in_specs=[pl.BlockSpec(memory_space=pltpu.SMEM)] * 3 + [pl.BlockSpec(memory_space=pltpu.VMEM)] * 3,
        out_specs=pl.BlockSpec(memory_space=pltpu.VMEM),
        scratch_shapes=[
            pltpu.VMEM((rows, 2 * PAD), jnp.float32),
            pltpu.VMEM((tiles + 1, 2 * PAD, 2 * LANES), jnp.bfloat16),
            pltpu.VMEM((wide // 2, 2 * LANES), jnp.float32),
            pltpu.VMEM((wide // 2, 2 * LANES), jnp.float32),
            pltpu.VMEM((wide, 2 * LANES), jnp.bfloat16),
            pltpu.VMEM((wide, 2 * LANES), jnp.bfloat16),
        ],
        compiler_params=pltpu.CompilerParams(vmem_limit_bytes=VMEM),
    )(*lists, left, right, vec)


def factor_body(row_ref, col_ref, node_ref, left_ref, col_out, node_out):
    blocks, _, span = row_ref.shape
    blank = jnp.zeros((16, LANES), jnp.float32)
    for block in range(blocks):
        for at in range(span // LANES):
            group = row_ref[block, :, pl.ds(at * LANES, LANES)]
            row = lax.broadcasted_iota(jnp.int32, group.shape, 0)
            place = jnp.where((row >= 4) & (row < 7), group, 0.0)
            square = jnp.sum(place * place, axis=0, keepdims=True)
            alpha = jnp.where(row == 0, 1.0, jnp.where(row == 7, square, -2.0 * place))
            a1 = rounded(alpha)
            a2 = rounded(alpha - a1)
            a3 = alpha - a1 - a2
            parts = [a1, a1, a2, a2, a1, a3, blank]
            left_ref[pl.ds((block * (span // LANES) + at) * LANES, LANES), :] = (
                jnp.concatenate(parts + parts, axis=0).T.astype(jnp.bfloat16)
            )

    def fill(source, target):
        blocks, _, span = source.shape
        per = span // LANES
        zero = jnp.zeros((64, LANES), jnp.bfloat16)
        pad = jnp.zeros((16, LANES), jnp.bfloat16)
        for block in range(blocks):
            for at in range(per):
                right = jnp.concatenate([right_factor(source[block, :, pl.ds(at * LANES, LANES)]), pad], axis=0)
                target[block * per + at] = jnp.concatenate(
                    [jnp.concatenate([right, zero], axis=0), jnp.concatenate([zero, right], axis=0)], axis=1
                )

    fill(col_ref, col_out)
    fill(node_ref, node_out)


def factors(row_points, col_points, node_points):
    def tiles(points):
        return points.shape[0] * points.shape[2] // LANES

    def shape(points):
        return jax.ShapeDtypeStruct((tiles(points), LANES, 2 * LANES), jnp.bfloat16)

    return pl.pallas_call(
        factor_body,
        out_shape=[
            jax.ShapeDtypeStruct((tiles(row_points) * LANES, LANES), jnp.bfloat16),
            shape(col_points),
            shape(node_points),
        ],
        in_specs=[pl.BlockSpec(memory_space=pltpu.VMEM)] * 3,
        out_specs=[pl.BlockSpec(memory_space=pltpu.VMEM)] * 3,
        compiler_params=pltpu.CompilerParams(vmem_limit_bytes=VMEM),
    )(row_points, col_points, node_points)


def node_rows_body(slab_ref, perm_ref, xyz_ref, cot_ref, xyz_out, cot_out, rows_a, rows_b, rows_c):
    count = cot_ref.shape[1]
    width = cot_ref.shape[0]
    blank = jnp.zeros((PAD - width, LANES), jnp.float32)
    for tile in range(count // LANES):
        here = pl.ds(tile * LANES, LANES)
        rows_a[here, :PAD] = jnp.concatenate([cot_ref[:, here], blank], axis=0).T

    def scatter(index, _):
        base = pl.multiple_of(index * 64, 64)
        for i in range(64):
            rows_b[pl.ds(slab_ref[base + i], 1), :] = rows_a[pl.ds(base + i, 1), :]
        return 0

    lax.fori_loop(0, count // 64, scatter, 0)
    for tile in range(count // LANES):
        here = pl.ds(tile * LANES, LANES)
        rows_b[here, PAD : PAD + 8] = xyz_ref[:, here].T

    def gather(index, _):
        base = pl.multiple_of(index * 64, 64)
        for i in range(64):
            rows_c[pl.ds(base + i, 1), :] = rows_b[pl.ds(perm_ref[base + i], 1), :]
        return 0

    lax.fori_loop(0, count // 64, gather, 0)
    for tile in range(count // LANES):
        here = rows_c[pl.ds(tile * LANES, LANES), :].T
        cot_out[0, :, tile, :] = here[:width]
        xyz_out[0, :, pl.ds(tile * LANES, LANES)] = here[PAD : PAD + 8]


def node_rows(slab, perm, xyz, cotangent):
    count = cotangent.shape[1]
    width = cotangent.shape[0]
    tiles = count // LANES
    return pl.pallas_call(
        node_rows_body,
        out_shape=[
            jax.ShapeDtypeStruct((1, 8, count), jnp.float32),
            jax.ShapeDtypeStruct((1, width, tiles, LANES), jnp.float32),
        ],
        in_specs=[pl.BlockSpec(memory_space=pltpu.SMEM)] * 2 + [pl.BlockSpec(memory_space=pltpu.VMEM)] * 2,
        out_specs=[pl.BlockSpec(memory_space=pltpu.VMEM)] * 2,
        scratch_shapes=[pltpu.VMEM((count, LANES), jnp.float32)] * 3,
        compiler_params=pltpu.CompilerParams(vmem_limit_bytes=VMEM),
    )(slab, perm, xyz, cotangent)


def pick_body(slot_ref, table_ref, out_ref, rows_a, rows_b):
    blocks, width, deep, _ = table_ref.shape
    count = out_ref.shape[1]
    for block in range(blocks):
        for tile in range(deep):
            rows_a[pl.ds((block * deep + tile) * LANES, LANES), :width] = table_ref[block, :, tile, :].T

    def gather(index, _):
        base = pl.multiple_of(index * 64, 64)
        for i in range(64):
            rows_b[pl.ds(base + i, 1), :] = rows_a[pl.ds(slot_ref[base + i], 1), :]
        return 0

    lax.fori_loop(0, count // 64, gather, 0)
    for tile in range(count // LANES):
        here = pl.ds(tile * LANES, LANES)
        out_ref[:, here] = rows_b[here, :].T[:width]


def pick(slots, table):
    blocks, width, deep, _ = table.shape
    count = slots.shape[0]
    return pl.pallas_call(
        pick_body,
        out_shape=jax.ShapeDtypeStruct((width, count), jnp.float32),
        in_specs=[pl.BlockSpec(memory_space=pltpu.SMEM), pl.BlockSpec(memory_space=pltpu.VMEM)],
        out_specs=pl.BlockSpec(memory_space=pltpu.VMEM),
        scratch_shapes=[
            pltpu.VMEM((blocks * deep * LANES, LANES), jnp.float32),
            pltpu.VMEM((count, LANES), jnp.float32),
        ],
        compiler_params=pltpu.CompilerParams(vmem_limit_bytes=VMEM),
    )(slots, table)


class Links:
    def __init__(self, nodes, ctrs):
        self.nodes, self.ctrs = nodes, ctrs
        self.node, self.ctr = lax.axis_index("node"), lax.axis_index("ctr")
        self.me = self.node * ctrs + self.ctr

    def on_node(self, hop):
        return (lax.rem(self.node + hop, self.nodes), self.ctr)

    def on_ctr(self, hop):
        return (self.node, lax.rem(self.ctr + hop, self.ctrs))

    def anyone(self, hop):
        other = lax.rem(self.me + hop, self.nodes * self.ctrs)
        return (other // self.ctrs, lax.rem(other, self.ctrs))

    def meet(self, targets):
        barrier = pltpu.get_barrier_semaphore()
        for target in targets:
            pl.semaphore_signal(barrier, inc=1, device_id=target, device_id_type=MESH)
        pl.semaphore_wait(barrier, len(targets))

    def node_hops(self):
        return range(1, self.nodes)

    def ctr_hops(self):
        return range(1, self.ctrs)

    def meet_sides(self):
        self.meet([self.on_node(h) for h in self.node_hops()] + [self.on_ctr(h) for h in self.ctr_hops()])

    def meet_all(self):
        self.meet([self.anyone(h) for h in range(1, self.nodes * self.ctrs)])


def send(source, target, sems, index, device):
    copy = pltpu.make_async_remote_copy(
        src_ref=source,
        dst_ref=target,
        send_sem=sems[0].at[index],
        recv_sem=sems[1].at[index],
        device_id=device,
        device_id_type=MESH,
    )
    copy.start()
    return copy


def finish(copies):
    for copy in copies:
        copy.wait()


def comm_call(body, nodes, ctrs, out_shape, scratch, collective, *args):
    return pl.pallas_call(
        functools.partial(body, nodes, ctrs),
        out_shape=out_shape,
        in_specs=[pl.BlockSpec(memory_space=pltpu.VMEM)] * len(args),
        out_specs=jax.tree.map(lambda _: pl.BlockSpec(memory_space=pltpu.VMEM), out_shape),
        scratch_shapes=scratch,
        compiler_params=pltpu.CompilerParams(
            collective_id=collective, has_side_effects=True, vmem_limit_bytes=VMEM
        ),
    )(*args)


def dma_pair(count):
    return [pltpu.SemaphoreType.DMA((count,))] * 2


TN = (((0,), (0,)), ((), ()))


def picked(tables, rows, lanes):
    high = lax.broadcasted_iota(jnp.int32, (tables[0].shape[0], rows.shape[1]), 0) == rows
    high = jnp.where(high, 1.0, 0.0).astype(jnp.bfloat16)
    low = lax.broadcasted_iota(jnp.int32, (LANES, rows.shape[1]), 0) == lanes
    found = []
    for table in tables:
        a1 = rounded(table)
        a2 = rounded(table - a1)
        a3 = table - a1 - a2
        parts = jnp.concatenate([a1, a2, a3], axis=1).astype(jnp.bfloat16)
        both = lax.dot_general(parts, high, TN, preferred_element_type=jnp.float32)
        value = both[:LANES] + both[LANES : 2 * LANES] + both[2 * LANES :]
        found.append(jnp.sum(jnp.where(low, value, 0.0), axis=0, keepdims=True))
    return found


def cell_keys(x, y, z):
    rows = x.shape[0]
    count = rows * LANES
    across = jnp.minimum((x * CELLS).astype(jnp.int32), CELLS - 1)
    along = jnp.minimum((y * CELLS).astype(jnp.int32), CELLS - 1)
    deep = jnp.minimum((z * DEPTH).astype(jnp.int32), DEPTH - 1)
    column = across * CELLS + jnp.where(across % 2 == 1, CELLS - 1 - along, along)
    deep = jnp.where(column % 2 == 1, DEPTH - 1 - deep, deep)
    index = lax.broadcasted_iota(jnp.int32, x.shape, 0) * LANES + lax.broadcasted_iota(jnp.int32, x.shape, 1)
    return ((column * DEPTH + deep) * count + index).astype(jnp.float32)


def sorted_keys(keys):
    rows = keys.shape[0]
    row = lax.broadcasted_iota(jnp.int32, keys.shape, 0)
    lane = lax.broadcasted_iota(jnp.int32, keys.shape, 1)
    bits = (rows * LANES).bit_length() - 1

    def bit(at):
        return (lane // 2**at) % 2 == 0 if at < 7 else (row // 2 ** (at - 7)) % 2 == 0

    zeros = [bit(at) for at in range(bits)]
    for level in range(1, bits + 1):
        for at in range(level - 1, -1, -1):
            axis, size, shift = (1, LANES, 2**at) if at < 7 else (0, rows, 2 ** (at - 7))
            other = jnp.where(
                zeros[at], pltpu.roll(keys, size - shift, axis), pltpu.roll(keys, shift, axis)
            )
            small = zeros[at] if level == bits else zeros[at] == zeros[level]
            keys = jnp.where(small, jnp.minimum(keys, other), jnp.maximum(keys, other))
    return keys


def setup_body(
    nodes, ctrs, own_ref, ids_ref, volume_ref, perm_ref, node_ref, ctr_ref, slab_ref,
    all_ref, mine_ref, plane_ref, table_ref, point_ref, *sems,
):
    links = Links(nodes, ctrs)
    links.meet_sides()
    mine = all_ref.at[links.ctr, links.node]
    copies = [send(own_ref, mine, sems[:2], h - 1, links.on_node(h)) for h in links.node_hops()]
    all_ref[links.ctr, links.node] = own_ref[...]
    keys = sorted_keys(cell_keys(*(volume_ref[k] for k in range(3))))
    slab_ref[...] = keys.astype(jnp.int32) % (keys.shape[0] * LANES)
    finish(copies)
    whole = all_ref.at[links.ctr]
    last = nodes - 1
    if ctrs == 4:
        far = lax.rem(links.ctr + 2, 4)
        near = (links.node, links.ctr + 1 - 2 * lax.rem(links.ctr, 2))
        across = send(whole, whole, sems[:2], last, (links.node, far))
        beside = send(whole, whole, sems[:2], last + 1, near)
        across.wait()
        other = all_ref.at[far]
        finish([send(other, other, sems[:2], last + 2, near), beside])
    else:
        finish([send(whole, whole, sems[:2], last - 1 + h, links.on_ctr(h)) for h in links.ctr_hops()])

    rows, tiles = own_ref.shape[1], mine_ref.shape[1]
    tables = [all_ref[:, :, k].reshape(-1, LANES) for k in range(3)]
    for at in range(tiles):
        ids = ids_ref[at : at + 1, :]
        device = ids // (rows * LANES)
        place = (device % ctrs * nodes + device // ctrs) * rows + ids // LANES % rows
        for k, value in enumerate(picked(tables, place, ids % LANES)):
            mine_ref[k, at : at + 1, :] = value
    copies = [
        send(mine_ref, plane_ref.at[links.node], sems[2:4], h - 1, links.on_node(h)) for h in links.node_hops()
    ]
    plane_ref[links.node] = mine_ref[...]
    finish(copies)

    for node in range(nodes):
        for k in range(3):
            table_ref[k, node * tiles : (node + 1) * tiles, :] = plane_ref[node, k]
    tables = [table_ref[k] for k in range(3)]
    count = tables[0].shape[0] * LANES
    keys = sorted_keys(cell_keys(*tables))
    perm_ref[...] = keys.astype(jnp.int32) % count
    blank = jnp.zeros((4, LANES), jnp.float32)
    for at in range(tiles):
        ids = perm_ref[pl.ds(at * nodes + links.node, 1), :]
        found = [(v - 0.5) * (1.0 / RADIUS) for v in picked(tables, ids // LANES, ids % LANES)]
        point_ref[:, at * LANES : (at + 1) * LANES] = jnp.concatenate(
            [blank] + found + [jnp.ones((1, LANES), jnp.float32)], axis=0
        )
    copies = [send(point_ref, node_ref.at[links.node], sems[4:6], h - 1, links.on_node(h)) for h in links.node_hops()]
    copies += [
        send(point_ref, ctr_ref.at[links.ctr], sems[4:6], nodes - 2 + h, links.on_ctr(h)) for h in links.ctr_hops()
    ]
    node_ref[links.node] = point_ref[...]
    ctr_ref[links.ctr] = point_ref[...]
    finish(copies)


def reduced(links, part_ref, landing, sems):
    copies = []
    for h in links.node_hops():
        device = links.on_node(h)
        copies.append(send(part_ref.at[device[0]], landing.at[h - 1], sems, h - 1, device))
    total = part_ref[links.node]
    for h, copy in zip(links.node_hops(), copies):
        copy.wait()
        total = total + landing[h - 1]
    return total


def wanted(rows, index):
    row = lax.broadcasted_iota(jnp.int32, (rows, LANES), 0)
    lane = lax.broadcasted_iota(jnp.int32, (rows, LANES), 1)
    return lane == row + 32 * index


def share_start(links, values, own, everyone, sems):
    line = 0.0
    for index, value in enumerate(values):
        column = jnp.sum(jnp.sum(value, axis=1), axis=1, keepdims=True)
        line += jnp.sum(
            jnp.where(wanted(column.shape[0], index), column, 0.0), axis=0, keepdims=True
        )
    own[...] = line
    hops = range(1, links.nodes * links.ctrs)
    copies = [send(own, everyone.at[links.me], sems, h - 1, links.anyone(h)) for h in hops]
    everyone[links.me] = own[...]
    return copies


def share_end(copies, count, rows, everyone):
    finish(copies)
    line = jnp.sum(everyone[...], axis=0)
    return [
        jnp.sum(jnp.where(wanted(rows, index), line, 0.0), axis=1, keepdims=True) for index in range(count)
    ]


def spread(column, ref):
    ref[...] = jnp.broadcast_to(column, ref.shape)
    return [ref[v : v + 1, :] for v in range(ref.shape[0])]


def pulled_body(nodes, ctrs, part_ref, own_ref, cols_ref, landing, s0, s1, t0, t1):
    links = Links(nodes, ctrs)
    links.meet_sides()
    own_ref[...] = reduced(links, part_ref, landing, (s0, s1))
    copies = [
        send(own_ref, cols_ref.at[links.ctr], (t0, t1), h - 1, links.on_ctr(h)) for h in links.ctr_hops()
    ]
    cols_ref[links.ctr] = own_ref[...]
    finish(copies)


def first_body(
    nodes, ctrs, part_ref, pulled_ref, pulled_cols, resid_ref, dir_cols, scal_ref,
    landing, image_ref, cols, line, every, scr0, scr1, s0, s1, t0, t1, u0, u1,
):
    links = Links(nodes, ctrs)
    links.meet_all()
    image = reduced(links, part_ref, landing, (s0, s1))
    image_ref[...] = image
    pulled = pulled_ref[...]
    told = share_start(
        links, [pulled * pulled, pulled * image, image * image], line, every, (t0, t1)
    )
    copies = [
        send(image_ref, cols.at[links.ctr], (u0, u1), h - 1, links.on_ctr(h)) for h in links.ctr_hops()
    ]
    cols[links.ctr] = image
    width = pulled_ref.shape[0]
    norm, curve, square = share_end(told, 3, width, every)
    alpha = norm / curve
    ratio = alpha * square / curve - 1.0
    alphas, ratios = spread(alpha, scr0), spread(ratio, scr1)
    scal_ref[0] = scr0[...]
    scal_ref[1] = scr1[...]
    for v in range(width):
        resid_ref[v] = pulled_ref[v] - alphas[v] * image_ref[v]
    finish(copies)
    for c in range(ctrs):
        for v in range(width):
            dir_cols[c, v] = (pulled_cols[c, v] - alphas[v] * cols[c, v]) + ratios[v] * pulled_cols[c, v]


def second_body(
    nodes, ctrs, part_ref, pulled_ref, resid_ref, scal_ref, out_ref,
    landing, final, line, every, scr0, s0, s1, t0, t1, u0, u1,
):
    links = Links(nodes, ctrs)
    links.meet_all()
    image = reduced(links, part_ref, landing, (s0, s1))
    width = pulled_ref.shape[0]
    alphas = [scal_ref[0, v : v + 1, :] for v in range(width)]
    ratios = [scal_ref[1, v : v + 1, :] for v in range(width)]
    for v in range(width):
        final[v] = resid_ref[v] + ratios[v] * pulled_ref[v]
    resid = resid_ref[...]
    told = share_start(links, [resid * resid, final[:width] * image], line, every, (t0, t1))
    final[width:] = image
    norm, curve = share_end(told, 2, width, every)
    seconds = spread(norm / curve, scr0)
    for v in range(width):
        final[v] = alphas[v] * pulled_ref[v] + seconds[v] * final[v]
        final[width + v] = resid_ref[v] - seconds[v] * final[width + v]
    copies = [
        send(final, out_ref.at[links.node], (u0, u1), h - 1, links.on_node(h)) for h in links.node_hops()
    ]
    out_ref[links.node] = final[...]
    finish(copies)


def local(nodes, ctrs, surface_xyz, centre_idx, volume_xyz, slab_ids, cotangent):
    width = cotangent.shape[0]
    owned = centre_idx.shape[0]
    total = owned * nodes
    here = lax.axis_index("node")
    f32 = jnp.float32
    vmem = lambda *shape: pltpu.VMEM(shape, f32)
    out = lambda *shape: jax.ShapeDtypeStruct(shape, f32)
    devices = nodes * ctrs

    slab = slab_ids % volume_xyz.shape[1]
    volume_points = jnp.concatenate(
        [scaled(volume_xyz), jnp.zeros((4, volume_xyz.shape[1]), f32)], axis=0
    )
    volume_points = jnp.concatenate([volume_points[4:], volume_points[:4]], axis=0)

    rows = surface_xyz.shape[1] // LANES
    tiles = owned // LANES
    perm, row_points, col_points, node_perm = comm_call(
        setup_body, nodes, ctrs,
        (
            jax.ShapeDtypeStruct((total // LANES, LANES), jnp.int32), out(nodes, 8, owned), out(ctrs, 8, owned),
            jax.ShapeDtypeStruct((volume_xyz.shape[1] // LANES, LANES), jnp.int32),
        ),
        [
            vmem(ctrs, nodes, 3, rows, LANES), vmem(3, tiles, LANES), vmem(nodes, 3, tiles, LANES),
            vmem(3, total // LANES, LANES), vmem(8, owned),
        ] + dma_pair(nodes + ctrs - 2) + dma_pair(nodes - 1) + dma_pair(nodes + ctrs - 2),
        0, surface_xyz.reshape(3, rows, LANES), centre_idx.reshape(tiles, LANES),
        volume_xyz.reshape(3, -1, LANES),
    )
    by_owner = perm.reshape(tiles, nodes, LANES)
    node_points, node_vec = node_rows(slab, node_perm.reshape(-1), volume_points, cotangent)
    left, col_right, node_right = factors(row_points, col_points, node_points)
    flat = lambda value: value.transpose(1, 0, 2).reshape(8, -1)[4:]
    groups = boxes(flat(row_points), GROUP)
    node_lists = near_lists(boxes(flat(node_points), LANES // 2), groups, 2)
    col_lists = near_lists(boxes(flat(col_points), LANES), groups, 1)

    places = jnp.arange(total, dtype=jnp.int32)
    hit = (by_owner.transpose(1, 0, 2).reshape(total) // LANES)[None, :] == (
        here * tiles + jnp.arange(tiles, dtype=jnp.int32)
    )[:, None]
    spots = jnp.concatenate(
        [jnp.where(hit, (places // LANES)[None, :], 0), jnp.where(hit, (places % LANES)[None, :], 0)], axis=0
    ).astype(jnp.bfloat16)
    lane = (
        by_owner.transpose(1, 0, 2).reshape(total)[:, None] % LANES == jnp.arange(LANES, dtype=jnp.int32)[None, :]
    ).astype(jnp.bfloat16)
    spots = jnp.dot(spots, lane, preferred_element_type=f32).astype(jnp.int32)
    slots = (spots[:tiles] * LANES + spots[tiles:]).reshape(owned)

    own_shape, scr = out(width, tiles, LANES), vmem(width, LANES)
    cols_shape = out(ctrs, width, tiles, LANES)
    landing = vmem(nodes - 1, width, tiles, LANES)
    line, every = vmem(1, LANES), vmem(devices, 1, LANES)
    part = apply_kernel(node_lists, left, node_right, node_vec, nodes)
    pulled, pulled_cols = comm_call(
        pulled_body, nodes, ctrs, (own_shape, cols_shape),
        [landing] + dma_pair(nodes - 1) + dma_pair(ctrs - 1), 3, part,
    )
    part = apply_kernel(col_lists, left, col_right, pulled_cols, nodes)
    resid, dir_cols, scal = comm_call(
        first_body, nodes, ctrs, (own_shape, cols_shape, out(2, width, LANES)),
        [landing, vmem(width, tiles, LANES), vmem(ctrs, width, tiles, LANES), line, every, scr, scr]
        + dma_pair(nodes - 1) + dma_pair(devices - 1) + dma_pair(ctrs - 1),
        4, part, pulled, pulled_cols,
    )
    part = apply_kernel(col_lists, left, col_right, dir_cols, nodes)
    final = comm_call(
        second_body, nodes, ctrs, out(nodes, 2 * width, tiles, LANES),
        [landing, vmem(2 * width, tiles, LANES), line, every, scr]
        + dma_pair(nodes - 1) + dma_pair(devices - 1) + dma_pair(nodes - 1),
        5, part, pulled, resid, scal,
    )
    final = pick(slots, final)
    return final[:width], final[width:]


def solution(mesh):
    return jax.shard_map(
        functools.partial(local, mesh.shape["node"], mesh.shape["ctr"]),
        mesh=mesh,
        in_specs=(
            P(None, ("node", "ctr")),
            P(("node", "ctr")),
            P(None, "node"),
            P("node"),
            P(None, "node"),
        ),
        out_specs=(P(None, ("node", "ctr")), P(None, ("node", "ctr"))),
        check_vma=False,
    )
```

```python
import functools
import math

import jax
import jax.numpy as jnp
from jax import lax
from jax.experimental import pallas as pl
from jax.experimental.pallas import tpu as pltpu
from jax.sharding import PartitionSpec as P

RADIUS = 0.2
LANES = 128
GROUP = 32
BATCH = 4
PAIR = 4
CELLS = 5
DEPTH = 64
PAD = 16
PIECES = 3
VMEM = 50 * 1024 * 1024
NT = (((1,), (1,)), ((), ()))
MESH = pl.DeviceIdType.MESH


def scaled(xyz):
    point = (xyz - 0.5) * (1.0 / RADIUS)
    return jnp.concatenate([point, jnp.ones((1, xyz.shape[1]), jnp.float32)], axis=0)


def rounded(value):
    return value.astype(jnp.bfloat16).astype(jnp.float32)


def right_factor(group):
    row = lax.broadcasted_iota(jnp.int32, group.shape, 0)
    place = jnp.where(row >= 4, group, 0.0)
    square = jnp.sum(jnp.where(row < 7, place * place, 0.0), axis=0, keepdims=True)
    beta = jnp.where(row == 0, square, place)
    b1 = rounded(beta)
    rest = beta - b1
    b2 = rounded(rest)
    b3 = rest - b2
    return jnp.concatenate([b1, b2, b1, b2, b3, b1], axis=0).astype(jnp.bfloat16)


def two_parts(vectors):
    v1 = rounded(vectors)
    return jnp.concatenate([v1, vectors - v1], axis=0).astype(jnp.bfloat16)


def boxes(points, size):
    tiles = points[:3].reshape(3, -1, size)
    return jnp.min(tiles, axis=2), jnp.max(tiles, axis=2)


def near_lists(tiles, groups, pieces):
    gap = jnp.maximum(
        jnp.maximum(tiles[0][:, :, None] - groups[1][:, None, :], groups[0][:, None, :] - tiles[1][:, :, None]),
        0.0,
    )
    near = jnp.sum(gap * gap, axis=0) < 1.0 + 1e-4
    size = near.shape[1]
    near = jnp.any(near.reshape(-1, pieces, size), axis=1)
    total = near.shape[0]
    count = jnp.sum(near.astype(jnp.int32), axis=1)
    upto = (jnp.arange(size)[:, None] <= jnp.arange(size)[None, :]).astype(jnp.bfloat16)
    seen = jnp.dot(near.astype(jnp.bfloat16), upto, preferred_element_type=jnp.float32).astype(jnp.int32)
    every = jnp.arange(size, dtype=jnp.int32)
    place = jnp.where(near, seen - 1, count[:, None] + every[None, :] - seen)
    order = jnp.sum(
        jnp.where(place[:, :, None] == every[None, None, :], every[None, :, None], 0), axis=1
    )
    batches = (count + BATCH - 1) // BATCH
    ranks = jnp.arange(total)
    ends = jnp.sum(jnp.where(ranks[:, None] <= ranks[None, :], batches[:, None], 0), axis=0)
    at = jnp.arange(total * size // BATCH + 8 * PAIR, dtype=jnp.int32) - 2 * PAIR
    passed = ends[:, None] <= at[None, :]
    tile = jnp.sum(passed.astype(jnp.int32), axis=0)
    start = jnp.sum(jnp.where(passed, batches[:, None], 0), axis=0)
    code = tile * size + (at - start) * BATCH
    items = jnp.where((at < 0) | (tile == total), total * size, code)
    return jnp.sum(batches, keepdims=True), items, jnp.pad((order * GROUP).reshape(-1), (0, size))


def apply_body(count, items, order, left_ref, right_ref, vec_ref, out_ref, acc, vec, q0, q1, k0, k1):
    rows = left_ref.shape[0]
    tiles = right_ref.shape[0]
    span = GROUP * BATCH
    half = span // 2
    banks, width, deep = vec_ref.shape[:3]
    acc[...] = jnp.zeros_like(acc)
    for ref in (q0, q1, k0, k1):
        ref[...] = jnp.zeros_like(ref)

    blank = jnp.zeros((PAD - width, LANES), jnp.float32)
    for bank in range(banks):
        for at in range(deep):
            parts = two_parts(jnp.concatenate([vec_ref[bank, :, at, :], blank], axis=0))
            vec[bank * deep + at] = jnp.concatenate([parts, parts], axis=1)
    vec[tiles] = jnp.zeros_like(vec[tiles])

    groups = rows // GROUP
    first_half = lax.broadcasted_iota(jnp.int32, (half, LANES), 1) < LANES // 2

    def item(index):
        code = items[index]
        tile = lax.div(code, groups)
        return tile, jnp.minimum(tile, tiles - 1), [
            pl.multiple_of(order[code + i], GROUP) for i in range(BATCH)
        ]

    def rows_at(places):
        return jnp.concatenate([left_ref[pl.ds(place, GROUP), :] for place in places], axis=0)

    def step(index, q_in, q_out, k_in, k_out):
        for unit in range(PAIR):
            tile, _, places = item(index * PAIR + unit)
            part = lax.dot_general(
                k_in[pl.ds(unit * span, span), :], vec[tile], NT, preferred_element_type=jnp.float32
            )
            for j, place in enumerate(places):
                acc[pl.ds(place, GROUP), :] += part[j * GROUP : (j + 1) * GROUP]
        for unit in range(PAIR):
            q = jnp.minimum(jnp.maximum(q_in[pl.ds(unit * half, half), :], 1e-30), 1.0)
            s = q * lax.rsqrt(q)
            w = 1.0 - s
            w2 = w * w
            k = (w2 * w2) * (0.25 + s)
            hi = k.astype(jnp.bfloat16)
            lo = (k - hi.astype(jnp.float32)).astype(jnp.bfloat16)
            for side in range(2):
                here = pl.ds(unit * span + side * half, half)
                lanes = slice(side * LANES, (side + 1) * LANES)
                k_out[here, :LANES] = hi[:, lanes]
                k_out[here, LANES:] = lo[:, lanes]
        for unit in range(PAIR):
            _, listed, places = item((index + 2) * PAIR + unit)
            left = jnp.where(first_half, rows_at(places[: BATCH // 2]), rows_at(places[BATCH // 2 :]))
            q_out[pl.ds(unit * half, half), :] = jnp.dot(
                left, right_ref[listed], preferred_element_type=jnp.float32
            )

    def two_steps(index, _):
        step(2 * index, q0, q1, k0, k1)
        step(2 * index + 1, q1, q0, k1, k0)
        return 0

    steps = (count[0] + PAIR - 1) // PAIR + 2
    lax.fori_loop(0, (steps + 1) // 2, two_steps, 0)

    owners, _, high, _ = out_ref.shape
    for owner in range(owners):
        for at in range(high):
            total = acc[pl.ds((owner * high + at) * LANES, LANES), :].T
            out_ref[owner, :, at, :] = 4.0 * (total[:width] + total[PAD : PAD + width])


def apply_kernel(lists, left, right, vec, owners):
    rows = left.shape[0]
    tiles = right.shape[0]
    width = vec.shape[1]
    wide = PAIR * GROUP * BATCH
    return pl.pallas_call(
        apply_body,
        out_shape=jax.ShapeDtypeStruct((owners, width, rows // owners // LANES, LANES), jnp.float32),
        in_specs=[pl.BlockSpec(memory_space=pltpu.SMEM)] * 3 + [pl.BlockSpec(memory_space=pltpu.VMEM)] * 3,
        out_specs=pl.BlockSpec(memory_space=pltpu.VMEM),
        scratch_shapes=[
            pltpu.VMEM((rows, 2 * PAD), jnp.float32),
            pltpu.VMEM((tiles + 1, 2 * PAD, 2 * LANES), jnp.bfloat16),
            pltpu.VMEM((wide // 2, 2 * LANES), jnp.float32),
            pltpu.VMEM((wide // 2, 2 * LANES), jnp.float32),
            pltpu.VMEM((wide, 2 * LANES), jnp.bfloat16),
            pltpu.VMEM((wide, 2 * LANES), jnp.bfloat16),
        ],
        compiler_params=pltpu.CompilerParams(vmem_limit_bytes=VMEM),
    )(*lists, left, right, vec)


def factor_body(row_ref, col_ref, node_ref, left_ref, col_out, node_out):
    blocks, _, span = row_ref.shape
    blank = jnp.zeros((16, LANES), jnp.float32)
    for block in range(blocks):
        for at in range(span // LANES):
            group = row_ref[block, :, pl.ds(at * LANES, LANES)]
            row = lax.broadcasted_iota(jnp.int32, group.shape, 0)
            place = jnp.where((row >= 4) & (row < 7), group, 0.0)
            square = jnp.sum(place * place, axis=0, keepdims=True)
            alpha = jnp.where(row == 0, 1.0, jnp.where(row == 7, square, -2.0 * place))
            a1 = rounded(alpha)
            a2 = rounded(alpha - a1)
            a3 = alpha - a1 - a2
            parts = [a1, a1, a2, a2, a1, a3, blank]
            left_ref[pl.ds((block * (span // LANES) + at) * LANES, LANES), :] = (
                jnp.concatenate(parts + parts, axis=0).T.astype(jnp.bfloat16)
            )

    def fill(source, target):
        blocks, _, span = source.shape
        per = span // LANES
        zero = jnp.zeros((64, LANES), jnp.bfloat16)
        pad = jnp.zeros((16, LANES), jnp.bfloat16)
        for block in range(blocks):
            for at in range(per):
                right = jnp.concatenate([right_factor(source[block, :, pl.ds(at * LANES, LANES)]), pad], axis=0)
                target[block * per + at] = jnp.concatenate(
                    [jnp.concatenate([right, zero], axis=0), jnp.concatenate([zero, right], axis=0)], axis=1
                )

    fill(col_ref, col_out)
    fill(node_ref, node_out)


def factors(row_points, col_points, node_points):
    def tiles(points):
        return points.shape[0] * points.shape[2] // LANES

    def shape(points):
        return jax.ShapeDtypeStruct((tiles(points), LANES, 2 * LANES), jnp.bfloat16)

    return pl.pallas_call(
        factor_body,
        out_shape=[
            jax.ShapeDtypeStruct((tiles(row_points) * LANES, LANES), jnp.bfloat16),
            shape(col_points),
            shape(node_points),
        ],
        in_specs=[pl.BlockSpec(memory_space=pltpu.VMEM)] * 3,
        out_specs=[pl.BlockSpec(memory_space=pltpu.VMEM)] * 3,
        compiler_params=pltpu.CompilerParams(vmem_limit_bytes=VMEM),
    )(row_points, col_points, node_points)


def node_rows_body(slab_ref, perm_ref, xyz_ref, cot_ref, xyz_out, cot_out, rows_a, rows_b, rows_c):
    count = cot_ref.shape[1]
    width = cot_ref.shape[0]
    blank = jnp.zeros((PAD - width, LANES), jnp.float32)
    for tile in range(count // LANES):
        here = pl.ds(tile * LANES, LANES)
        rows_a[here, :PAD] = jnp.concatenate([cot_ref[:, here], blank], axis=0).T

    def scatter(index, _):
        base = pl.multiple_of(index * 64, 64)
        for i in range(64):
            rows_b[pl.ds(slab_ref[base + i], 1), :] = rows_a[pl.ds(base + i, 1), :]
        return 0

    lax.fori_loop(0, count // 64, scatter, 0)
    for tile in range(count // LANES):
        here = pl.ds(tile * LANES, LANES)
        rows_b[here, PAD : PAD + 8] = xyz_ref[:, here].T

    def gather(index, _):
        base = pl.multiple_of(index * 64, 64)
        for i in range(64):
            rows_c[pl.ds(base + i, 1), :] = rows_b[pl.ds(perm_ref[base + i], 1), :]
        return 0

    lax.fori_loop(0, count // 64, gather, 0)
    for tile in range(count // LANES):
        here = rows_c[pl.ds(tile * LANES, LANES), :].T
        cot_out[0, :, tile, :] = here[:width]
        xyz_out[0, :, pl.ds(tile * LANES, LANES)] = here[PAD : PAD + 8]


def node_rows(slab, perm, xyz, cotangent):
    count = cotangent.shape[1]
    width = cotangent.shape[0]
    tiles = count // LANES
    return pl.pallas_call(
        node_rows_body,
        out_shape=[
            jax.ShapeDtypeStruct((1, 8, count), jnp.float32),
            jax.ShapeDtypeStruct((1, width, tiles, LANES), jnp.float32),
        ],
        in_specs=[pl.BlockSpec(memory_space=pltpu.SMEM)] * 2 + [pl.BlockSpec(memory_space=pltpu.VMEM)] * 2,
        out_specs=[pl.BlockSpec(memory_space=pltpu.VMEM)] * 2,
        scratch_shapes=[pltpu.VMEM((count, LANES), jnp.float32)] * 3,
        compiler_params=pltpu.CompilerParams(vmem_limit_bytes=VMEM),
    )(slab, perm, xyz, cotangent)


def pick_body(slot_ref, table_ref, sol_ref, res_ref, rows_a, rows_b):
    blocks, width, deep, _ = table_ref.shape
    count = sol_ref.shape[1]
    half = width // 2
    for block in range(blocks):
        for tile in range(deep):
            rows_a[pl.ds((block * deep + tile) * LANES, LANES), :width] = table_ref[block, :, tile, :].T

    def gather(index, _):
        base = pl.multiple_of(index * 64, 64)
        for i in range(64):
            rows_b[pl.ds(base + i, 1), :] = rows_a[pl.ds(slot_ref[base + i], 1), :]
        return 0

    lax.fori_loop(0, count // 64, gather, 0)
    for tile in range(count // LANES):
        here = pl.ds(tile * LANES, LANES)
        values = rows_b[here, :].T
        sol_ref[:, here] = values[:half]
        res_ref[:, here] = values[half:width]


def pick(slots, table):
    blocks, width, deep, _ = table.shape
    count = slots.shape[0]
    return pl.pallas_call(
        pick_body,
        out_shape=[jax.ShapeDtypeStruct((width // 2, count), jnp.float32)] * 2,
        in_specs=[pl.BlockSpec(memory_space=pltpu.SMEM), pl.BlockSpec(memory_space=pltpu.VMEM)],
        out_specs=[pl.BlockSpec(memory_space=pltpu.VMEM)] * 2,
        scratch_shapes=[
            pltpu.VMEM((blocks * deep * LANES, LANES), jnp.float32),
            pltpu.VMEM((count, LANES), jnp.float32),
        ],
        compiler_params=pltpu.CompilerParams(vmem_limit_bytes=VMEM),
    )(slots, table)


class Links:
    def __init__(self, nodes, ctrs):
        self.nodes, self.ctrs = nodes, ctrs
        self.node, self.ctr = lax.axis_index("node"), lax.axis_index("ctr")
        self.me = self.node * ctrs + self.ctr

    def on_node(self, hop):
        return (lax.rem(self.node + hop, self.nodes), self.ctr)

    def on_ctr(self, hop):
        return (self.node, lax.rem(self.ctr + hop, self.ctrs))

    def anyone(self, hop):
        other = lax.rem(self.me + hop, self.nodes * self.ctrs)
        return (other // self.ctrs, lax.rem(other, self.ctrs))

    def meet(self, targets):
        barrier = pltpu.get_barrier_semaphore()
        for target in targets:
            pl.semaphore_signal(barrier, inc=1, device_id=target, device_id_type=MESH)
        pl.semaphore_wait(barrier, len(targets))

    def node_hops(self):
        return range(1, self.nodes)

    def ctr_hops(self):
        return range(1, self.ctrs)

    def meet_sides(self):
        self.meet([self.on_node(h) for h in self.node_hops()] + [self.on_ctr(h) for h in self.ctr_hops()])

    def meet_all(self):
        self.meet([self.anyone(h) for h in range(1, self.nodes * self.ctrs)])


def send(source, target, sems, index, device):
    copy = pltpu.make_async_remote_copy(
        src_ref=source,
        dst_ref=target,
        send_sem=sems[0].at[index],
        recv_sem=sems[1].at[index],
        device_id=device,
        device_id_type=MESH,
    )
    copy.start()
    return copy


def finish(copies):
    for copy in copies:
        copy.wait()


def comm_call(body, nodes, ctrs, out_shape, scratch, collective, *args):
    return pl.pallas_call(
        functools.partial(body, nodes, ctrs),
        out_shape=out_shape,
        in_specs=[pl.BlockSpec(memory_space=pltpu.VMEM)] * len(args),
        out_specs=jax.tree.map(lambda _: pl.BlockSpec(memory_space=pltpu.VMEM), out_shape),
        scratch_shapes=scratch,
        compiler_params=pltpu.CompilerParams(
            collective_id=collective, has_side_effects=True, vmem_limit_bytes=VMEM
        ),
    )(*args)


def dma_pair(count):
    return [pltpu.SemaphoreType.DMA((count,))] * 2


TN = (((0,), (0,)), ((), ()))


def picked(tables, rows, lanes):
    high = lax.broadcasted_iota(jnp.int32, (tables[0].shape[0], rows.shape[1]), 0) == rows
    high = jnp.where(high, 1.0, 0.0).astype(jnp.bfloat16)
    low = lax.broadcasted_iota(jnp.int32, (LANES, rows.shape[1]), 0) == lanes
    found = []
    for table in tables:
        a1 = rounded(table)
        a2 = rounded(table - a1)
        a3 = table - a1 - a2
        parts = jnp.concatenate([a1, a2, a3], axis=1).astype(jnp.bfloat16)
        both = lax.dot_general(parts, high, TN, preferred_element_type=jnp.float32)
        value = both[:LANES] + both[LANES : 2 * LANES] + both[2 * LANES :]
        found.append(jnp.sum(jnp.where(low, value, 0.0), axis=0, keepdims=True))
    return found


def cell_keys(x, y, z):
    rows = x.shape[0]
    count = rows * LANES
    across = jnp.minimum((x * CELLS).astype(jnp.int32), CELLS - 1)
    along = jnp.minimum((y * CELLS).astype(jnp.int32), CELLS - 1)
    deep = jnp.minimum((z * DEPTH).astype(jnp.int32), DEPTH - 1)
    column = across * CELLS + jnp.where(across % 2 == 1, CELLS - 1 - along, along)
    deep = jnp.where(column % 2 == 1, DEPTH - 1 - deep, deep)
    index = lax.broadcasted_iota(jnp.int32, x.shape, 0) * LANES + lax.broadcasted_iota(jnp.int32, x.shape, 1)
    return ((column * DEPTH + deep) * count + index).astype(jnp.float32)


def sorted_keys(keys):
    rows = keys.shape[0]
    row = lax.broadcasted_iota(jnp.int32, keys.shape, 0)
    lane = lax.broadcasted_iota(jnp.int32, keys.shape, 1)
    bits = (rows * LANES).bit_length() - 1

    def bit(at):
        return (lane // 2**at) % 2 == 0 if at < 7 else (row // 2 ** (at - 7)) % 2 == 0

    zeros = [bit(at) for at in range(bits)]
    for level in range(1, bits + 1):
        for at in range(level - 1, -1, -1):
            axis, size, shift = (1, LANES, 2**at) if at < 7 else (0, rows, 2 ** (at - 7))
            other = jnp.where(
                zeros[at], pltpu.roll(keys, size - shift, axis), pltpu.roll(keys, shift, axis)
            )
            small = zeros[at] if level == bits else zeros[at] == zeros[level]
            keys = jnp.where(small, jnp.minimum(keys, other), jnp.maximum(keys, other))
    return keys


def setup_body(
    nodes, ctrs, own_ref, ids_ref, volume_ref, perm_ref, node_ref, ctr_ref, slab_ref,
    all_ref, mine_ref, plane_ref, table_ref, point_ref, *sems,
):
    links = Links(nodes, ctrs)
    links.meet_sides()
    mine = all_ref.at[links.ctr, links.node]
    copies = [send(own_ref, mine, sems[:2], h - 1, links.on_node(h)) for h in links.node_hops()]
    all_ref[links.ctr, links.node] = own_ref[...]
    keys = sorted_keys(cell_keys(*(volume_ref[k] for k in range(3))))
    slab_ref[...] = keys.astype(jnp.int32) % (keys.shape[0] * LANES)
    finish(copies)
    whole = all_ref.at[links.ctr]
    last = nodes - 1
    if ctrs == 4:
        far = lax.rem(links.ctr + 2, 4)
        near = (links.node, links.ctr + 1 - 2 * lax.rem(links.ctr, 2))
        across = send(whole, whole, sems[:2], last, (links.node, far))
        beside = send(whole, whole, sems[:2], last + 1, near)
        across.wait()
        other = all_ref.at[far]
        finish([send(other, other, sems[:2], last + 2, near), beside])
    else:
        finish([send(whole, whole, sems[:2], last - 1 + h, links.on_ctr(h)) for h in links.ctr_hops()])

    rows, tiles = own_ref.shape[1], mine_ref.shape[1]
    tables = [all_ref[:, :, k].reshape(-1, LANES) for k in range(3)]
    for at in range(tiles):
        ids = ids_ref[at : at + 1, :]
        device = ids // (rows * LANES)
        place = (device % ctrs * nodes + device // ctrs) * rows + ids // LANES % rows
        for k, value in enumerate(picked(tables, place, ids % LANES)):
            mine_ref[k, at : at + 1, :] = value
    copies = [
        send(mine_ref, plane_ref.at[links.node], sems[2:4], h - 1, links.on_node(h)) for h in links.node_hops()
    ]
    plane_ref[links.node] = mine_ref[...]
    finish(copies)

    for node in range(nodes):
        for k in range(3):
            table_ref[k, node * tiles : (node + 1) * tiles, :] = plane_ref[node, k]
    tables = [table_ref[k] for k in range(3)]
    count = tables[0].shape[0] * LANES
    keys = sorted_keys(cell_keys(*tables))
    perm_ref[...] = keys.astype(jnp.int32) % count
    blank = jnp.zeros((4, LANES), jnp.float32)
    for at in range(tiles):
        ids = perm_ref[pl.ds(at * nodes + links.node, 1), :]
        found = [(v - 0.5) * (1.0 / RADIUS) for v in picked(tables, ids // LANES, ids % LANES)]
        point_ref[:, at * LANES : (at + 1) * LANES] = jnp.concatenate(
            [blank] + found + [jnp.ones((1, LANES), jnp.float32)], axis=0
        )
    copies = [send(point_ref, node_ref.at[links.node], sems[4:6], h - 1, links.on_node(h)) for h in links.node_hops()]
    copies += [
        send(point_ref, ctr_ref.at[links.ctr], sems[4:6], nodes - 2 + h, links.on_ctr(h)) for h in links.ctr_hops()
    ]
    node_ref[links.node] = point_ref[...]
    ctr_ref[links.ctr] = point_ref[...]
    finish(copies)


def reduced(links, part_ref, landing, sems):
    copies = []
    for h in links.node_hops():
        device = links.on_node(h)
        copies.append(send(part_ref.at[device[0]], landing.at[h - 1], sems, h - 1, device))
    total = part_ref[links.node]
    for h, copy in zip(links.node_hops(), copies):
        copy.wait()
        total = total + landing[h - 1]
    return total


def wanted(rows, index):
    row = lax.broadcasted_iota(jnp.int32, (rows, LANES), 0)
    lane = lax.broadcasted_iota(jnp.int32, (rows, LANES), 1)
    return lane == row + 32 * index


def share_start(links, values, own, everyone, sems):
    line = 0.0
    for index, value in enumerate(values):
        column = jnp.sum(jnp.sum(value, axis=1), axis=1, keepdims=True)
        line += jnp.sum(
            jnp.where(wanted(column.shape[0], index), column, 0.0), axis=0, keepdims=True
        )
    own[...] = line
    hops = range(1, links.nodes * links.ctrs)
    copies = [send(own, everyone.at[links.me], sems, h - 1, links.anyone(h)) for h in hops]
    everyone[links.me] = own[...]
    return copies


def share_end(copies, count, rows, everyone):
    finish(copies)
    line = jnp.sum(everyone[...], axis=0)
    return [
        jnp.sum(jnp.where(wanted(rows, index), line, 0.0), axis=1, keepdims=True) for index in range(count)
    ]


def spread(column, ref):
    ref[...] = jnp.broadcast_to(column, ref.shape)
    return [ref[v : v + 1, :] for v in range(ref.shape[0])]


def pulled_body(nodes, ctrs, part_ref, own_ref, cols_ref, landing, s0, s1, t0, t1):
    links = Links(nodes, ctrs)
    links.meet_sides()
    own_ref[...] = reduced(links, part_ref, landing, (s0, s1))
    copies = [
        send(own_ref, cols_ref.at[links.ctr], (t0, t1), h - 1, links.on_ctr(h)) for h in links.ctr_hops()
    ]
    cols_ref[links.ctr] = own_ref[...]
    finish(copies)


def first_body(
    nodes, ctrs, part_ref, pulled_ref, pulled_cols, resid_ref, dir_cols, scal_ref,
    landing, image_ref, cols, line, every, scr0, scr1, s0, s1, t0, t1, u0, u1,
):
    links = Links(nodes, ctrs)
    links.meet_all()
    image = reduced(links, part_ref, landing, (s0, s1))
    image_ref[...] = image
    pulled = pulled_ref[...]
    told = share_start(
        links, [pulled * pulled, pulled * image, image * image], line, every, (t0, t1)
    )
    copies = [
        send(image_ref, cols.at[links.ctr], (u0, u1), h - 1, links.on_ctr(h)) for h in links.ctr_hops()
    ]
    cols[links.ctr] = image
    width = pulled_ref.shape[0]
    norm, curve, square = share_end(told, 3, width, every)
    alpha = norm / curve
    ratio = alpha * square / curve - 1.0
    alphas, ratios = spread(alpha, scr0), spread(ratio, scr1)
    scal_ref[0] = scr0[...]
    scal_ref[1] = scr1[...]
    for v in range(width):
        resid_ref[v] = pulled_ref[v] - alphas[v] * image_ref[v]
    finish(copies)
    for c in range(ctrs):
        for v in range(width):
            dir_cols[c, v] = (pulled_cols[c, v] - alphas[v] * cols[c, v]) + ratios[v] * pulled_cols[c, v]


def second_body(
    nodes, ctrs, part_ref, pulled_ref, resid_ref, scal_ref, out_ref,
    landing, final, line, every, scr0, s0, s1, t0, t1, u0, u1,
):
    links = Links(nodes, ctrs)
    links.meet_all()
    image = reduced(links, part_ref, landing, (s0, s1))
    width = pulled_ref.shape[0]
    alphas = [scal_ref[0, v : v + 1, :] for v in range(width)]
    ratios = [scal_ref[1, v : v + 1, :] for v in range(width)]
    for v in range(width):
        final[v] = resid_ref[v] + ratios[v] * pulled_ref[v]
    resid = resid_ref[...]
    told = share_start(links, [resid * resid, final[:width] * image], line, every, (t0, t1))
    final[width:] = image
    norm, curve = share_end(told, 2, width, every)
    seconds = spread(norm / curve, scr0)
    for v in range(width):
        final[v] = alphas[v] * pulled_ref[v] + seconds[v] * final[v]
        final[width + v] = resid_ref[v] - seconds[v] * final[width + v]
    out_ref[links.node] = final[...]
    if nodes % 2:
        mine = out_ref.at[links.node]
        finish([send(final, mine, (u0, u1), h - 1, links.on_node(h)) for h in links.node_hops()])
        return
    beside = (links.node + 1 - 2 * lax.rem(links.node, 2), links.ctr)
    half = nodes // 2
    size = 2 * width // PIECES
    copies, relays = [], []
    for piece in range(PIECES):
        base, rows = piece * (nodes - 1), pl.ds(piece * size, size)
        mine, target = final.at[rows], out_ref.at[links.node, rows]
        copies.append([send(mine, target, (u0, u1), base + h, links.on_node(2 * h)) for h in range(1, half)])
        relays.append(send(mine, target, (u0, u1), base, beside))
    for piece in range(PIECES):
        base, rows = piece * (nodes - 1), pl.ds(piece * size, size)
        for h, copy in zip(range(1, half), copies[piece]):
            copy.wait()
            came = out_ref.at[lax.rem(links.node + nodes - 2 * h, nodes), rows]
            relays.append(send(came, came, (u0, u1), base + half - 1 + h, beside))
    finish(relays)


def local(nodes, ctrs, surface_xyz, centre_idx, volume_xyz, slab_ids, cotangent):
    width = cotangent.shape[0]
    owned = centre_idx.shape[0]
    total = owned * nodes
    here = lax.axis_index("node")
    f32 = jnp.float32
    vmem = lambda *shape: pltpu.VMEM(shape, f32)
    out = lambda *shape: jax.ShapeDtypeStruct(shape, f32)
    devices = nodes * ctrs

    slab = slab_ids % volume_xyz.shape[1]
    volume_points = jnp.concatenate(
        [scaled(volume_xyz), jnp.zeros((4, volume_xyz.shape[1]), f32)], axis=0
    )
    volume_points = jnp.concatenate([volume_points[4:], volume_points[:4]], axis=0)

    rows = surface_xyz.shape[1] // LANES
    tiles = owned // LANES
    perm, row_points, col_points, node_perm = comm_call(
        setup_body, nodes, ctrs,
        (
            jax.ShapeDtypeStruct((total // LANES, LANES), jnp.int32), out(nodes, 8, owned), out(ctrs, 8, owned),
            jax.ShapeDtypeStruct((volume_xyz.shape[1] // LANES, LANES), jnp.int32),
        ),
        [
            vmem(ctrs, nodes, 3, rows, LANES), vmem(3, tiles, LANES), vmem(nodes, 3, tiles, LANES),
            vmem(3, total // LANES, LANES), vmem(8, owned),
        ] + dma_pair(nodes + ctrs - 2) + dma_pair(nodes - 1) + dma_pair(nodes + ctrs - 2),
        0, surface_xyz.reshape(3, rows, LANES), centre_idx.reshape(tiles, LANES),
        volume_xyz.reshape(3, -1, LANES),
    )
    by_owner = perm.reshape(tiles, nodes, LANES)
    node_points, node_vec = node_rows(slab, node_perm.reshape(-1), volume_points, cotangent)
    left, col_right, node_right = factors(row_points, col_points, node_points)
    flat = lambda value: value.transpose(1, 0, 2).reshape(8, -1)[4:]
    groups = boxes(flat(row_points), GROUP)
    node_lists = near_lists(boxes(flat(node_points), LANES // 2), groups, 2)
    col_lists = near_lists(boxes(flat(col_points), LANES), groups, 1)

    places = jnp.arange(total, dtype=jnp.int32)
    hit = (by_owner.transpose(1, 0, 2).reshape(total) // LANES)[None, :] == (
        here * tiles + jnp.arange(tiles, dtype=jnp.int32)
    )[:, None]
    spots = jnp.concatenate(
        [jnp.where(hit, (places // LANES)[None, :], 0), jnp.where(hit, (places % LANES)[None, :], 0)], axis=0
    ).astype(jnp.bfloat16)
    lane = (
        by_owner.transpose(1, 0, 2).reshape(total)[:, None] % LANES == jnp.arange(LANES, dtype=jnp.int32)[None, :]
    ).astype(jnp.bfloat16)
    spots = jnp.dot(spots, lane, preferred_element_type=f32).astype(jnp.int32)
    slots = (spots[:tiles] * LANES + spots[tiles:]).reshape(owned)

    own_shape, scr = out(width, tiles, LANES), vmem(width, LANES)
    cols_shape = out(ctrs, width, tiles, LANES)
    landing = vmem(nodes - 1, width, tiles, LANES)
    line, every = vmem(1, LANES), vmem(devices, 1, LANES)
    part = apply_kernel(node_lists, left, node_right, node_vec, nodes)
    pulled, pulled_cols = comm_call(
        pulled_body, nodes, ctrs, (own_shape, cols_shape),
        [landing] + dma_pair(nodes - 1) + dma_pair(ctrs - 1), 3, part,
    )
    part = apply_kernel(col_lists, left, col_right, pulled_cols, nodes)
    resid, dir_cols, scal = comm_call(
        first_body, nodes, ctrs, (own_shape, cols_shape, out(2, width, LANES)),
        [landing, vmem(width, tiles, LANES), vmem(ctrs, width, tiles, LANES), line, every, scr, scr]
        + dma_pair(nodes - 1) + dma_pair(devices - 1) + dma_pair(ctrs - 1),
        4, part, pulled, pulled_cols,
    )
    part = apply_kernel(col_lists, left, col_right, dir_cols, nodes)
    final = comm_call(
        second_body, nodes, ctrs, out(nodes, 2 * width, tiles, LANES),
        [landing, vmem(2 * width, tiles, LANES), line, every, scr]
        + dma_pair(nodes - 1) + dma_pair(devices - 1) + dma_pair(PIECES * (nodes - 1)),
        5, part, pulled, resid, scal,
    )
    return tuple(pick(slots, final))


def solution(mesh):
    return jax.shard_map(
        functools.partial(local, mesh.shape["node"], mesh.shape["ctr"]),
        mesh=mesh,
        in_specs=(
            P(None, ("node", "ctr")),
            P(("node", "ctr")),
            P(None, "node"),
            P("node"),
            P(None, "node"),
        ),
        out_specs=(P(None, ("node", "ctr")), P(None, ("node", "ctr"))),
        check_vma=False,
    )
```

```python
import functools
import math

import jax
import jax.numpy as jnp
from jax import lax
from jax.experimental import pallas as pl
from jax.experimental.pallas import tpu as pltpu
from jax.sharding import PartitionSpec as P

RADIUS = 0.2
LANES = 128
GROUP = 32
BATCH = 4
PAIR = 4
CELLS = 5
DEPTH = 64
PAD = 16
PIECES = 3
VMEM = 50 * 1024 * 1024
NT = (((1,), (1,)), ((), ()))
MESH = pl.DeviceIdType.MESH


def scaled(xyz):
    point = (xyz - 0.5) * (1.0 / RADIUS)
    return jnp.concatenate([point, jnp.ones((1, xyz.shape[1]), jnp.float32)], axis=0)


def rounded(value):
    return value.astype(jnp.bfloat16).astype(jnp.float32)


def right_factor(group):
    row = lax.broadcasted_iota(jnp.int32, group.shape, 0)
    place = jnp.where(row >= 4, group, 0.0)
    square = jnp.sum(jnp.where(row < 7, place * place, 0.0), axis=0, keepdims=True)
    beta = jnp.where(row == 0, square, place)
    b1 = rounded(beta)
    rest = beta - b1
    b2 = rounded(rest)
    b3 = rest - b2
    return jnp.concatenate([b1, b2, b1, b2, b3, b1], axis=0).astype(jnp.bfloat16)


def two_parts(vectors):
    v1 = rounded(vectors)
    return jnp.concatenate([v1, vectors - v1], axis=0).astype(jnp.bfloat16)


def boxes(points, size):
    tiles = points[:3].reshape(3, -1, size)
    return jnp.min(tiles, axis=2), jnp.max(tiles, axis=2)


def near_lists(tiles, groups, pieces):
    gap = jnp.maximum(
        jnp.maximum(tiles[0][:, :, None] - groups[1][:, None, :], groups[0][:, None, :] - tiles[1][:, :, None]),
        0.0,
    )
    near = jnp.sum(gap * gap, axis=0) < 1.0 + 1e-4
    size = near.shape[1]
    near = jnp.any(near.reshape(-1, pieces, size), axis=1)
    total = near.shape[0]
    count = jnp.sum(near.astype(jnp.int32), axis=1)
    upto = (jnp.arange(size)[:, None] <= jnp.arange(size)[None, :]).astype(jnp.bfloat16)
    seen = jnp.dot(near.astype(jnp.bfloat16), upto, preferred_element_type=jnp.float32).astype(jnp.int32)
    every = jnp.arange(size, dtype=jnp.int32)
    place = jnp.where(near, seen - 1, count[:, None] + every[None, :] - seen)
    order = jnp.sum(
        jnp.where(place[:, :, None] == every[None, None, :], every[None, :, None], 0), axis=1
    )
    batches = (count + BATCH - 1) // BATCH
    ranks = jnp.arange(total)
    ends = jnp.sum(jnp.where(ranks[:, None] <= ranks[None, :], batches[:, None], 0), axis=0)
    at = jnp.arange(total * size // BATCH + 8 * PAIR, dtype=jnp.int32) - 2 * PAIR
    passed = ends[:, None] <= at[None, :]
    tile = jnp.sum(passed.astype(jnp.int32), axis=0)
    start = jnp.sum(jnp.where(passed, batches[:, None], 0), axis=0)
    code = tile * size + (at - start) * BATCH
    items = jnp.where((at < 0) | (tile == total), total * size, code)
    return jnp.sum(batches, keepdims=True), items, jnp.pad((order * GROUP).reshape(-1), (0, size))


def apply_body(count, items, order, left_ref, right_ref, vec_ref, out_ref, acc, vec, q0, q1, k0, k1):
    rows = left_ref.shape[0]
    tiles = right_ref.shape[0]
    span = GROUP * BATCH
    half = span // 2
    banks, width, deep = vec_ref.shape[:3]
    acc[...] = jnp.zeros_like(acc)
    for ref in (q0, q1, k0, k1):
        ref[...] = jnp.zeros_like(ref)

    blank = jnp.zeros((PAD - width, LANES), jnp.float32)
    for bank in range(banks):
        for at in range(deep):
            parts = two_parts(jnp.concatenate([vec_ref[bank, :, at, :], blank], axis=0))
            vec[bank * deep + at] = jnp.concatenate([parts, parts], axis=1)
    vec[tiles] = jnp.zeros_like(vec[tiles])

    groups = rows // GROUP
    first_half = lax.broadcasted_iota(jnp.int32, (half, LANES), 1) < LANES // 2

    def item(index):
        code = items[index]
        tile = lax.div(code, groups)
        return tile, jnp.minimum(tile, tiles - 1), [
            pl.multiple_of(order[code + i], GROUP) for i in range(BATCH)
        ]

    def rows_at(places):
        return jnp.concatenate([left_ref[pl.ds(place, GROUP), :] for place in places], axis=0)

    def step(index, q_in, q_out, k_in, k_out):
        for unit in range(PAIR):
            tile, _, places = item(index * PAIR + unit)
            part = lax.dot_general(
                k_in[pl.ds(unit * span, span), :], vec[tile], NT, preferred_element_type=jnp.float32
            )
            for j, place in enumerate(places):
                acc[pl.ds(place, GROUP), :] += part[j * GROUP : (j + 1) * GROUP]
        for unit in range(PAIR):
            q = jnp.minimum(jnp.maximum(q_in[pl.ds(unit * half, half), :], 1e-30), 1.0)
            s = q * lax.rsqrt(q)
            w = 1.0 - s
            w2 = w * w
            k = (w2 * w2) * (0.25 + s)
            hi = k.astype(jnp.bfloat16)
            lo = (k - hi.astype(jnp.float32)).astype(jnp.bfloat16)
            for side in range(2):
                here = pl.ds(unit * span + side * half, half)
                lanes = slice(side * LANES, (side + 1) * LANES)
                k_out[here, :LANES] = hi[:, lanes]
                k_out[here, LANES:] = lo[:, lanes]
        for unit in range(PAIR):
            _, listed, places = item((index + 2) * PAIR + unit)
            left = jnp.where(first_half, rows_at(places[: BATCH // 2]), rows_at(places[BATCH // 2 :]))
            q_out[pl.ds(unit * half, half), :] = jnp.dot(
                left, right_ref[listed], preferred_element_type=jnp.float32
            )

    def two_steps(index, _):
        step(2 * index, q0, q1, k0, k1)
        step(2 * index + 1, q1, q0, k1, k0)
        return 0

    steps = (count[0] + PAIR - 1) // PAIR + 2
    lax.fori_loop(0, (steps + 1) // 2, two_steps, 0)

    owners, _, high, _ = out_ref.shape
    for owner in range(owners):
        for at in range(high):
            total = acc[pl.ds((owner * high + at) * LANES, LANES), :].T
            out_ref[owner, :, at, :] = 4.0 * (total[:width] + total[PAD : PAD + width])


def apply_kernel(lists, left, right, vec, owners):
    rows = left.shape[0]
    tiles = right.shape[0]
    width = vec.shape[1]
    wide = PAIR * GROUP * BATCH
    return pl.pallas_call(
        apply_body,
        out_shape=jax.ShapeDtypeStruct((owners, width, rows // owners // LANES, LANES), jnp.float32),
        in_specs=[pl.BlockSpec(memory_space=pltpu.SMEM)] * 3 + [pl.BlockSpec(memory_space=pltpu.VMEM)] * 3,
        out_specs=pl.BlockSpec(memory_space=pltpu.VMEM),
        scratch_shapes=[
            pltpu.VMEM((rows, 2 * PAD), jnp.float32),
            pltpu.VMEM((tiles + 1, 2 * PAD, 2 * LANES), jnp.bfloat16),
            pltpu.VMEM((wide // 2, 2 * LANES), jnp.float32),
            pltpu.VMEM((wide // 2, 2 * LANES), jnp.float32),
            pltpu.VMEM((wide, 2 * LANES), jnp.bfloat16),
            pltpu.VMEM((wide, 2 * LANES), jnp.bfloat16),
        ],
        compiler_params=pltpu.CompilerParams(vmem_limit_bytes=VMEM),
    )(*lists, left, right, vec)


def factor_body(row_ref, col_ref, node_ref, left_ref, col_out, node_out):
    blocks, _, span = row_ref.shape
    blank = jnp.zeros((16, LANES), jnp.float32)
    for block in range(blocks):
        for at in range(span // LANES):
            group = row_ref[block, :, pl.ds(at * LANES, LANES)]
            row = lax.broadcasted_iota(jnp.int32, group.shape, 0)
            place = jnp.where((row >= 4) & (row < 7), group, 0.0)
            square = jnp.sum(place * place, axis=0, keepdims=True)
            alpha = jnp.where(row == 0, 1.0, jnp.where(row == 7, square, -2.0 * place))
            a1 = rounded(alpha)
            a2 = rounded(alpha - a1)
            a3 = alpha - a1 - a2
            parts = [a1, a1, a2, a2, a1, a3, blank]
            left_ref[pl.ds((block * (span // LANES) + at) * LANES, LANES), :] = (
                jnp.concatenate(parts + parts, axis=0).T.astype(jnp.bfloat16)
            )

    def fill(source, target):
        blocks, _, span = source.shape
        per = span // LANES
        zero = jnp.zeros((64, LANES), jnp.bfloat16)
        pad = jnp.zeros((16, LANES), jnp.bfloat16)
        for block in range(blocks):
            for at in range(per):
                right = jnp.concatenate([right_factor(source[block, :, pl.ds(at * LANES, LANES)]), pad], axis=0)
                target[block * per + at] = jnp.concatenate(
                    [jnp.concatenate([right, zero], axis=0), jnp.concatenate([zero, right], axis=0)], axis=1
                )

    fill(col_ref, col_out)
    fill(node_ref, node_out)


def factors(row_points, col_points, node_points):
    def tiles(points):
        return points.shape[0] * points.shape[2] // LANES

    def shape(points):
        return jax.ShapeDtypeStruct((tiles(points), LANES, 2 * LANES), jnp.bfloat16)

    return pl.pallas_call(
        factor_body,
        out_shape=[
            jax.ShapeDtypeStruct((tiles(row_points) * LANES, LANES), jnp.bfloat16),
            shape(col_points),
            shape(node_points),
        ],
        in_specs=[pl.BlockSpec(memory_space=pltpu.VMEM)] * 3,
        out_specs=[pl.BlockSpec(memory_space=pltpu.VMEM)] * 3,
        compiler_params=pltpu.CompilerParams(vmem_limit_bytes=VMEM),
    )(row_points, col_points, node_points)


def node_rows_body(slab_ref, perm_ref, xyz_ref, cot_ref, xyz_out, cot_out, rows_a, rows_b, rows_c):
    count = cot_ref.shape[1]
    width = cot_ref.shape[0]
    blank = jnp.zeros((PAD - width, LANES), jnp.float32)
    for tile in range(count // LANES):
        here = pl.ds(tile * LANES, LANES)
        rows_a[here, :PAD] = jnp.concatenate([cot_ref[:, here], blank], axis=0).T

    def scatter(index, _):
        base = pl.multiple_of(index * 64, 64)
        for i in range(64):
            rows_b[pl.ds(slab_ref[base + i], 1), :] = rows_a[pl.ds(base + i, 1), :]
        return 0

    lax.fori_loop(0, count // 64, scatter, 0)
    for tile in range(count // LANES):
        here = pl.ds(tile * LANES, LANES)
        rows_b[here, PAD : PAD + 8] = xyz_ref[:, here].T

    def gather(index, _):
        base = pl.multiple_of(index * 64, 64)
        for i in range(64):
            rows_c[pl.ds(base + i, 1), :] = rows_b[pl.ds(perm_ref[base + i], 1), :]
        return 0

    lax.fori_loop(0, count // 64, gather, 0)
    for tile in range(count // LANES):
        here = rows_c[pl.ds(tile * LANES, LANES), :].T
        cot_out[0, :, tile, :] = here[:width]
        xyz_out[0, :, pl.ds(tile * LANES, LANES)] = here[PAD : PAD + 8]


def node_rows(slab, perm, xyz, cotangent):
    count = cotangent.shape[1]
    width = cotangent.shape[0]
    tiles = count // LANES
    return pl.pallas_call(
        node_rows_body,
        out_shape=[
            jax.ShapeDtypeStruct((1, 8, count), jnp.float32),
            jax.ShapeDtypeStruct((1, width, tiles, LANES), jnp.float32),
        ],
        in_specs=[pl.BlockSpec(memory_space=pltpu.SMEM)] * 2 + [pl.BlockSpec(memory_space=pltpu.VMEM)] * 2,
        out_specs=[pl.BlockSpec(memory_space=pltpu.VMEM)] * 2,
        scratch_shapes=[pltpu.VMEM((count, LANES), jnp.float32)] * 3,
        compiler_params=pltpu.CompilerParams(vmem_limit_bytes=VMEM),
    )(slab, perm, xyz, cotangent)


def pick_body(slot_ref, table_ref, sol_ref, res_ref, rows_a, rows_b):
    blocks, width, deep, _ = table_ref.shape
    count = sol_ref.shape[1]
    half = width // 2
    for block in range(blocks):
        for tile in range(deep):
            rows_a[pl.ds((block * deep + tile) * LANES, LANES), :width] = table_ref[block, :, tile, :].T

    def gather(index, _):
        base = pl.multiple_of(index * 64, 64)
        for i in range(64):
            rows_b[pl.ds(base + i, 1), :] = rows_a[pl.ds(slot_ref[base + i], 1), :]
        return 0

    lax.fori_loop(0, count // 64, gather, 0)
    for tile in range(count // LANES):
        here = pl.ds(tile * LANES, LANES)
        values = rows_b[here, :].T
        sol_ref[:, here] = values[:half]
        res_ref[:, here] = values[half:width]


def pick(slots, table):
    blocks, width, deep, _ = table.shape
    count = slots.shape[0]
    return pl.pallas_call(
        pick_body,
        out_shape=[jax.ShapeDtypeStruct((width // 2, count), jnp.float32)] * 2,
        in_specs=[pl.BlockSpec(memory_space=pltpu.SMEM), pl.BlockSpec(memory_space=pltpu.VMEM)],
        out_specs=[pl.BlockSpec(memory_space=pltpu.VMEM)] * 2,
        scratch_shapes=[
            pltpu.VMEM((blocks * deep * LANES, LANES), jnp.float32),
            pltpu.VMEM((count, LANES), jnp.float32),
        ],
        compiler_params=pltpu.CompilerParams(vmem_limit_bytes=VMEM),
    )(slots, table)


class Links:
    def __init__(self, nodes, ctrs):
        self.nodes, self.ctrs = nodes, ctrs
        self.node, self.ctr = lax.axis_index("node"), lax.axis_index("ctr")
        self.me = self.node * ctrs + self.ctr

    def on_node(self, hop):
        return (lax.rem(self.node + hop, self.nodes), self.ctr)

    def on_ctr(self, hop):
        return (self.node, lax.rem(self.ctr + hop, self.ctrs))

    def anyone(self, hop):
        other = lax.rem(self.me + hop, self.nodes * self.ctrs)
        return (other // self.ctrs, lax.rem(other, self.ctrs))

    def meet(self, targets):
        barrier = pltpu.get_barrier_semaphore()
        for target in targets:
            pl.semaphore_signal(barrier, inc=1, device_id=target, device_id_type=MESH)
        pl.semaphore_wait(barrier, len(targets))

    def node_hops(self):
        return range(1, self.nodes)

    def ctr_hops(self):
        return range(1, self.ctrs)

    def meet_sides(self):
        self.meet([self.on_node(h) for h in self.node_hops()] + [self.on_ctr(h) for h in self.ctr_hops()])

    def meet_all(self):
        self.meet([self.anyone(h) for h in range(1, self.nodes * self.ctrs)])


def send(source, target, sems, index, device):
    copy = pltpu.make_async_remote_copy(
        src_ref=source,
        dst_ref=target,
        send_sem=sems[0].at[index],
        recv_sem=sems[1].at[index],
        device_id=device,
        device_id_type=MESH,
    )
    copy.start()
    return copy


def finish(copies):
    for copy in copies:
        copy.wait()


def comm_call(body, nodes, ctrs, out_shape, scratch, collective, *args):
    return pl.pallas_call(
        functools.partial(body, nodes, ctrs),
        out_shape=out_shape,
        in_specs=[pl.BlockSpec(memory_space=pltpu.VMEM)] * len(args),
        out_specs=jax.tree.map(lambda _: pl.BlockSpec(memory_space=pltpu.VMEM), out_shape),
        scratch_shapes=scratch,
        compiler_params=pltpu.CompilerParams(
            collective_id=collective, has_side_effects=True, vmem_limit_bytes=VMEM
        ),
    )(*args)


def dma_pair(count):
    return [pltpu.SemaphoreType.DMA((count,))] * 2


TN = (((0,), (0,)), ((), ()))


def three_parts(tables):
    found = []
    for table in tables:
        a1 = rounded(table)
        a2 = rounded(table - a1)
        found += [a1, a2, table - a1 - a2]
    return jnp.concatenate(found, axis=1).astype(jnp.bfloat16)


def picked(parts, rows, lanes):
    high = lax.broadcasted_iota(jnp.int32, (parts.shape[0], rows.shape[1]), 0) == rows
    high = jnp.where(high, 1.0, 0.0).astype(jnp.bfloat16)
    low = lax.broadcasted_iota(jnp.int32, (LANES, rows.shape[1]), 0) == lanes
    both = lax.dot_general(parts, high, TN, preferred_element_type=jnp.float32)
    found = []
    for first in range(0, parts.shape[1], 3 * LANES):
        one, two, three = (both[first + i * LANES : first + (i + 1) * LANES] for i in range(3))
        found.append(jnp.sum(jnp.where(low, one + two + three, 0.0), axis=0, keepdims=True))
    return found


def spans(tiles):
    step = 2 - tiles % 2
    return [range(at, at + step) for at in range(0, tiles, step)]


def cell_keys(x, y, z):
    rows = x.shape[0]
    count = rows * LANES
    across = jnp.minimum((x * CELLS).astype(jnp.int32), CELLS - 1)
    along = jnp.minimum((y * CELLS).astype(jnp.int32), CELLS - 1)
    deep = jnp.minimum((z * DEPTH).astype(jnp.int32), DEPTH - 1)
    column = across * CELLS + jnp.where(across % 2 == 1, CELLS - 1 - along, along)
    deep = jnp.where(column % 2 == 1, DEPTH - 1 - deep, deep)
    index = lax.broadcasted_iota(jnp.int32, x.shape, 0) * LANES + lax.broadcasted_iota(jnp.int32, x.shape, 1)
    return ((column * DEPTH + deep) * count + index).astype(jnp.float32)


def sorted_keys(keys):
    rows = keys.shape[0]
    row = lax.broadcasted_iota(jnp.int32, keys.shape, 0)
    lane = lax.broadcasted_iota(jnp.int32, keys.shape, 1)
    bits = (rows * LANES).bit_length() - 1

    def bit(at):
        return (lane // 2**at) % 2 == 0 if at < 7 else (row // 2 ** (at - 7)) % 2 == 0

    zeros = [bit(at) for at in range(bits)]
    for level in range(1, bits + 1):
        for at in range(level - 1, -1, -1):
            axis, size, shift = (1, LANES, 2**at) if at < 7 else (0, rows, 2 ** (at - 7))
            other = jnp.where(
                zeros[at], pltpu.roll(keys, size - shift, axis), pltpu.roll(keys, shift, axis)
            )
            small = zeros[at] if level == bits else zeros[at] == zeros[level]
            keys = jnp.where(small, jnp.minimum(keys, other), jnp.maximum(keys, other))
    return keys


def setup_body(
    nodes, ctrs, own_ref, ids_ref, volume_ref, perm_ref, node_ref, ctr_ref, slab_ref,
    all_ref, mine_ref, plane_ref, table_ref, point_ref, *sems,
):
    links = Links(nodes, ctrs)
    links.meet_sides()
    mine = all_ref.at[links.ctr, links.node]
    copies = [send(own_ref, mine, sems[:2], h - 1, links.on_node(h)) for h in links.node_hops()]
    all_ref[links.ctr, links.node] = own_ref[...]
    keys = sorted_keys(cell_keys(*(volume_ref[k] for k in range(3))))
    slab_ref[...] = keys.astype(jnp.int32) % (keys.shape[0] * LANES)
    finish(copies)
    whole = all_ref.at[links.ctr]
    last = nodes - 1
    if ctrs == 4:
        far = lax.rem(links.ctr + 2, 4)
        near = (links.node, links.ctr + 1 - 2 * lax.rem(links.ctr, 2))
        across = send(whole, whole, sems[:2], last, (links.node, far))
        beside = send(whole, whole, sems[:2], last + 1, near)
        across.wait()
        other = all_ref.at[far]
        finish([send(other, other, sems[:2], last + 2, near), beside])
    else:
        finish([send(whole, whole, sems[:2], last - 1 + h, links.on_ctr(h)) for h in links.ctr_hops()])

    rows, tiles = own_ref.shape[1], mine_ref.shape[1]
    parts = three_parts([all_ref[:, :, k].reshape(-1, LANES) for k in range(3)])
    for span in spans(tiles):
        ids = jnp.concatenate([ids_ref[at : at + 1, :] for at in span], axis=1)
        device = ids // (rows * LANES)
        place = (device % ctrs * nodes + device // ctrs) * rows + ids // LANES % rows
        for k, value in enumerate(picked(parts, place, ids % LANES)):
            for i, at in enumerate(span):
                mine_ref[k, at : at + 1, :] = value[:, i * LANES : (i + 1) * LANES]
    copies = [
        send(mine_ref, plane_ref.at[links.node], sems[2:4], h - 1, links.on_node(h)) for h in links.node_hops()
    ]
    plane_ref[links.node] = mine_ref[...]
    finish(copies)

    for node in range(nodes):
        for k in range(3):
            table_ref[k, node * tiles : (node + 1) * tiles, :] = plane_ref[node, k]
    tables = [table_ref[k] for k in range(3)]
    count = tables[0].shape[0] * LANES
    keys = sorted_keys(cell_keys(*tables))
    perm_ref[...] = keys.astype(jnp.int32) % count
    blank = jnp.zeros((4, 2 * LANES), jnp.float32)
    parts = three_parts(tables)
    for span in spans(tiles):
        ids = jnp.concatenate([perm_ref[pl.ds(at * nodes + links.node, 1), :] for at in span], axis=1)
        found = [(v - 0.5) * (1.0 / RADIUS) for v in picked(parts, ids // LANES, ids % LANES)]
        wide = len(span) * LANES
        point_ref[:, span[0] * LANES : span[0] * LANES + wide] = jnp.concatenate(
            [blank[:, :wide]] + found + [jnp.ones((1, wide), jnp.float32)], axis=0
        )
    copies = [send(point_ref, node_ref.at[links.node], sems[4:6], h - 1, links.on_node(h)) for h in links.node_hops()]
    copies += [
        send(point_ref, ctr_ref.at[links.ctr], sems[4:6], nodes - 2 + h, links.on_ctr(h)) for h in links.ctr_hops()
    ]
    node_ref[links.node] = point_ref[...]
    ctr_ref[links.ctr] = point_ref[...]
    finish(copies)


def reduced(links, part_ref, landing, sems):
    copies = []
    for h in links.node_hops():
        device = links.on_node(h)
        copies.append(send(part_ref.at[device[0]], landing.at[h - 1], sems, h - 1, device))
    total = part_ref[links.node]
    for h, copy in zip(links.node_hops(), copies):
        copy.wait()
        total = total + landing[h - 1]
    return total


def wanted(rows, index):
    row = lax.broadcasted_iota(jnp.int32, (rows, LANES), 0)
    lane = lax.broadcasted_iota(jnp.int32, (rows, LANES), 1)
    return lane == row + 32 * index


def share_start(links, values, own, everyone, sems):
    line = 0.0
    for index, value in enumerate(values):
        column = jnp.sum(jnp.sum(value, axis=1), axis=1, keepdims=True)
        line += jnp.sum(
            jnp.where(wanted(column.shape[0], index), column, 0.0), axis=0, keepdims=True
        )
    own[...] = line
    hops = range(1, links.nodes * links.ctrs)
    copies = [send(own, everyone.at[links.me], sems, h - 1, links.anyone(h)) for h in hops]
    everyone[links.me] = own[...]
    return copies


def share_end(copies, count, rows, everyone):
    finish(copies)
    line = jnp.sum(everyone[...], axis=0)
    return [
        jnp.sum(jnp.where(wanted(rows, index), line, 0.0), axis=1, keepdims=True) for index in range(count)
    ]


def spread(column, ref):
    ref[...] = jnp.broadcast_to(column, ref.shape)
    return [ref[v : v + 1, :] for v in range(ref.shape[0])]


def pulled_body(nodes, ctrs, part_ref, own_ref, cols_ref, landing, s0, s1, t0, t1):
    links = Links(nodes, ctrs)
    links.meet_sides()
    own_ref[...] = reduced(links, part_ref, landing, (s0, s1))
    copies = [
        send(own_ref, cols_ref.at[links.ctr], (t0, t1), h - 1, links.on_ctr(h)) for h in links.ctr_hops()
    ]
    cols_ref[links.ctr] = own_ref[...]
    finish(copies)


def first_body(
    nodes, ctrs, part_ref, pulled_ref, pulled_cols, resid_ref, dir_cols, scal_ref,
    landing, image_ref, cols, line, every, scr0, scr1, s0, s1, t0, t1, u0, u1,
):
    links = Links(nodes, ctrs)
    links.meet_all()
    image = reduced(links, part_ref, landing, (s0, s1))
    image_ref[...] = image
    pulled = pulled_ref[...]
    told = share_start(
        links, [pulled * pulled, pulled * image, image * image], line, every, (t0, t1)
    )
    copies = [
        send(image_ref, cols.at[links.ctr], (u0, u1), h - 1, links.on_ctr(h)) for h in links.ctr_hops()
    ]
    cols[links.ctr] = image
    width = pulled_ref.shape[0]
    norm, curve, square = share_end(told, 3, width, every)
    alpha = norm / curve
    ratio = alpha * square / curve - 1.0
    alphas, ratios = spread(alpha, scr0), spread(ratio, scr1)
    scal_ref[0] = scr0[...]
    scal_ref[1] = scr1[...]
    for v in range(width):
        resid_ref[v] = pulled_ref[v] - alphas[v] * image_ref[v]
    finish(copies)
    for c in range(ctrs):
        for v in range(width):
            dir_cols[c, v] = (pulled_cols[c, v] - alphas[v] * cols[c, v]) + ratios[v] * pulled_cols[c, v]


def second_body(
    nodes, ctrs, part_ref, pulled_ref, resid_ref, scal_ref, out_ref,
    landing, final, line, every, scr0, s0, s1, t0, t1, u0, u1,
):
    links = Links(nodes, ctrs)
    links.meet_all()
    image = reduced(links, part_ref, landing, (s0, s1))
    width = pulled_ref.shape[0]
    alphas = [scal_ref[0, v : v + 1, :] for v in range(width)]
    ratios = [scal_ref[1, v : v + 1, :] for v in range(width)]
    for v in range(width):
        final[v] = resid_ref[v] + ratios[v] * pulled_ref[v]
    resid = resid_ref[...]
    told = share_start(links, [resid * resid, final[:width] * image], line, every, (t0, t1))
    final[width:] = image
    norm, curve = share_end(told, 2, width, every)
    seconds = spread(norm / curve, scr0)
    for v in range(width):
        final[v] = alphas[v] * pulled_ref[v] + seconds[v] * final[v]
        final[width + v] = resid_ref[v] - seconds[v] * final[width + v]
    out_ref[links.node] = final[...]
    if nodes % 2:
        mine = out_ref.at[links.node]
        finish([send(final, mine, (u0, u1), h - 1, links.on_node(h)) for h in links.node_hops()])
        return
    beside = (links.node + 1 - 2 * lax.rem(links.node, 2), links.ctr)
    half = nodes // 2
    size = 2 * width // PIECES
    copies, relays = [], []
    for piece in range(PIECES):
        base, rows = piece * (nodes - 1), pl.ds(piece * size, size)
        mine, target = final.at[rows], out_ref.at[links.node, rows]
        copies.append([send(mine, target, (u0, u1), base + h, links.on_node(2 * h)) for h in range(1, half)])
        relays.append(send(mine, target, (u0, u1), base, beside))
    for piece in range(PIECES):
        base, rows = piece * (nodes - 1), pl.ds(piece * size, size)
        for h, copy in zip(range(1, half), copies[piece]):
            copy.wait()
            came = out_ref.at[lax.rem(links.node + nodes - 2 * h, nodes), rows]
            relays.append(send(came, came, (u0, u1), base + half - 1 + h, beside))
    finish(relays)


def local(nodes, ctrs, surface_xyz, centre_idx, volume_xyz, slab_ids, cotangent):
    width = cotangent.shape[0]
    owned = centre_idx.shape[0]
    total = owned * nodes
    here = lax.axis_index("node")
    f32 = jnp.float32
    vmem = lambda *shape: pltpu.VMEM(shape, f32)
    out = lambda *shape: jax.ShapeDtypeStruct(shape, f32)
    devices = nodes * ctrs

    slab = slab_ids % volume_xyz.shape[1]
    volume_points = jnp.concatenate(
        [scaled(volume_xyz), jnp.zeros((4, volume_xyz.shape[1]), f32)], axis=0
    )
    volume_points = jnp.concatenate([volume_points[4:], volume_points[:4]], axis=0)

    rows = surface_xyz.shape[1] // LANES
    tiles = owned // LANES
    perm, row_points, col_points, node_perm = comm_call(
        setup_body, nodes, ctrs,
        (
            jax.ShapeDtypeStruct((total // LANES, LANES), jnp.int32), out(nodes, 8, owned), out(ctrs, 8, owned),
            jax.ShapeDtypeStruct((volume_xyz.shape[1] // LANES, LANES), jnp.int32),
        ),
        [
            vmem(ctrs, nodes, 3, rows, LANES), vmem(3, tiles, LANES), vmem(nodes, 3, tiles, LANES),
            vmem(3, total // LANES, LANES), vmem(8, owned),
        ] + dma_pair(nodes + ctrs - 2) + dma_pair(nodes - 1) + dma_pair(nodes + ctrs - 2),
        0, surface_xyz.reshape(3, rows, LANES), centre_idx.reshape(tiles, LANES),
        volume_xyz.reshape(3, -1, LANES),
    )
    by_owner = perm.reshape(tiles, nodes, LANES)
    node_points, node_vec = node_rows(slab, node_perm.reshape(-1), volume_points, cotangent)
    left, col_right, node_right = factors(row_points, col_points, node_points)
    flat = lambda value: value.transpose(1, 0, 2).reshape(8, -1)[4:]
    groups = boxes(flat(row_points), GROUP)
    node_lists = near_lists(boxes(flat(node_points), LANES // 2), groups, 2)
    col_lists = near_lists(boxes(flat(col_points), LANES), groups, 1)

    places = jnp.arange(total, dtype=jnp.int32)
    hit = (by_owner.transpose(1, 0, 2).reshape(total) // LANES)[None, :] == (
        here * tiles + jnp.arange(tiles, dtype=jnp.int32)
    )[:, None]
    spots = jnp.concatenate(
        [jnp.where(hit, (places // LANES)[None, :], 0), jnp.where(hit, (places % LANES)[None, :], 0)], axis=0
    ).astype(jnp.bfloat16)
    lane = (
        by_owner.transpose(1, 0, 2).reshape(total)[:, None] % LANES == jnp.arange(LANES, dtype=jnp.int32)[None, :]
    ).astype(jnp.bfloat16)
    spots = jnp.dot(spots, lane, preferred_element_type=f32).astype(jnp.int32)
    slots = (spots[:tiles] * LANES + spots[tiles:]).reshape(owned)

    own_shape, scr = out(width, tiles, LANES), vmem(width, LANES)
    cols_shape = out(ctrs, width, tiles, LANES)
    landing = vmem(nodes - 1, width, tiles, LANES)
    line, every = vmem(1, LANES), vmem(devices, 1, LANES)
    part = apply_kernel(node_lists, left, node_right, node_vec, nodes)
    pulled, pulled_cols = comm_call(
        pulled_body, nodes, ctrs, (own_shape, cols_shape),
        [landing] + dma_pair(nodes - 1) + dma_pair(ctrs - 1), 3, part,
    )
    part = apply_kernel(col_lists, left, col_right, pulled_cols, nodes)
    resid, dir_cols, scal = comm_call(
        first_body, nodes, ctrs, (own_shape, cols_shape, out(2, width, LANES)),
        [landing, vmem(width, tiles, LANES), vmem(ctrs, width, tiles, LANES), line, every, scr, scr]
        + dma_pair(nodes - 1) + dma_pair(devices - 1) + dma_pair(ctrs - 1),
        4, part, pulled, pulled_cols,
    )
    part = apply_kernel(col_lists, left, col_right, dir_cols, nodes)
    final = comm_call(
        second_body, nodes, ctrs, out(nodes, 2 * width, tiles, LANES),
        [landing, vmem(2 * width, tiles, LANES), line, every, scr]
        + dma_pair(nodes - 1) + dma_pair(devices - 1) + dma_pair(PIECES * (nodes - 1)),
        5, part, pulled, resid, scal,
    )
    return tuple(pick(slots, final))


def solution(mesh):
    return jax.shard_map(
        functools.partial(local, mesh.shape["node"], mesh.shape["ctr"]),
        mesh=mesh,
        in_specs=(
            P(None, ("node", "ctr")),
            P(("node", "ctr")),
            P(None, "node"),
            P("node"),
            P(None, "node"),
        ),
        out_specs=(P(None, ("node", "ctr")), P(None, ("node", "ctr"))),
        check_vma=False,
    )
```

```python
import functools
import math

import jax
import jax.numpy as jnp
from jax import lax
from jax.experimental import pallas as pl
from jax.experimental.pallas import tpu as pltpu
from jax.sharding import PartitionSpec as P

RADIUS = 0.2
LANES = 128
GROUP = 32
BATCH = 4
PAIR = 4
CELLS = 5
DEPTH = 64
PAD = 16
PIECES = 3
VMEM = 50 * 1024 * 1024
NT = (((1,), (1,)), ((), ()))
MESH = pl.DeviceIdType.MESH


def scaled(xyz):
    point = (xyz - 0.5) * (1.0 / RADIUS)
    return jnp.concatenate([point, jnp.ones((1, xyz.shape[1]), jnp.float32)], axis=0)


def rounded(value):
    return value.astype(jnp.bfloat16).astype(jnp.float32)


def right_factor(group):
    row = lax.broadcasted_iota(jnp.int32, group.shape, 0)
    place = jnp.where(row >= 4, group, 0.0)
    square = jnp.sum(jnp.where(row < 7, place * place, 0.0), axis=0, keepdims=True)
    beta = jnp.where(row == 0, square, place)
    b1 = rounded(beta)
    rest = beta - b1
    b2 = rounded(rest)
    b3 = rest - b2
    return jnp.concatenate([b1, b2, b1, b2, b3, b1], axis=0).astype(jnp.bfloat16)


def two_parts(vectors):
    v1 = rounded(vectors)
    return jnp.concatenate([v1, vectors - v1], axis=0).astype(jnp.bfloat16)


def boxes(points, size):
    tiles = points[:3].reshape(3, -1, size)
    return jnp.min(tiles, axis=2), jnp.max(tiles, axis=2)


def near_lists(tiles, groups, pieces):
    gap = jnp.maximum(
        jnp.maximum(tiles[0][:, :, None] - groups[1][:, None, :], groups[0][:, None, :] - tiles[1][:, :, None]),
        0.0,
    )
    near = jnp.sum(gap * gap, axis=0) < 1.0 + 1e-4
    size = near.shape[1]
    near = jnp.any(near.reshape(-1, pieces, size), axis=1)
    total = near.shape[0]
    count = jnp.sum(near.astype(jnp.int32), axis=1)
    upto = (jnp.arange(size)[:, None] <= jnp.arange(size)[None, :]).astype(jnp.bfloat16)
    seen = jnp.dot(near.astype(jnp.bfloat16), upto, preferred_element_type=jnp.float32).astype(jnp.int32)
    every = jnp.arange(size, dtype=jnp.int32)
    place = jnp.where(near, seen - 1, count[:, None] + every[None, :] - seen)
    order = jnp.sum(
        jnp.where(place[:, :, None] == every[None, None, :], every[None, :, None], 0), axis=1
    )
    batches = (count + BATCH - 1) // BATCH
    ranks = jnp.arange(total)
    ends = jnp.sum(jnp.where(ranks[:, None] <= ranks[None, :], batches[:, None], 0), axis=0)
    at = jnp.arange(total * size // BATCH + 8 * PAIR, dtype=jnp.int32) - 2 * PAIR
    passed = ends[:, None] <= at[None, :]
    tile = jnp.sum(passed.astype(jnp.int32), axis=0)
    start = jnp.sum(jnp.where(passed, batches[:, None], 0), axis=0)
    code = tile * size + (at - start) * BATCH
    items = jnp.where((at < 0) | (tile == total), total * size, code)
    return jnp.sum(batches, keepdims=True), items, jnp.pad((order * GROUP).reshape(-1), (0, size))


def apply_body(count, items, order, left_ref, right_ref, vec_ref, out_ref, acc, vec, q0, q1, k0, k1):
    rows = left_ref.shape[0]
    tiles = right_ref.shape[0]
    span = GROUP * BATCH
    half = span // 2
    banks, width, deep = vec_ref.shape[:3]
    acc[...] = jnp.zeros_like(acc)
    for ref in (q0, q1, k0, k1):
        ref[...] = jnp.zeros_like(ref)

    blank = jnp.zeros((PAD - width, LANES), jnp.float32)
    for bank in range(banks):
        for at in range(deep):
            parts = two_parts(jnp.concatenate([vec_ref[bank, :, at, :], blank], axis=0))
            vec[bank * deep + at] = jnp.concatenate([parts, parts], axis=1)
    vec[tiles] = jnp.zeros_like(vec[tiles])

    groups = rows // GROUP
    first_half = lax.broadcasted_iota(jnp.int32, (half, LANES), 1) < LANES // 2

    def item(index):
        code = items[index]
        tile = lax.div(code, groups)
        return tile, jnp.minimum(tile, tiles - 1), [
            pl.multiple_of(order[code + i], GROUP) for i in range(BATCH)
        ]

    def rows_at(places):
        return jnp.concatenate([left_ref[pl.ds(place, GROUP), :] for place in places], axis=0)

    def step(index, q_in, q_out, k_in, k_out):
        for unit in range(PAIR):
            tile, _, places = item(index * PAIR + unit)
            part = lax.dot_general(
                k_in[pl.ds(unit * span, span), :], vec[tile], NT, preferred_element_type=jnp.float32
            )
            for j, place in enumerate(places):
                acc[pl.ds(place, GROUP), :] += part[j * GROUP : (j + 1) * GROUP]
        for unit in range(PAIR):
            q = jnp.minimum(jnp.maximum(q_in[pl.ds(unit * half, half), :], 1e-30), 1.0)
            s = q * lax.rsqrt(q)
            w = 1.0 - s
            w2 = w * w
            k = (w2 * w2) * (0.25 + s)
            hi = k.astype(jnp.bfloat16)
            lo = (k - hi.astype(jnp.float32)).astype(jnp.bfloat16)
            for side in range(2):
                here = pl.ds(unit * span + side * half, half)
                lanes = slice(side * LANES, (side + 1) * LANES)
                k_out[here, :LANES] = hi[:, lanes]
                k_out[here, LANES:] = lo[:, lanes]
        for unit in range(PAIR):
            _, listed, places = item((index + 2) * PAIR + unit)
            left = jnp.where(first_half, rows_at(places[: BATCH // 2]), rows_at(places[BATCH // 2 :]))
            q_out[pl.ds(unit * half, half), :] = jnp.dot(
                left, right_ref[listed], preferred_element_type=jnp.float32
            )

    def two_steps(index, _):
        step(2 * index, q0, q1, k0, k1)
        step(2 * index + 1, q1, q0, k1, k0)
        return 0

    steps = (count[0] + PAIR - 1) // PAIR + 2
    lax.fori_loop(0, (steps + 1) // 2, two_steps, 0)

    owners, _, high, _ = out_ref.shape
    for owner in range(owners):
        for at in range(high):
            total = acc[pl.ds((owner * high + at) * LANES, LANES), :].T
            out_ref[owner, :, at, :] = 4.0 * (total[:width] + total[PAD : PAD + width])


def apply_kernel(lists, left, right, vec, owners):
    rows = left.shape[0]
    tiles = right.shape[0]
    width = vec.shape[1]
    wide = PAIR * GROUP * BATCH
    return pl.pallas_call(
        apply_body,
        out_shape=jax.ShapeDtypeStruct((owners, width, rows // owners // LANES, LANES), jnp.float32),
        in_specs=[pl.BlockSpec(memory_space=pltpu.SMEM)] * 3 + [pl.BlockSpec(memory_space=pltpu.VMEM)] * 3,
        out_specs=pl.BlockSpec(memory_space=pltpu.VMEM),
        scratch_shapes=[
            pltpu.VMEM((rows, 2 * PAD), jnp.float32),
            pltpu.VMEM((tiles + 1, 2 * PAD, 2 * LANES), jnp.bfloat16),
            pltpu.VMEM((wide // 2, 2 * LANES), jnp.float32),
            pltpu.VMEM((wide // 2, 2 * LANES), jnp.float32),
            pltpu.VMEM((wide, 2 * LANES), jnp.bfloat16),
            pltpu.VMEM((wide, 2 * LANES), jnp.bfloat16),
        ],
        compiler_params=pltpu.CompilerParams(vmem_limit_bytes=VMEM),
    )(*lists, left, right, vec)


def factor_body(row_ref, col_ref, node_ref, left_ref, col_out, node_out):
    blocks, _, span = row_ref.shape
    blank = jnp.zeros((16, LANES), jnp.float32)
    for block in range(blocks):
        for at in range(span // LANES):
            group = row_ref[block, :, pl.ds(at * LANES, LANES)]
            row = lax.broadcasted_iota(jnp.int32, group.shape, 0)
            place = jnp.where((row >= 4) & (row < 7), group, 0.0)
            square = jnp.sum(place * place, axis=0, keepdims=True)
            alpha = jnp.where(row == 0, 1.0, jnp.where(row == 7, square, -2.0 * place))
            a1 = rounded(alpha)
            a2 = rounded(alpha - a1)
            a3 = alpha - a1 - a2
            parts = [a1, a1, a2, a2, a1, a3, blank]
            left_ref[pl.ds((block * (span // LANES) + at) * LANES, LANES), :] = (
                jnp.concatenate(parts + parts, axis=0).T.astype(jnp.bfloat16)
            )

    def fill(source, target):
        blocks, _, span = source.shape
        per = span // LANES
        zero = jnp.zeros((64, LANES), jnp.bfloat16)
        pad = jnp.zeros((16, LANES), jnp.bfloat16)
        for block in range(blocks):
            for at in range(per):
                right = jnp.concatenate([right_factor(source[block, :, pl.ds(at * LANES, LANES)]), pad], axis=0)
                target[block * per + at] = jnp.concatenate(
                    [jnp.concatenate([right, zero], axis=0), jnp.concatenate([zero, right], axis=0)], axis=1
                )

    fill(col_ref, col_out)
    fill(node_ref, node_out)


def factors(row_points, col_points, node_points):
    def tiles(points):
        return points.shape[0] * points.shape[2] // LANES

    def shape(points):
        return jax.ShapeDtypeStruct((tiles(points), LANES, 2 * LANES), jnp.bfloat16)

    return pl.pallas_call(
        factor_body,
        out_shape=[
            jax.ShapeDtypeStruct((tiles(row_points) * LANES, LANES), jnp.bfloat16),
            shape(col_points),
            shape(node_points),
        ],
        in_specs=[pl.BlockSpec(memory_space=pltpu.VMEM)] * 3,
        out_specs=[pl.BlockSpec(memory_space=pltpu.VMEM)] * 3,
        compiler_params=pltpu.CompilerParams(vmem_limit_bytes=VMEM),
    )(row_points, col_points, node_points)


def node_rows_body(slab_ref, perm_ref, xyz_ref, cot_ref, xyz_out, cot_out, rows_a, rows_b, rows_c):
    count = cot_ref.shape[1]
    width = cot_ref.shape[0]
    blank = jnp.zeros((PAD - width, LANES), jnp.float32)
    for tile in range(count // LANES):
        here = pl.ds(tile * LANES, LANES)
        rows_a[here, :PAD] = jnp.concatenate([cot_ref[:, here], blank], axis=0).T

    def scatter(index, _):
        base = pl.multiple_of(index * 64, 64)
        for i in range(64):
            rows_b[pl.ds(slab_ref[base + i], 1), :] = rows_a[pl.ds(base + i, 1), :]
        return 0

    lax.fori_loop(0, count // 64, scatter, 0)
    for tile in range(count // LANES):
        here = pl.ds(tile * LANES, LANES)
        rows_b[here, PAD : PAD + 8] = xyz_ref[:, here].T

    def gather(index, _):
        base = pl.multiple_of(index * 64, 64)
        for i in range(64):
            rows_c[pl.ds(base + i, 1), :] = rows_b[pl.ds(perm_ref[base + i], 1), :]
        return 0

    lax.fori_loop(0, count // 64, gather, 0)
    for tile in range(count // LANES):
        here = rows_c[pl.ds(tile * LANES, LANES), : PAD + 8].T
        cot_out[0, :, tile, :] = here[:width]
        xyz_out[0, :, pl.ds(tile * LANES, LANES)] = here[PAD : PAD + 8]


def node_rows(slab, perm, xyz, cotangent):
    count = cotangent.shape[1]
    width = cotangent.shape[0]
    tiles = count // LANES
    return pl.pallas_call(
        node_rows_body,
        out_shape=[
            jax.ShapeDtypeStruct((1, 8, count), jnp.float32),
            jax.ShapeDtypeStruct((1, width, tiles, LANES), jnp.float32),
        ],
        in_specs=[pl.BlockSpec(memory_space=pltpu.SMEM)] * 2 + [pl.BlockSpec(memory_space=pltpu.VMEM)] * 2,
        out_specs=[pl.BlockSpec(memory_space=pltpu.VMEM)] * 2,
        scratch_shapes=[pltpu.VMEM((count, LANES), jnp.float32)] * 3,
        compiler_params=pltpu.CompilerParams(vmem_limit_bytes=VMEM),
    )(slab, perm, xyz, cotangent)


def pick_body(slot_ref, table_ref, sol_ref, res_ref, rows_a, rows_b):
    blocks, width, deep, _ = table_ref.shape
    count = sol_ref.shape[1]
    half = width // 2
    for block in range(blocks):
        for tile in range(deep):
            rows_a[pl.ds((block * deep + tile) * LANES, LANES), :width] = table_ref[block, :, tile, :].T

    def gather(index, _):
        base = pl.multiple_of(index * 64, 64)
        for i in range(64):
            rows_b[pl.ds(base + i, 1), :] = rows_a[pl.ds(slot_ref[base + i], 1), :]
        return 0

    lax.fori_loop(0, count // 64, gather, 0)
    for tile in range(count // LANES):
        here = pl.ds(tile * LANES, LANES)
        values = rows_b[here, :width].T
        sol_ref[:, here] = values[:half]
        res_ref[:, here] = values[half:width]


def pick(slots, table):
    blocks, width, deep, _ = table.shape
    count = slots.shape[0]
    return pl.pallas_call(
        pick_body,
        out_shape=[jax.ShapeDtypeStruct((width // 2, count), jnp.float32)] * 2,
        in_specs=[pl.BlockSpec(memory_space=pltpu.SMEM), pl.BlockSpec(memory_space=pltpu.VMEM)],
        out_specs=[pl.BlockSpec(memory_space=pltpu.VMEM)] * 2,
        scratch_shapes=[
            pltpu.VMEM((blocks * deep * LANES, LANES), jnp.float32),
            pltpu.VMEM((count, LANES), jnp.float32),
        ],
        compiler_params=pltpu.CompilerParams(vmem_limit_bytes=VMEM),
    )(slots, table)


class Links:
    def __init__(self, nodes, ctrs):
        self.nodes, self.ctrs = nodes, ctrs
        self.node, self.ctr = lax.axis_index("node"), lax.axis_index("ctr")
        self.me = self.node * ctrs + self.ctr

    def on_node(self, hop):
        return (lax.rem(self.node + hop, self.nodes), self.ctr)

    def on_ctr(self, hop):
        return (self.node, lax.rem(self.ctr + hop, self.ctrs))

    def anyone(self, hop):
        other = lax.rem(self.me + hop, self.nodes * self.ctrs)
        return (other // self.ctrs, lax.rem(other, self.ctrs))

    def meet(self, targets):
        barrier = pltpu.get_barrier_semaphore()
        for target in targets:
            pl.semaphore_signal(barrier, inc=1, device_id=target, device_id_type=MESH)
        pl.semaphore_wait(barrier, len(targets))

    def node_hops(self):
        return range(1, self.nodes)

    def ctr_hops(self):
        return range(1, self.ctrs)

    def meet_sides(self):
        self.meet([self.on_node(h) for h in self.node_hops()] + [self.on_ctr(h) for h in self.ctr_hops()])

    def meet_all(self):
        self.meet([self.anyone(h) for h in range(1, self.nodes * self.ctrs)])


def send(source, target, sems, index, device):
    copy = pltpu.make_async_remote_copy(
        src_ref=source,
        dst_ref=target,
        send_sem=sems[0].at[index],
        recv_sem=sems[1].at[index],
        device_id=device,
        device_id_type=MESH,
    )
    copy.start()
    return copy


def finish(copies):
    for copy in copies:
        copy.wait()


def comm_call(body, nodes, ctrs, out_shape, scratch, collective, *args):
    return pl.pallas_call(
        functools.partial(body, nodes, ctrs),
        out_shape=out_shape,
        in_specs=[pl.BlockSpec(memory_space=pltpu.VMEM)] * len(args),
        out_specs=jax.tree.map(lambda _: pl.BlockSpec(memory_space=pltpu.VMEM), out_shape),
        scratch_shapes=scratch,
        compiler_params=pltpu.CompilerParams(
            collective_id=collective, has_side_effects=True, vmem_limit_bytes=VMEM
        ),
    )(*args)


def dma_pair(count):
    return [pltpu.SemaphoreType.DMA((count,))] * 2


TN = (((0,), (0,)), ((), ()))


def three_parts(tables):
    found = []
    for table in tables:
        a1 = rounded(table)
        a2 = rounded(table - a1)
        found += [a1, a2, table - a1 - a2]
    return jnp.concatenate(found, axis=1).astype(jnp.bfloat16)


def picked(parts, rows, lanes):
    high = lax.broadcasted_iota(jnp.int32, (parts.shape[0], rows.shape[1]), 0) == rows
    high = jnp.where(high, 1.0, 0.0).astype(jnp.bfloat16)
    low = lax.broadcasted_iota(jnp.int32, (LANES, rows.shape[1]), 0) == lanes
    both = lax.dot_general(parts, high, TN, preferred_element_type=jnp.float32)
    found = []
    for first in range(0, parts.shape[1], 3 * LANES):
        one, two, three = (both[first + i * LANES : first + (i + 1) * LANES] for i in range(3))
        found.append(jnp.sum(jnp.where(low, one + two + three, 0.0), axis=0, keepdims=True))
    return found


def in_rows(flat, tiled):
    for at in range(tiled.shape[1]):
        here = flat[:, at * LANES : (at + 1) * LANES]
        for k in range(3):
            tiled[k, at : at + 1, :] = here[k : k + 1]


def spans(tiles):
    step = 2 - tiles % 2
    return [range(at, at + step) for at in range(0, tiles, step)]


def cell_keys(x, y, z):
    rows = x.shape[0]
    count = rows * LANES
    across = jnp.minimum((x * CELLS).astype(jnp.int32), CELLS - 1)
    along = jnp.minimum((y * CELLS).astype(jnp.int32), CELLS - 1)
    deep = jnp.minimum((z * DEPTH).astype(jnp.int32), DEPTH - 1)
    column = across * CELLS + jnp.where(across % 2 == 1, CELLS - 1 - along, along)
    deep = jnp.where(column % 2 == 1, DEPTH - 1 - deep, deep)
    index = lax.broadcasted_iota(jnp.int32, x.shape, 0) * LANES + lax.broadcasted_iota(jnp.int32, x.shape, 1)
    return ((column * DEPTH + deep) * count + index).astype(jnp.float32)


def sorted_keys(keys):
    rows = keys.shape[0]
    row = lax.broadcasted_iota(jnp.int32, keys.shape, 0)
    lane = lax.broadcasted_iota(jnp.int32, keys.shape, 1)
    bits = (rows * LANES).bit_length() - 1

    def bit(at):
        return (lane // 2**at) % 2 == 0 if at < 7 else (row // 2 ** (at - 7)) % 2 == 0

    zeros = [bit(at) for at in range(bits)]
    for level in range(1, bits + 1):
        for at in range(level - 1, -1, -1):
            axis, size, shift = (1, LANES, 2**at) if at < 7 else (0, rows, 2 ** (at - 7))
            other = jnp.where(
                zeros[at], pltpu.roll(keys, size - shift, axis), pltpu.roll(keys, shift, axis)
            )
            small = zeros[at] if level == bits else zeros[at] == zeros[level]
            keys = jnp.where(small, jnp.minimum(keys, other), jnp.maximum(keys, other))
    return keys


def setup_body(
    nodes, ctrs, surface_ref, ids_ref, volume_flat, perm_ref, node_ref, ctr_ref, slab_ref,
    own_ref, volume_ref, all_ref, mine_ref, plane_ref, table_ref, point_ref, *sems,
):
    links = Links(nodes, ctrs)
    in_rows(surface_ref, own_ref)
    links.meet_sides()
    mine = all_ref.at[links.ctr, links.node]
    copies = [send(own_ref, mine, sems[:2], h - 1, links.on_node(h)) for h in links.node_hops()]
    all_ref[links.ctr, links.node] = own_ref[...]
    in_rows(volume_flat, volume_ref)
    keys = sorted_keys(cell_keys(*(volume_ref[k] for k in range(3))))
    slab_ref[...] = keys.astype(jnp.int32) % (keys.shape[0] * LANES)
    finish(copies)
    whole = all_ref.at[links.ctr]
    last = nodes - 1
    if ctrs == 4:
        far = lax.rem(links.ctr + 2, 4)
        near = (links.node, links.ctr + 1 - 2 * lax.rem(links.ctr, 2))
        across = send(whole, whole, sems[:2], last, (links.node, far))
        beside = send(whole, whole, sems[:2], last + 1, near)
        across.wait()
        other = all_ref.at[far]
        finish([send(other, other, sems[:2], last + 2, near), beside])
    else:
        finish([send(whole, whole, sems[:2], last - 1 + h, links.on_ctr(h)) for h in links.ctr_hops()])

    rows, tiles = own_ref.shape[1], mine_ref.shape[1]
    parts = three_parts([all_ref[:, :, k].reshape(-1, LANES) for k in range(3)])
    for span in spans(tiles):
        ids = jnp.concatenate([ids_ref[at : at + 1, :] for at in span], axis=1)
        device = ids // (rows * LANES)
        place = (device % ctrs * nodes + device // ctrs) * rows + ids // LANES % rows
        for k, value in enumerate(picked(parts, place, ids % LANES)):
            for i, at in enumerate(span):
                mine_ref[k, at : at + 1, :] = value[:, i * LANES : (i + 1) * LANES]
    copies = [
        send(mine_ref, plane_ref.at[links.node], sems[2:4], h - 1, links.on_node(h)) for h in links.node_hops()
    ]
    plane_ref[links.node] = mine_ref[...]
    finish(copies)

    for node in range(nodes):
        for k in range(3):
            table_ref[k, node * tiles : (node + 1) * tiles, :] = plane_ref[node, k]
    tables = [table_ref[k] for k in range(3)]
    count = tables[0].shape[0] * LANES
    keys = sorted_keys(cell_keys(*tables))
    perm_ref[...] = keys.astype(jnp.int32) % count
    blank = jnp.zeros((4, 2 * LANES), jnp.float32)
    parts = three_parts(tables)
    for span in spans(tiles):
        ids = jnp.concatenate([perm_ref[pl.ds(at * nodes + links.node, 1), :] for at in span], axis=1)
        found = [(v - 0.5) * (1.0 / RADIUS) for v in picked(parts, ids // LANES, ids % LANES)]
        wide = len(span) * LANES
        point_ref[:, span[0] * LANES : span[0] * LANES + wide] = jnp.concatenate(
            [blank[:, :wide]] + found + [jnp.ones((1, wide), jnp.float32)], axis=0
        )
    copies = [send(point_ref, node_ref.at[links.node], sems[4:6], h - 1, links.on_node(h)) for h in links.node_hops()]
    copies += [
        send(point_ref, ctr_ref.at[links.ctr], sems[4:6], nodes - 2 + h, links.on_ctr(h)) for h in links.ctr_hops()
    ]
    node_ref[links.node] = point_ref[...]
    ctr_ref[links.ctr] = point_ref[...]
    finish(copies)


def reduced(links, part_ref, landing, sems):
    copies = []
    for h in links.node_hops():
        device = links.on_node(h)
        copies.append(send(part_ref.at[device[0]], landing.at[h - 1], sems, h - 1, device))
    total = part_ref[links.node]
    for h, copy in zip(links.node_hops(), copies):
        copy.wait()
        total = total + landing[h - 1]
    return total


def wanted(rows, index):
    row = lax.broadcasted_iota(jnp.int32, (rows, LANES), 0)
    lane = lax.broadcasted_iota(jnp.int32, (rows, LANES), 1)
    return lane == row + 32 * index


def share_start(links, values, own, everyone, sems):
    line = 0.0
    for index, value in enumerate(values):
        column = jnp.sum(jnp.sum(value, axis=1), axis=1, keepdims=True)
        line += jnp.sum(
            jnp.where(wanted(column.shape[0], index), column, 0.0), axis=0, keepdims=True
        )
    own[...] = line
    hops = range(1, links.nodes * links.ctrs)
    copies = [send(own, everyone.at[links.me], sems, h - 1, links.anyone(h)) for h in hops]
    everyone[links.me] = own[...]
    return copies


def share_end(copies, count, rows, everyone):
    finish(copies)
    line = jnp.sum(everyone[...], axis=0)
    return [
        jnp.sum(jnp.where(wanted(rows, index), line, 0.0), axis=1, keepdims=True) for index in range(count)
    ]


def spread(column, ref):
    ref[...] = jnp.broadcast_to(column, ref.shape)
    return [ref[v : v + 1, :] for v in range(ref.shape[0])]


def pulled_body(nodes, ctrs, part_ref, own_ref, cols_ref, landing, s0, s1, t0, t1):
    links = Links(nodes, ctrs)
    links.meet_sides()
    own_ref[...] = reduced(links, part_ref, landing, (s0, s1))
    copies = [
        send(own_ref, cols_ref.at[links.ctr], (t0, t1), h - 1, links.on_ctr(h)) for h in links.ctr_hops()
    ]
    cols_ref[links.ctr] = own_ref[...]
    finish(copies)


def first_body(
    nodes, ctrs, part_ref, pulled_ref, pulled_cols, resid_ref, dir_cols, scal_ref,
    landing, image_ref, cols, line, every, scr0, scr1, s0, s1, t0, t1, u0, u1,
):
    links = Links(nodes, ctrs)
    links.meet_all()
    image = reduced(links, part_ref, landing, (s0, s1))
    image_ref[...] = image
    pulled = pulled_ref[...]
    told = share_start(
        links, [pulled * pulled, pulled * image, image * image], line, every, (t0, t1)
    )
    copies = [
        send(image_ref, cols.at[links.ctr], (u0, u1), h - 1, links.on_ctr(h)) for h in links.ctr_hops()
    ]
    cols[links.ctr] = image
    width = pulled_ref.shape[0]
    norm, curve, square = share_end(told, 3, width, every)
    alpha = norm / curve
    ratio = alpha * square / curve - 1.0
    alphas, ratios = spread(alpha, scr0), spread(ratio, scr1)
    scal_ref[0] = scr0[...]
    scal_ref[1] = scr1[...]
    for v in range(width):
        resid_ref[v] = pulled_ref[v] - alphas[v] * image_ref[v]
    finish(copies)
    for c in range(ctrs):
        for v in range(width):
            dir_cols[c, v] = (pulled_cols[c, v] - alphas[v] * cols[c, v]) + ratios[v] * pulled_cols[c, v]


def second_body(
    nodes, ctrs, part_ref, pulled_ref, resid_ref, scal_ref, out_ref,
    landing, final, line, every, scr0, s0, s1, t0, t1, u0, u1,
):
    links = Links(nodes, ctrs)
    links.meet_all()
    image = reduced(links, part_ref, landing, (s0, s1))
    width = pulled_ref.shape[0]
    alphas = [scal_ref[0, v : v + 1, :] for v in range(width)]
    ratios = [scal_ref[1, v : v + 1, :] for v in range(width)]
    for v in range(width):
        final[v] = resid_ref[v] + ratios[v] * pulled_ref[v]
    resid = resid_ref[...]
    told = share_start(links, [resid * resid, final[:width] * image], line, every, (t0, t1))
    final[width:] = image
    norm, curve = share_end(told, 2, width, every)
    seconds = spread(norm / curve, scr0)
    for v in range(width):
        final[v] = alphas[v] * pulled_ref[v] + seconds[v] * final[v]
        final[width + v] = resid_ref[v] - seconds[v] * final[width + v]
    out_ref[links.node] = final[...]
    if nodes % 2:
        mine = out_ref.at[links.node]
        finish([send(final, mine, (u0, u1), h - 1, links.on_node(h)) for h in links.node_hops()])
        return
    beside = (links.node + 1 - 2 * lax.rem(links.node, 2), links.ctr)
    half = nodes // 2
    size = 2 * width // PIECES
    copies, relays = [], []
    for piece in range(PIECES):
        base, rows = piece * (nodes - 1), pl.ds(piece * size, size)
        mine, target = final.at[rows], out_ref.at[links.node, rows]
        copies.append([send(mine, target, (u0, u1), base + h, links.on_node(2 * h)) for h in range(1, half)])
        relays.append(send(mine, target, (u0, u1), base, beside))
    for piece in range(PIECES):
        base, rows = piece * (nodes - 1), pl.ds(piece * size, size)
        for h, copy in zip(range(1, half), copies[piece]):
            copy.wait()
            came = out_ref.at[lax.rem(links.node + nodes - 2 * h, nodes), rows]
            relays.append(send(came, came, (u0, u1), base + half - 1 + h, beside))
    finish(relays)


def local(nodes, ctrs, surface_xyz, centre_idx, volume_xyz, slab_ids, cotangent):
    width = cotangent.shape[0]
    owned = centre_idx.shape[0]
    total = owned * nodes
    here = lax.axis_index("node")
    f32 = jnp.float32
    vmem = lambda *shape: pltpu.VMEM(shape, f32)
    out = lambda *shape: jax.ShapeDtypeStruct(shape, f32)
    devices = nodes * ctrs

    slab = slab_ids % volume_xyz.shape[1]
    volume_points = jnp.concatenate(
        [scaled(volume_xyz), jnp.zeros((4, volume_xyz.shape[1]), f32)], axis=0
    )
    volume_points = jnp.concatenate([volume_points[4:], volume_points[:4]], axis=0)

    rows = surface_xyz.shape[1] // LANES
    tiles = owned // LANES
    perm, row_points, col_points, node_perm = comm_call(
        setup_body, nodes, ctrs,
        (
            jax.ShapeDtypeStruct((total // LANES, LANES), jnp.int32), out(nodes, 8, owned), out(ctrs, 8, owned),
            jax.ShapeDtypeStruct((volume_xyz.shape[1] // LANES, LANES), jnp.int32),
        ),
        [
            vmem(3, rows, LANES), vmem(3, volume_xyz.shape[1] // LANES, LANES),
            vmem(ctrs, nodes, 3, rows, LANES), vmem(3, tiles, LANES), vmem(nodes, 3, tiles, LANES),
            vmem(3, total // LANES, LANES), vmem(8, owned),
        ] + dma_pair(nodes + ctrs - 2) + dma_pair(nodes - 1) + dma_pair(nodes + ctrs - 2),
        0, surface_xyz, centre_idx.reshape(tiles, LANES),
        volume_xyz,
    )
    by_owner = perm.reshape(tiles, nodes, LANES)
    node_points, node_vec = node_rows(slab, node_perm.reshape(-1), volume_points, cotangent)
    left, col_right, node_right = factors(row_points, col_points, node_points)
    flat = lambda value: value.transpose(1, 0, 2).reshape(8, -1)[4:]
    groups = boxes(flat(row_points), GROUP)
    node_lists = near_lists(boxes(flat(node_points), LANES // 4), groups, 4)
    col_lists = near_lists(boxes(flat(col_points), LANES), groups, 1)

    places = jnp.arange(total, dtype=jnp.int32)
    hit = (by_owner.transpose(1, 0, 2).reshape(total) // LANES)[None, :] == (
        here * tiles + jnp.arange(tiles, dtype=jnp.int32)
    )[:, None]
    spots = jnp.concatenate(
        [jnp.where(hit, (places // LANES)[None, :], 0), jnp.where(hit, (places % LANES)[None, :], 0)], axis=0
    ).astype(jnp.bfloat16)
    lane = (
        by_owner.transpose(1, 0, 2).reshape(total)[:, None] % LANES == jnp.arange(LANES, dtype=jnp.int32)[None, :]
    ).astype(jnp.bfloat16)
    spots = jnp.dot(spots, lane, preferred_element_type=f32).astype(jnp.int32)
    slots = (spots[:tiles] * LANES + spots[tiles:]).reshape(owned)

    own_shape, scr = out(width, tiles, LANES), vmem(width, LANES)
    cols_shape = out(ctrs, width, tiles, LANES)
    landing = vmem(nodes - 1, width, tiles, LANES)
    line, every = vmem(1, LANES), vmem(devices, 1, LANES)
    part = apply_kernel(node_lists, left, node_right, node_vec, nodes)
    pulled, pulled_cols = comm_call(
        pulled_body, nodes, ctrs, (own_shape, cols_shape),
        [landing] + dma_pair(nodes - 1) + dma_pair(ctrs - 1), 3, part,
    )
    part = apply_kernel(col_lists, left, col_right, pulled_cols, nodes)
    resid, dir_cols, scal = comm_call(
        first_body, nodes, ctrs, (own_shape, cols_shape, out(2, width, LANES)),
        [landing, vmem(width, tiles, LANES), vmem(ctrs, width, tiles, LANES), line, every, scr, scr]
        + dma_pair(nodes - 1) + dma_pair(devices - 1) + dma_pair(ctrs - 1),
        4, part, pulled, pulled_cols,
    )
    part = apply_kernel(col_lists, left, col_right, dir_cols, nodes)
    final = comm_call(
        second_body, nodes, ctrs, out(nodes, 2 * width, tiles, LANES),
        [landing, vmem(2 * width, tiles, LANES), line, every, scr]
        + dma_pair(nodes - 1) + dma_pair(devices - 1) + dma_pair(PIECES * (nodes - 1)),
        5, part, pulled, resid, scal,
    )
    return tuple(pick(slots, final))


def solution(mesh):
    return jax.shard_map(
        functools.partial(local, mesh.shape["node"], mesh.shape["ctr"]),
        mesh=mesh,
        in_specs=(
            P(None, ("node", "ctr")),
            P(("node", "ctr")),
            P(None, "node"),
            P("node"),
            P(None, "node"),
        ),
        out_specs=(P(None, ("node", "ctr")), P(None, ("node", "ctr"))),
        check_vma=False,
    )
```
